32 devices in a mesh: gx: 8 (over y, x, core), gy: 4 (over z).
Axes of the slice: x: 2, y: 2, z: 4, core: 2. Of those that a mesh axis runs over, the one named last changes fastest.
Arguments:
- qm_density: float32 [288, 288, 288], P('gx', 'gy'), may hold values from -6 to 6
- mm_coords: float32 [8, 4, 3, 1024], P('gx', 'gy'), may hold values from 0 to 1
- mm_charge: float32 [8, 4, 1024], P('gx', 'gy'), may hold values from -1.8 to 1.8
- mm_types: int32 [8, 4, 1024], P('gx', 'gy'), may hold values from 0 to 15
- type_radius: float32 [16], replicated, may hold values from 0.02 to 0.2
- mm_cells: int32 [8, 4, 1024], P('gx', 'gy'), may hold values from 0 to 746495
- block_counts: int32 [8, 4, 32], P('gx', 'gy'), may hold values from 17 to 32
- block_owner: int32 [8, 4, 32, 1], P('gx', 'gy'), may hold values from 0 to 7; in each aligned block of 32 rows (0 to 31, 32 to 63, ..., all dimensions but the last counted through in order) at most 8 rows name the same one
- neighbour_tiles: int32 [8, 4, 32, 3], P('gx', 'gy'), may hold values from 0 to 8, all different within a row
Outputs:
- potential: float32 [288, 288, 288], P('gx', 'gy')
- mm_potential: float32 [8, 4, 1024], P('gx', 'gy')
- pair_force: float32 [8, 4, 3, 1024], P('gx', 'gy')
The draws below stay inside these ranges and needn't reach their ends.
Inputs may be any that keep to these rules, and one draw needn't show every extreme that they name: `block_owner`: within one tile no grid owner is named by more than 8 blocks, a bound that the blocks of some tile reach. `neighbour_tiles`: A block's 3 tiles are different.
All inputs are finite; a program needn't handle non-finite values.
Results may differ from the reference program's by a relative error of at most 0.0003.
Values sent between devices are 32-bit elements; how exact they have to be, the bound alone decides.
No kernel may reach another device: no remote copies, remote signals or barrier semaphores. Data moves between devices by JAX's collectives and lax.ppermute only.
A program may use at most 64 MiB of HBM per device.

```python
import math
import jax
import jax.numpy as jnp
import numpy as np
from jax import lax

GRID = 288
BLOCKS = 32
BLOCK_ATOMS = 32
LISTED = 3
TYPES = 16
TILES_X = 8
TILES_Y = 4
TILE_ATOMS = 1024
CAPACITY = 8
CELLS_DEV = 746496
N_GX = 8
N_GY = 4


def plant(result, rng, low, largest):
    extent = result.shape
    spot = [jax.random.randint(jax.random.fold_in(rng, axis), (), 0, extent[axis]) for axis in range(len(extent))]
    result = result.at[tuple(spot)].set(low)
    longest = extent.index(max(extent))
    spot[longest] = (spot[longest] + 1) % extent[longest]
    return result.at[tuple(spot)].set(largest)


def block_levels(rng, extent, cuts, least, high):
    factor_of, own = 1.0, jax.random.fold_in(rng, 6)
    for position, blocks in cuts:
        heights = jnp.exp(jax.random.uniform(jax.random.fold_in(own, position), (blocks,), jnp.float32, least / len(cuts), high / len(cuts)))
        factor_of = factor_of * jnp.repeat(heights, extent[position] // blocks).reshape([-1 if axis == position else 1 for axis in range(len(extent))])
    return factor_of


def choose_distinct(key, rows, count, top, lift):
    sequence = jax.random.permutation(jax.random.fold_in(key, 1), count)
    pull = sequence
    for power in range(3):
        pull = pull * pull // count
    pull = pull * lift // count
    chance = jax.random.randint(jax.random.fold_in(key, 2), (rows, count), 0, 4096) + pull
    sure = jax.random.permutation(jax.random.fold_in(key, 3), rows)[jnp.arange(count) % rows]
    chance = jnp.where(jnp.arange(rows)[:, None] == sure[None, :], 1 << 14, chance)
    priority = chance * count + jnp.arange(count)
    return lax.top_k(priority.astype(jnp.int32), top)[1].astype(jnp.int32)


def shared_out(key, own, number, rows, number_of, top, most, slope):
    order = jax.random.permutation(key, number_of)
    crowded, usual = portions_of(number_of, rows * top, most, slope, True), portions_of(number_of, rows * top, most, slope, False)
    places = jnp.arange(number_of)

    def named(sizes, offset_by):
        used = int((sizes > 0).sum())
        fixed = max(1, used // 4)
        passed = fixed + (places - fixed + offset_by * (used - fixed)) % max(1, number_of - fixed)
        return jnp.zeros((number_of,), jnp.int32).at[order[jnp.where(places < fixed, places, passed)]].set(jnp.asarray(sizes, jnp.int32))

    sizes = jnp.where(number % 4 == 0, named(crowded, number // 4), named(usual, number - number // 4 - 1))
    mixed = jax.random.permutation(jax.random.fold_in(own, 3), number_of)
    giver, taker = mixed[0:number_of // 2 * 2:2], mixed[1:number_of // 2 * 2:2]
    room = jnp.minimum(sizes[giver] - 1, most - sizes[taker]) // 2
    room = jnp.where((giver == order[0]) | (taker == order[0]) | (sizes[taker] == 0), 0, jnp.maximum(room, 0))
    passed = jax.random.randint(jax.random.fold_in(own, 4), (number_of // 2,), 0, 1 << 20) % (room + 1)
    sizes = sizes.at[giver].add(-passed).at[taker].add(passed)
    labels = jnp.searchsorted(jnp.cumsum(sizes), jnp.arange(rows * top), side="right").astype(jnp.int32)
    table = labels.reshape(top, rows).T
    table = table[jax.random.permutation(jax.random.fold_in(own, 1), rows)]
    offset_by = jax.random.randint(jax.random.fold_in(own, 2), (rows, 1), 0, top)
    return jnp.take_along_axis(table, (jnp.arange(top)[None, :] + offset_by) % top, axis=1)


def portions_of(amount, total, most, skew, full):
    weights = [(1 << 20) // math.isqrt(rank ** skew) + 1 for rank in range(1, amount + 1)]
    largest = most if full else min(most, max(-(-total // amount), total * weights[0] // sum(weights)))
    least = 1 if total - largest >= amount - 1 else 0
    counts, rest = [largest] + [least] * (amount - 1), total - largest - least * (amount - 1)
    while rest > 0:
        free = [i for i in range(1, amount) if counts[i] < largest] or [i for i in range(1, amount) if counts[i] < most]
        whole, remaining = sum([weights[i] for i in free]), rest
        for i in free:
            more = min(most - counts[i], max(1, remaining * weights[i] // whole), rest)
            counts[i] = counts[i] + more
            rest = rest - more
    return np.array(counts)


def gaussian(own_key, extent, width, most, split=(), held_as=jnp.bfloat16):
    drawn = jax.random.normal(own_key, extent, jnp.float32) * width
    if len(split) > 0:
        drawn = block_levels(own_key, extent, split, -0.22, 0.18) * drawn
    return jnp.clip(drawn, min=-most, max=most).astype(held_as)


def setup_inputs(seed: int = 0) -> dict:
    keys = jax.random.split(jax.random.key(seed), 10)
    qm_density = gaussian(keys[0], (GRID, GRID, GRID), 1.0, 6.0, ((0, 8), (1, 4)), jnp.float32)
    mm_coords = jnp.clip(1.0 * jax.random.uniform(keys[1], (TILES_X, TILES_Y, 3, TILE_ATOMS), jnp.float32) ** block_levels(keys[1], (TILES_X, TILES_Y, 3, TILE_ATOMS), ((0, 8), (1, 4)), -0.2, 0.2), 0.0, 1.0)
    mm_charge = gaussian(keys[2], (TILES_X, TILES_Y, TILE_ATOMS), 0.3, 1.8, ((0, 8), (1, 4)), jnp.float32)
    mm_types = plant(jax.random.randint(keys[3], (TILES_X, TILES_Y, TILE_ATOMS), 0, TYPES), jax.random.fold_in(keys[3], 1), 0, TYPES - 1).astype(jnp.int32)
    type_radius = jnp.clip(jnp.exp(jax.random.uniform(keys[4], (TYPES,), jnp.float32, math.log(0.02), math.log(0.2))), 0.02, 0.2)
    mm_cells = plant(jax.random.randint(keys[5], (TILES_X, TILES_Y, TILE_ATOMS), 0, CELLS_DEV), jax.random.fold_in(keys[5], 1), 0, CELLS_DEV - 1).astype(jnp.int32)
    block_counts = plant(jax.random.randint(keys[6], (TILES_X, TILES_Y, BLOCKS), BLOCK_ATOMS // 2 + 1, BLOCK_ATOMS + 1), jax.random.fold_in(keys[6], 1), BLOCK_ATOMS // 2 + 1, BLOCK_ATOMS).astype(jnp.int32)
    block_owner_keys = jax.random.split(jax.random.fold_in(keys[7], 1), TILES_X * TILES_Y * BLOCKS // BLOCKS)
    block_owner_turns = jax.random.permutation(jax.random.fold_in(keys[7], 3), TILES_X * TILES_Y * BLOCKS // BLOCKS)
    block_owner = jax.vmap(lambda own, number: shared_out(jax.random.fold_in(keys[7], 2), own, number, BLOCKS, N_GX, 1, CAPACITY, 2))(block_owner_keys, block_owner_turns).reshape((TILES_X, TILES_Y, BLOCKS, 1))
    neighbour_tiles = choose_distinct(keys[8], TILES_X * TILES_Y * BLOCKS, 9, LISTED, 0).reshape((TILES_X, TILES_Y, BLOCKS, LISTED))
    return dict(qm_density=qm_density, mm_coords=mm_coords, mm_charge=mm_charge, mm_types=mm_types, type_radius=type_radius, mm_cells=mm_cells, block_counts=block_counts, block_owner=block_owner, neighbour_tiles=neighbour_tiles)


SCREENING = 0.003

def stiffness(mode_index, length):
    return 4.0 * jnp.sin(jnp.pi * mode_index.astype(jnp.float32) / length) ** 2

def pair_forces(own_rows, pair_partners, shift_x, shift_y):
    sep_x = own_rows[:, 0, :, None, None] - (pair_partners[:, None, :, 0, :] + shift_x[:, None, :, None])
    sep_y = own_rows[:, 1, :, None, None] - (pair_partners[:, None, :, 1, :] + shift_y[:, None, :, None])
    sep_z = own_rows[:, 2, :, None, None] - pair_partners[:, None, :, 2, :]
    soften = (own_rows[:, 4, :, None, None] + pair_partners[:, None, :, 4, :]) ** 2
    inverse_root = lax.rsqrt(sep_x * sep_x + sep_y * sep_y + sep_z * sep_z + soften)
    strength = own_rows[:, 3, :, None, None] * pair_partners[:, None, :, 3, :] * inverse_root * inverse_root * inverse_root
    force_x = lax.optimization_barrier(jnp.sum(strength * sep_x, axis=(2, 3)))
    force_y = lax.optimization_barrier(jnp.sum(strength * sep_y, axis=(2, 3)))
    force_z = lax.optimization_barrier(jnp.sum(strength * sep_z, axis=(2, 3)))
    return jnp.stack([force_x, force_y, force_z], 0).reshape(3, -1)

def reference(qm_density, mm_coords, mm_charge, mm_types, type_radius, mm_cells, block_counts, block_owner, neighbour_tiles):
    x_local = GRID // N_GX
    local_y_rows = GRID // N_GY
    lanes = jnp.arange(BLOCK_ATOMS, dtype=jnp.int32)
    live = (lanes[None, None, None, :] < block_counts[..., None]).astype(jnp.float32).reshape(TILES_X, TILES_Y, TILE_ATOMS)
    charge_live = mm_charge * live
    owner_atom = jnp.broadcast_to(block_owner, (TILES_X, TILES_Y, BLOCKS, BLOCK_ATOMS)).reshape(TILES_X, TILES_Y, TILE_ATOMS)
    tile_rows = jnp.arange(TILES_Y, dtype=jnp.int32)[None, :, None]
    cell_x = owner_atom * x_local + mm_cells // (local_y_rows * GRID)
    cell_y = tile_rows * local_y_rows + mm_cells // GRID % local_y_rows
    cell_z = mm_cells % GRID
    flat_index = ((cell_x * GRID + cell_y) * GRID + cell_z).reshape(-1).astype(jnp.int32)
    density = qm_density.reshape(-1).at[flat_index].add(charge_live.reshape(-1)).reshape(GRID, GRID, GRID)
    mode_index = jnp.arange(GRID, dtype=jnp.int32)
    stiff = stiffness(mode_index, GRID)
    denominator = stiff[:, None, None] + stiff[None, :, None] + stiff[None, None, :] + SCREENING
    spectrum = jnp.fft.fftn(density)
    potential = jnp.real(jnp.fft.ifftn(spectrum / denominator)).astype(jnp.float32)
    mm_potential = potential.reshape(-1)[flat_index].reshape(TILES_X, TILES_Y, TILE_ATOMS) * live
    atom_radius = type_radius[mm_types]
    atom_rows = jnp.concatenate([mm_coords, charge_live[:, :, None, :], atom_radius[:, :, None, :]], axis=2)

    def tile_force(tile_number):
        tile_x = tile_number // TILES_Y
        tile_y = tile_number % TILES_Y
        enumerated_pairs = neighbour_tiles[tile_x, tile_y]
        step_x = enumerated_pairs // 3 - 1
        step_y = enumerated_pairs % 3 - 1
        pair_partners = atom_rows[(tile_x + step_x) % TILES_X, (tile_y + step_y) % TILES_Y]
        own_rows = atom_rows[tile_x, tile_y].reshape(5, BLOCKS, BLOCK_ATOMS).transpose(1, 0, 2)
        return pair_forces(own_rows, pair_partners, step_x.astype(jnp.float32), step_y.astype(jnp.float32))
    pair_force = lax.map(tile_force, jnp.arange(TILES_X * TILES_Y, dtype=jnp.int32))
    pair_force = pair_force.reshape(TILES_X, TILES_Y, 3, TILE_ATOMS)
    return (potential, mm_potential, pair_force)
```

```python
import functools

import jax
import jax.numpy as jnp
import ml_dtypes
import numpy as np
from jax import lax
from jax.experimental import pallas as pl
from jax.experimental.pallas import tpu as pltpu
from jax.sharding import PartitionSpec as P

SCREENING = 0.003
HIGH_ACCURACY = lax.Precision.HIGHEST
VMEM_LIMIT = 56 * 1024 * 1024


def padded(block, sides, width):
    for axis, dim in sides:
        count = lax.axis_size(axis)
        forward = [(i, i + 1) for i in range(count - 1)]
        forward.append((count - 1, 0))
        backward = [(target, source) for source, target in forward]
        low = lax.ppermute(
            lax.slice_in_dim(block, block.shape[dim] - width, None, axis=dim), axis, forward
        )
        high = lax.ppermute(lax.slice_in_dim(block, 0, width, axis=dim), axis, backward)
        block = jnp.concatenate([low, block, high], axis=dim)
    return block


def round_up(value, unit):
    return -(-value // unit) * unit


def sine_matrix(length):
    nodes = np.arange(length, dtype=np.float64)
    return np.sqrt(2.0 / length) * np.sin(np.pi * np.outer(nodes, nodes) / length)


def cas_matrix(length):
    nodes = np.arange(length)
    angle = 2.0 * np.pi * (np.outer(nodes, nodes) % length) / length
    return np.cos(angle) + np.sin(angle)


def split_pair(matrix):
    full = np.asarray(matrix, np.float32)
    high = full.astype(ml_dtypes.bfloat16)
    low = (full - high.astype(np.float32)).astype(ml_dtypes.bfloat16)
    return high, low


def left_triple(matrix):
    high, low = split_pair(matrix)
    return np.concatenate([high, low, high], axis=1)


class Plan:
    def __init__(self, x_len, y_len, grid, n_gx, n_gy):
        self.x_len, self.y_len, self.grid = x_len, y_len, grid
        self.n_gx, self.n_gy = n_gx, n_gy
        self.y_pad = round_up(y_len, 8)
        self.x_pad = round_up(x_len, 8)
        self.parts = n_gx * n_gy
        self.modes = -(-grid // self.parts)
        self.half = round_up(y_len + x_len, 128)
        self.kx_pad = round_up(n_gx, 8)
        self.j_pad = round_up(n_gy, 8)
        self.lanes = round_up(grid, 128)
        self.stack_rows = 3 * self.y_pad + 3 * self.x_pad

    def y_matrix(self):
        out = np.zeros((self.y_pad, self.y_pad))
        out[: self.y_len, : self.y_len] = sine_matrix(self.y_len)
        return out

    def interface_table(self):
        x_len, y_len, half = self.x_len, self.y_len, self.half
        y_pad, x_pad = self.y_pad, self.x_pad
        sine_x, sine_y = sine_matrix(x_len), sine_matrix(y_len)
        out = np.zeros((self.stack_rows, 2 * half))
        row = 0
        out[row : row + y_len, :y_len] = sine_y
        row += y_pad
        out[row : row + y_len, half : half + y_len] = sine_y
        row += y_pad
        out[row : row + x_len, y_len : y_len + x_len] = sine_x
        row += x_pad
        out[row : row + x_len, half + y_len : half + y_len + x_len] = sine_x
        row += x_pad
        out[row : row + y_len, :y_len] = np.eye(y_len)
        row += y_pad
        out[row + 1 : row + x_len, y_len + 1 : y_len + x_len] = np.eye(x_len - 1)
        return out

    def gather_table(self):
        n_gx, n_gy, parts = self.n_gx, self.n_gy, self.parts
        cas_x = cas_matrix(n_gx)
        out = np.zeros((n_gy * self.kx_pad + n_gx * self.j_pad, 2 * parts))
        for i in range(n_gx):
            for j in range(n_gy):
                col = i * n_gy + j
                base = j * self.kx_pad
                out[base : base + n_gx, col] = cas_x[:, i]
                out[base : base + n_gx, parts + col] = cas_x[:, (i + 1) % n_gx]
                base = n_gy * self.kx_pad + i * self.j_pad
                out[base + j, col] = 1.0
                out[base + (j + 1) % n_gy, parts + col] = 1.0
        return out

    def line_tables(self):
        scaled = cas_matrix(self.grid) / np.sqrt(self.grid)
        along_y = np.zeros((self.n_gy, self.half, self.grid))
        along_x = np.zeros((self.n_gx, self.half, self.grid))
        for j in range(self.n_gy):
            along_y[j, : self.y_len] = scaled[j * self.y_len : (j + 1) * self.y_len]
        for i in range(self.n_gx):
            along_x[i, self.y_len : self.y_len + self.x_len] = scaled[
                i * self.x_len : (i + 1) * self.x_len
            ]
        return along_y, along_x

    def expand_table(self):
        ratio = self.grid // self.n_gy
        full = cas_matrix(self.grid)
        out = np.zeros((self.j_pad, self.grid))
        for j in range(self.n_gy):
            out[j] = full[(j * ratio) % self.grid]
        return out

    def stiff(self, count, length):
        return 4.0 * np.sin(np.pi * np.arange(count) / length) ** 2


def f32(table):
    return jnp.asarray(np.asarray(table, np.float32))


def dot(a, b, dims=((1,), (0,)), precision=None):
    return lax.dot_general(
        a, b, (dims, ((), ())), precision=precision, preferred_element_type=jnp.float32
    )


def exact_dot(a, b, dims=((1,), (0,))):
    return dot(a, b, dims, HIGH_ACCURACY)


def left_apply(table, value):
    high = value.astype(jnp.bfloat16).astype(jnp.float32)
    low = value - high
    stacked = jnp.concatenate([high, high, low], axis=0).astype(jnp.bfloat16)
    return dot(table, stacked)


def right_apply(value, table_high, table_low):
    high = value.astype(jnp.bfloat16)
    low = (value - high.astype(jnp.float32)).astype(jnp.bfloat16)
    return dot(high, table_high) + dot(high, table_low) + dot(low, table_high)


def slab_count(plan):
    for count in (4, 3, 2):
        if plan.x_len % count == 0:
            return count
    return 1


def forward_kernel(
    plan,
    edge_x,
    density,
    cas_high,
    cas_low,
    y_table,
    x_table,
    stiff_yz,
    stiff_x,
    edge_y,
    interface,
    spectrum,
    message,
    work,
    stack,
    edge_rows,
    turned,
):
    x_len, y_len, y_pad, x_pad = plan.x_len, plan.y_len, plan.y_pad, plan.x_pad
    grid, lane_count = plan.grid, plan.lanes
    slabs = slab_count(plan) if y_pad == y_len else 1

    def along_z(step, carry):
        start = step * slabs
        rows = density[pl.ds(start, slabs)].reshape(slabs * y_len, grid)
        turned_rows = right_apply(rows, cas_high[...], cas_low[...])
        if y_pad == y_len:
            work[pl.ds(start, slabs)] = turned_rows.reshape(slabs, y_len, lane_count)
        else:
            work[start, :y_len, :] = turned_rows
            work[start, y_len:, :] = jnp.zeros((y_pad - y_len, lane_count), jnp.float32)
        return carry

    lax.fori_loop(0, x_len // slabs, along_z, 0)
    base = 2 * y_pad + 2 * x_pad
    stack[2 * y_pad :, :] = jnp.zeros((stack.shape[0] - 2 * y_pad, lane_count), jnp.float32)
    stack[base : base + y_pad, :] = work[0]
    for x in range(x_len):
        stack[base + y_pad + x : base + y_pad + x + 1, :] = work[x, 0:1, :]

    def along_y(x, carry):
        work[x] = left_apply(y_table[...], work[x])
        return carry

    lax.fori_loop(0, x_len, along_y, 0)

    def along_x(tile, carry):
        rows = pl.ds(pl.multiple_of(tile * 8, 8), 8)
        block = work[:, rows, :].reshape(x_len * 8, lane_count)
        spectrum[:, rows, :] = left_apply(x_table[...], block).reshape(x_len, 8, lane_count)
        return carry

    lax.fori_loop(0, y_pad // 8, along_x, 0)
    for start in range(0, lane_count, 128):
        lanes = slice(start, start + 128)
        base_stiff = stiff_yz[:, lanes]
        near_weight = edge_y[0]
        far_weight = edge_y[1]

        def edges(x, carry):
            near, far = carry
            value = spectrum[x, :, lanes] / (base_stiff + stiff_x[x])
            near_sum = jnp.sum(value * near_weight, axis=0, keepdims=True)
            far_sum = jnp.sum(value * far_weight, axis=0, keepdims=True)
            edge_rows[0, pl.ds(x, 1), :] = near_sum
            edge_rows[1, pl.ds(x, 1), :] = far_sum
            return near + edge_x[0, x] * value, far + edge_x[1, x] * value

        zero = jnp.zeros((y_pad, 128), jnp.float32)
        near, far = lax.fori_loop(0, x_len, edges, (zero, zero))
        stack[0:y_pad, lanes] = near
        stack[y_pad : 2 * y_pad, lanes] = far
        stack[2 * y_pad : 2 * y_pad + x_len, lanes] = edge_rows[0, :x_len, :]
        far_row = 2 * y_pad + x_pad
        stack[far_row : far_row + x_len, lanes] = edge_rows[1, :x_len, :]
    turned[...] = exact_dot(stack[...], interface[...], ((0,), (0,)))
    total = plan.parts * plan.modes
    for mode in range(grid):
        message[mode] = turned[mode : mode + 1, :]
    if total > grid:
        message[grid:total] = jnp.zeros((total - grid, 1, 2 * plan.half), jnp.float32)


def interface_kernel(
    plan,
    first_mode,
    stiff_z,
    incoming,
    gather,
    scatter,
    along_y,
    along_x,
    along_y_back,
    along_x_back,
    expand,
    stiff_x,
    stiff_y,
    outgoing,
    rows,
    folded_y,
    folded_x,
    lines,
):
    grid, half, parts, modes = plan.grid, plan.half, plan.parts, plan.modes
    kx_pad, j_pad, n_gx, n_gy = plan.kx_pad, plan.j_pad, plan.n_gx, plan.n_gy
    groups = grid // n_gx

    def collect(source, carry):
        for mode in range(modes):
            both = incoming[source * modes + mode]
            rows[mode, pl.ds(source, 1), :] = both[:, :half]
            rows[mode, pl.ds(parts + source, 1), :] = both[:, half:]
        return carry

    lax.fori_loop(0, parts, collect, 0)
    for mode in range(modes):
        lines[mode] = exact_dot(gather[...], rows[mode])
    total_y = jnp.zeros((modes * kx_pad, grid), jnp.float32)
    for j in range(n_gy):
        part = lines[:, j * kx_pad : (j + 1) * kx_pad, :].reshape(modes * kx_pad, half)
        total_y = total_y + exact_dot(part, along_y[j])
    folded_y[...] = total_y.reshape(modes, kx_pad, grid)
    total_x = jnp.zeros((modes * j_pad, grid), jnp.float32)
    base = n_gy * kx_pad
    for i in range(n_gx):
        part = lines[:, base + i * j_pad : base + (i + 1) * j_pad, :].reshape(modes * j_pad, half)
        total_x = total_x + exact_dot(part, along_x[i])
    folded_x[...] = total_x.reshape(modes, j_pad, grid)

    def solve(mode, carry):
        spread = exact_dot(folded_x[mode], expand[...], ((0,), (0,)))
        number = spread.reshape(groups, kx_pad, grid) + folded_y[mode][None]
        bottom = stiff_x[...] + (stiff_y[...] + stiff_z[first_mode[0] + mode])
        value = number / bottom.reshape(groups, kx_pad, grid)
        folded_y[mode] = jnp.sum(value, axis=0)
        folded_x[mode] = exact_dot(expand[...], value.reshape(grid, grid), ((1,), (1,)))
        return carry

    lax.fori_loop(0, modes, solve, 0)
    all_y = folded_y[...].reshape(modes * kx_pad, grid)
    for j in range(n_gy):
        lines[:, j * kx_pad : (j + 1) * kx_pad, :] = exact_dot(all_y, along_y_back[j]).reshape(
            modes, kx_pad, half
        )
    all_x = folded_x[...].reshape(modes * j_pad, grid)
    for i in range(n_gx):
        lines[:, base + i * j_pad : base + (i + 1) * j_pad, :] = exact_dot(
            all_x, along_x_back[i]
        ).reshape(modes, j_pad, half)
    for mode in range(modes):
        rows[mode] = exact_dot(scatter[...], lines[mode])

    def distribute(target, carry):
        for mode in range(modes):
            outgoing[target * modes + mode, :, :half] = rows[mode, pl.ds(target, 1), :]
            outgoing[target * modes + mode, :, half:] = rows[mode, pl.ds(parts + target, 1), :]
        return carry

    lax.fori_loop(0, parts, distribute, 0)


def backward_kernel(
    plan,
    edge_x,
    spectrum,
    message,
    cas_high,
    cas_low,
    y_table,
    x_table,
    stiff_yz,
    stiff_x,
    edge_y,
    interface,
    potential,
    work,
    stack,
    edge_rows,
    turned,
):
    x_len, y_len, y_pad, x_pad = plan.x_len, plan.y_len, plan.y_pad, plan.x_pad
    grid, lane_count = plan.grid, plan.lanes
    slabs = slab_count(plan) if y_pad == y_len else 1
    for mode in range(grid):
        turned[mode : mode + 1, :] = message[mode]
    if lane_count > grid:
        turned[grid:, :] = jnp.zeros((lane_count - grid, turned.shape[1]), jnp.float32)
    stack[...] = exact_dot(interface[...], turned[...], ((1,), (1,)))

    for start in range(0, lane_count, 128):
        lanes = slice(start, start + 128)
        base_stiff = stiff_yz[:, lanes]
        near_weight = edge_y[0]
        far_weight = edge_y[1]
        near = stack[0:y_pad, lanes]
        far = stack[y_pad : 2 * y_pad, lanes]
        edge_rows[0] = stack[2 * y_pad : 2 * y_pad + x_pad, lanes]
        edge_rows[1] = stack[2 * y_pad + x_pad : 2 * y_pad + 2 * x_pad, lanes]

        def add_edges(x, carry):
            value = spectrum[x, :, lanes] + edge_x[0, x] * near + edge_x[1, x] * far
            value = value + near_weight * edge_rows[0, pl.ds(x, 1), :]
            value = value + far_weight * edge_rows[1, pl.ds(x, 1), :]
            work[x, :, lanes] = value / (base_stiff + stiff_x[x])
            return carry

        lax.fori_loop(0, x_len, add_edges, 0)

    def along_x(tile, carry):
        rows = pl.ds(pl.multiple_of(tile * 8, 8), 8)
        block = work[:, rows, :].reshape(x_len * 8, lane_count)
        work[:, rows, :] = left_apply(x_table[...], block).reshape(x_len, 8, lane_count)
        return carry

    lax.fori_loop(0, y_pad // 8, along_x, 0)

    def along_y(x, carry):
        work[x] = left_apply(y_table[...], work[x])
        return carry

    lax.fori_loop(0, x_len, along_y, 0)
    base = 2 * y_pad + 2 * x_pad
    work[0] = work[0] + stack[base : base + y_pad, :]
    for x in range(1, x_len):
        row = base + y_pad + x
        work[x, 0:1, :] = work[x, 0:1, :] + stack[row : row + 1, :]

    def along_z(step, carry):
        start = step * slabs
        if y_pad == y_len:
            rows = work[pl.ds(start, slabs)].reshape(slabs * y_len, lane_count)
        else:
            rows = work[start, :y_len, :]
        out = right_apply(rows, cas_high[...], cas_low[...])
        potential[pl.ds(start, slabs)] = out.reshape(slabs, y_len, grid)
        return carry

    lax.fori_loop(0, x_len // slabs, along_z, 0)


VMEM = pl.BlockSpec(memory_space=pltpu.VMEM)
SMEM = pl.BlockSpec(memory_space=pltpu.SMEM)


def solve_poisson(density):
    x_len, y_len, grid = density.shape
    plan = Plan(x_len, y_len, grid, lax.axis_size("gx"), lax.axis_size("gy"))
    params = pltpu.CompilerParams(vmem_limit_bytes=VMEM_LIMIT)
    y_pad, x_pad, half = plan.y_pad, plan.x_pad, plan.half
    cas_z = np.zeros((grid, plan.lanes))
    cas_z[:, :grid] = cas_matrix(grid) / np.sqrt(grid)
    cas_high, cas_low = split_pair(cas_z)
    y_table = left_triple(plan.y_matrix())
    x_table = left_triple(np.kron(sine_matrix(x_len), np.eye(8)))
    stiff_z = plan.stiff(grid, grid)
    stiff_lanes = np.zeros(plan.lanes)
    stiff_lanes[:grid] = stiff_z
    stiff_yz = f32(plan.stiff(y_pad, 2 * y_len)[:, None] + stiff_lanes[None, :] + SCREENING)
    local_x = f32(plan.stiff(x_len, 2 * x_len))
    sine_x, sine_y = sine_matrix(x_len), plan.y_matrix()
    edge_x = f32(np.stack([sine_x[1], sine_x[x_len - 1]]))
    edge_y = f32(
        np.broadcast_to(
            np.stack([sine_y[1], sine_y[y_len - 1]])[:, :, None], (2, y_pad, 128)
        )
    )
    interface = f32(plan.interface_table())
    total = plan.parts * plan.modes
    scratch = [
        pltpu.VMEM((x_len, y_pad, plan.lanes), jnp.float32),
        pltpu.VMEM((plan.stack_rows, plan.lanes), jnp.float32),
        pltpu.VMEM((2, x_pad, 128), jnp.float32),
        pltpu.VMEM((plan.lanes, 2 * half), jnp.float32),
    ]
    spectrum, message = pl.pallas_call(
        functools.partial(forward_kernel, plan),
        out_shape=(
            jax.ShapeDtypeStruct((x_len, y_pad, plan.lanes), jnp.float32),
            jax.ShapeDtypeStruct((total, 1, 2 * half), jnp.float32),
        ),
        in_specs=[SMEM] + [VMEM] * 6 + [SMEM] + [VMEM] * 2,
        out_specs=(VMEM, VMEM),
        scratch_shapes=scratch,
        compiler_params=params,
        name="forward_solve",
    )(
        edge_x,
        density,
        cas_high,
        cas_low,
        y_table,
        x_table,
        stiff_yz,
        local_x,
        edge_y,
        interface,
    )
    incoming = lax.all_to_all(message, ("gx", "gy"), split_axis=0, concat_axis=0, tiled=True)
    gather = plan.gather_table()
    along_y, along_x = plan.line_tables()
    position = lax.axis_index("gx") * plan.n_gy + lax.axis_index("gy")
    first_mode = (position * plan.modes).astype(jnp.int32).reshape(1)
    padded_z = np.zeros(total)
    padded_z[:grid] = stiff_z
    outgoing = pl.pallas_call(
        functools.partial(interface_kernel, plan),
        out_shape=jax.ShapeDtypeStruct((total, 1, 2 * half), jnp.float32),
        in_specs=[SMEM] * 2 + [VMEM] * 10,
        out_specs=VMEM,
        scratch_shapes=[
            pltpu.VMEM((plan.modes, 2 * plan.parts, half), jnp.float32),
            pltpu.VMEM((plan.modes, plan.kx_pad, grid), jnp.float32),
            pltpu.VMEM((plan.modes, plan.j_pad, grid), jnp.float32),
            pltpu.VMEM((plan.modes, gather.shape[0], half), jnp.float32),
        ],
        compiler_params=params,
        name="interface_solve",
    )(
        first_mode,
        f32((padded_z + SCREENING) * grid),
        incoming,
        f32(gather),
        f32(gather.T),
        f32(along_y),
        f32(along_x),
        f32(along_y.transpose(0, 2, 1)),
        f32(along_x.transpose(0, 2, 1)),
        f32(plan.expand_table()),
        f32(stiff_z[:, None] * grid),
        f32(stiff_z[None, :] * grid),
    )
    returned = lax.all_to_all(outgoing, ("gx", "gy"), split_axis=0, concat_axis=0, tiled=True)
    return pl.pallas_call(
        functools.partial(backward_kernel, plan),
        out_shape=jax.ShapeDtypeStruct((x_len, y_len, grid), jnp.float32),
        in_specs=[SMEM] + [VMEM] * 7 + [SMEM] + [VMEM] * 2,
        out_specs=VMEM,
        scratch_shapes=scratch,
        compiler_params=params,
        name="backward_solve",
    )(
        edge_x,
        spectrum,
        returned,
        cas_high.T,
        cas_low.T,
        y_table,
        x_table,
        stiff_yz,
        local_x,
        edge_y,
        interface,
    )


def slot_select(owners, target, capacity):
    n_blocks = owners.shape[-1]
    block_ids = jnp.arange(n_blocks, dtype=jnp.int32)
    mine = owners == target
    earlier = block_ids[None, :] < block_ids[:, None]
    slot_rank = jnp.sum((mine[:, None, :] & earlier[None, :, :]).astype(jnp.int32), axis=2)
    slot_ids = jnp.arange(capacity, dtype=jnp.int32)
    chosen = mine[:, None, :] & (slot_rank[:, None, :] == slot_ids[None, :, None])
    return chosen.astype(jnp.float32)


def cell_tables(slot_cells, plane_count, grid_len):
    planes = jnp.arange(plane_count, dtype=jnp.int32)
    depths = jnp.arange(grid_len, dtype=jnp.int32)
    place = ((slot_cells // grid_len)[:, None] == planes[None, :]).astype(jnp.float32)
    depth = ((slot_cells % grid_len)[:, None] == depths[None, :]).astype(jnp.float32)
    return (place, depth)


def deposit_and_solve(qm_density, slot_charge, slot_cells):
    x_local, local_y_rows, grid_len = qm_density.shape
    plane_count = x_local * local_y_rows
    place, depth = cell_tables(slot_cells, plane_count, grid_len)
    added = jnp.einsum("sp,sz->pz", place, depth * slot_charge[:, None], precision=HIGH_ACCURACY)
    density = qm_density.reshape(plane_count, grid_len) + added
    potential = solve_poisson(density.reshape(x_local, local_y_rows, grid_len))
    sampled_rows = jnp.dot(place, potential.reshape(plane_count, grid_len), precision=HIGH_ACCURACY)
    slot_values = jnp.sum(sampled_rows * depth, axis=1)
    return (potential, slot_values)


def group_forces(group_data):
    own_rows, pair_partners, shift_x, shift_y = group_data
    sep_x = own_rows[:, 0, :, None, None] - (
        pair_partners[:, None, :, 0, :] + shift_x[:, None, :, None]
    )
    sep_y = own_rows[:, 1, :, None, None] - (
        pair_partners[:, None, :, 1, :] + shift_y[:, None, :, None]
    )
    sep_z = own_rows[:, 2, :, None, None] - pair_partners[:, None, :, 2, :]
    soften = (own_rows[:, 4, :, None, None] + pair_partners[:, None, :, 4, :]) ** 2
    inverse_root = lax.rsqrt(sep_x * sep_x + sep_y * sep_y + sep_z * sep_z + soften)
    strength = (
        own_rows[:, 3, :, None, None]
        * pair_partners[:, None, :, 3, :]
        * inverse_root
        * inverse_root
        * inverse_root
    )
    force_x = jnp.sum(strength * sep_x, axis=(2, 3))
    force_y = jnp.sum(strength * sep_y, axis=(2, 3))
    force_z = jnp.sum(strength * sep_z, axis=(2, 3))
    return jnp.stack([force_x, force_y, force_z], 0)


def body(
    qm_density,
    mm_coords,
    mm_charge,
    mm_types,
    type_radius,
    mm_cells,
    block_counts,
    block_owner,
    neighbour_tiles,
):
    n_blocks = block_counts.shape[2]
    tile_atoms = mm_charge.shape[2]
    block_atoms = tile_atoms // n_blocks
    x_local, local_y_rows, grid_len = qm_density.shape
    cells_dev = x_local * local_y_rows * grid_len
    lanes = jnp.arange(block_atoms, dtype=jnp.int32)
    live = (
        (lanes[None, :] < block_counts.reshape(n_blocks, 1)).astype(jnp.float32).reshape(tile_atoms)
    )
    charge_live = mm_charge.reshape(tile_atoms) * live
    cells = mm_cells.reshape(tile_atoms)
    owners = block_owner.reshape(n_blocks)
    my_row = lax.axis_index("gx")
    n_rows = lax.axis_size("gx")
    capacity = 2 * n_blocks // n_rows
    owner_atom = jnp.broadcast_to(owners[:, None], (n_blocks, block_atoms)).reshape(tile_atoms)
    coded = (owner_atom * cells_dev + cells).astype(jnp.float32)
    stacked = jnp.stack([charge_live, coded], 0)[:, None, :]
    all_members = lax.all_gather(stacked, "gx", axis=1, tiled=True)
    all_code = all_members[1].astype(jnp.int32)
    all_owners = all_code.reshape(n_rows, n_blocks, block_atoms)[:, :, 0] // cells_dev
    selection = slot_select(all_owners, my_row, capacity)
    block_data = jnp.stack([all_members[0], (all_code % cells_dev).astype(jnp.float32)], 0)
    block_data = block_data.reshape(2, n_rows, n_blocks, block_atoms)
    slots = jnp.einsum("tkb,ctba->ctka", selection, block_data, precision=HIGH_ACCURACY)
    slot_charge = slots[0].reshape(-1)
    slot_cells = slots[1].reshape(-1).astype(jnp.int32)
    potential, slot_values = deposit_and_solve(qm_density, slot_charge, slot_cells)
    slot_values = slot_values.reshape(n_rows, capacity, block_atoms)
    spread = jnp.einsum("tkb,tka->tba", selection, slot_values, precision=HIGH_ACCURACY).reshape(
        n_rows * tile_atoms
    )
    sampled = lax.psum_scatter(spread, "gx", scatter_dimension=0, tiled=True)
    mm_potential = (sampled * live).reshape(1, 1, tile_atoms)
    type_count = type_radius.shape[0]
    type_match = (
        mm_types.reshape(1, tile_atoms) == jnp.arange(type_count, dtype=jnp.int32)[:, None]
    ).astype(jnp.float32)
    atom_radius = jnp.sum(type_radius[:, None] * type_match, axis=0)
    atom_rows = jnp.concatenate(
        [mm_coords.reshape(3, tile_atoms), charge_live[None, :], atom_radius[None, :]], axis=0
    )
    widened_grid = padded(atom_rows[None, None], (("gx", 0), ("gy", 1)), 1)
    widened_grid = widened_grid.reshape(9, 5, tile_atoms)
    enumerated_pairs = neighbour_tiles.reshape(n_blocks, -1)
    tile_selector = (
        enumerated_pairs[:, :, None] == jnp.arange(9, dtype=jnp.int32)[None, None, :]
    ).astype(jnp.float32)
    pair_partners = jnp.einsum(
        "kdv,vmq->kdmq", tile_selector, widened_grid, precision=HIGH_ACCURACY
    )
    shift_x = (enumerated_pairs // 3 - 1).astype(jnp.float32)
    shift_y = (enumerated_pairs % 3 - 1).astype(jnp.float32)
    own_rows = atom_rows.reshape(5, n_blocks, block_atoms).transpose(1, 0, 2)
    group_size = 8
    n_groups = n_blocks // group_size
    forces = lax.map(
        group_forces,
        (
            own_rows.reshape(n_groups, group_size, 5, block_atoms),
            pair_partners.reshape(n_groups, group_size, enumerated_pairs.shape[1], 5, tile_atoms),
            shift_x.reshape(n_groups, group_size, -1),
            shift_y.reshape(n_groups, group_size, -1),
        ),
    )
    pair_force = forces.transpose(1, 0, 2, 3).reshape(1, 1, 3, tile_atoms)
    return (potential, mm_potential, pair_force)


def solution(mesh):
    placed = (
        P("gx", "gy", None),
        P("gx", "gy", None, None),
        P("gx", "gy", None),
        P("gx", "gy", None),
        P(),
        P("gx", "gy", None),
        P("gx", "gy", None),
        P("gx", "gy", None, None),
        P("gx", "gy", None, None),
    )
    return jax.shard_map(
        body,
        mesh=mesh,
        in_specs=placed,
        out_specs=(P("gx", "gy", None), P("gx", "gy", None), P("gx", "gy", None, None)),
        check_vma=False,
    )
```

```python
import functools

import jax
import jax.numpy as jnp
import ml_dtypes
import numpy as np
from jax import lax
from jax.experimental import pallas as pl
from jax.experimental.pallas import tpu as pltpu
from jax.sharding import PartitionSpec as P

SCREENING = 0.003
HIGH_ACCURACY = lax.Precision.HIGHEST
COPIES = 4
MIB = 1024 * 1024


def round_up(value, unit):
    return -(-value // unit) * unit


def sine_matrix(length):
    nodes = np.arange(length, dtype=np.float64)
    return np.sqrt(2.0 / length) * np.sin(np.pi * np.outer(nodes, nodes) / length)


def cas_matrix(length):
    nodes = np.arange(length)
    angle = 2.0 * np.pi * (np.outer(nodes, nodes) % length) / length
    return np.cos(angle) + np.sin(angle)


def stiffness(count, length):
    return 4.0 * np.sin(np.pi * np.arange(count) / length) ** 2


def split_pair(matrix):
    full = np.asarray(matrix, np.float32)
    high = full.astype(ml_dtypes.bfloat16)
    low = (full - high.astype(np.float32)).astype(ml_dtypes.bfloat16)
    return high, low


def table_triple(matrix, axis):
    high, low = split_pair(matrix)
    return np.concatenate([high, low, high], axis=axis)


def f32(table):
    return np.asarray(table, np.float32)


class Plan:
    def __init__(self, x_len, y_len, grid, n_gx, n_gy):
        self.x_len, self.y_len, self.grid = x_len, y_len, grid
        self.n_gx, self.n_gy = n_gx, n_gy
        self.y_pad = round_up(y_len, 8)
        self.x_pad = round_up(x_len, 8)
        self.lanes = round_up(grid, 128)
        self.lane_tiles = self.lanes // 128
        self.planes = x_len * self.y_pad
        self.span = self.lane_tiles * self.planes * 128
        self.parts = n_gx * n_gy
        self.modes = -(-grid // self.parts)
        self.half = round_up(y_len + x_len, 128)
        self.kx_pad = round_up(n_gx, 8)
        self.j_pad = round_up(n_gy, 8)
        self.stack_rows = round_up(3 * self.y_pad + 2 * self.x_pad, 128)

    def y_matrix(self):
        out = np.zeros((self.y_pad, self.y_pad))
        out[: self.y_len, : self.y_len] = sine_matrix(self.y_len)
        return out

    def z_matrix(self):
        out = np.zeros((self.lanes, self.lanes))
        out[: self.grid, : self.grid] = cas_matrix(self.grid) / np.sqrt(self.grid)
        return out

    def diagonal(self):
        z_part = np.zeros(self.lanes)
        z_part[: self.grid] = stiffness(self.grid, self.grid)
        y_part = stiffness(self.y_pad, 2 * self.y_len)
        return 2.0 + y_part[:, None] + z_part[None, :] + SCREENING

    def edge_weights(self):
        sine_y = self.y_matrix()
        both = np.stack([sine_y[1], sine_y[self.y_len - 1]])
        return np.broadcast_to(both[:, :, None], (2, self.y_pad, 128))

    def interface_table(self):
        x_len, y_len, half = self.x_len, self.y_len, self.half
        y_pad, x_pad = self.y_pad, self.x_pad
        sine_y = sine_matrix(y_len)
        out = np.zeros((self.stack_rows, 2 * half))
        out[:y_len, :y_len] = sine_y
        row = y_pad
        out[row : row + y_len, half : half + y_len] = sine_y
        row += y_pad
        out[row : row + y_len, :y_len] = np.eye(y_len)
        row += y_pad
        out[row + 1 : row + x_len, y_len + 1 : y_len + x_len] = np.eye(x_len - 1)
        row += x_pad
        far = half + y_len
        out[row + 1 : row + x_len, far + 1 : far + x_len] = np.eye(x_len - 1)
        return out

    def gather_table(self):
        n_gx, n_gy, parts = self.n_gx, self.n_gy, self.parts
        cas_x = cas_matrix(n_gx)
        out = np.zeros((n_gy * self.kx_pad + n_gx * self.j_pad, 2 * parts))
        for i in range(n_gx):
            for j in range(n_gy):
                col = i * n_gy + j
                base = j * self.kx_pad
                out[base : base + n_gx, col] = cas_x[:, i]
                out[base : base + n_gx, parts + col] = cas_x[:, (i + 1) % n_gx]
                base = n_gy * self.kx_pad + i * self.j_pad
                out[base + j, col] = 1.0
                out[base + (j + 1) % n_gy, parts + col] = 1.0
        return out

    def line_tables(self):
        scaled = cas_matrix(self.grid) / np.sqrt(self.grid)
        along_y = np.zeros((self.n_gy, self.half, self.lanes))
        along_x = np.zeros((self.n_gx, self.half, self.lanes))
        y_len, x_len, grid = self.y_len, self.x_len, self.grid
        for j in range(self.n_gy):
            along_y[j, :y_len, :grid] = scaled[j * y_len : (j + 1) * y_len]
        for i in range(self.n_gx):
            along_x[i, y_len : y_len + x_len, :grid] = scaled[i * x_len : (i + 1) * x_len]
        return along_y.reshape(-1, self.lanes), along_x.reshape(-1, self.lanes)

    def expand_table(self):
        ratio = self.grid // self.n_gy
        full = cas_matrix(self.grid)
        out = np.zeros((self.j_pad, self.lanes))
        for j in range(self.n_gy):
            out[j, : self.grid] = full[(j * ratio) % self.grid]
        return out


def dot(a, b, dims=((1,), (0,)), precision=None):
    return lax.dot_general(
        a, b, (dims, ((), ())), precision=precision, preferred_element_type=jnp.float32
    )


def value_triple(value, axis):
    high = value.astype(jnp.bfloat16).astype(jnp.float32)
    return jnp.concatenate([high, high, value - high], axis=axis).astype(jnp.bfloat16)


def left_apply(table, value):
    return dot(table, value_triple(value, 0))


def right_apply(value, table):
    return dot(value_triple(value, 1), table)


def slab_count(plan):
    if plan.y_pad != plan.y_len:
        return 1
    return max(count for count in (4, 3, 2, 1) if plan.x_len % count == 0)


def inverse(value):
    guess = pl.reciprocal(value, approx=True)
    guess = guess * (2.0 - value * guess)
    return guess * (2.0 - value * guess)


def owned_blocks(plan, codes, first_code, n_blocks, block_atoms, visit):
    base = first_code[0]

    def tile(source, carry):
        def block(number, inner):
            start = number * block_atoms
            lead = codes[source, start].astype(jnp.int32) - base

            @pl.when((lead >= 0) & (lead < plan.span))
            def _():
                visit(source, number, start, base)

            return inner

        return lax.fori_loop(0, n_blocks, block, carry)

    lax.fori_loop(0, plan.n_gx, tile, 0)


def chunked_loop(count, unroll, body, init):
    while count % unroll:
        unroll -= 1

    def group(step, carry):
        for k in range(unroll):
            carry = body(step * unroll + k, carry)
        return carry

    return lax.fori_loop(0, count // unroll, group, init)


def forward_kernel(
    plan,
    n_blocks,
    block_atoms,
    codes,
    first_code,
    density,
    z_table,
    y_table,
    diagonal,
    edge_y,
    interface,
    spectrum,
    message,
    *scratch,
):
    added = scratch[:COPIES]
    solved, factors, stack, heads, edge_rows, turned = scratch[COPIES:]
    x_len, y_len, y_pad, x_pad = plan.x_len, plan.y_len, plan.y_pad, plan.x_pad
    grid, lane_count, planes = plan.grid, plan.lanes, plan.planes
    slabs = slab_count(plan)
    tile_atoms = n_blocks * block_atoms
    lane_ids = lax.broadcasted_iota(jnp.int32, (1, 128), 1)

    def clear(step, carry):
        for copy in added:
            copy[pl.ds(pl.multiple_of(step * y_pad, 8), y_pad), :] = jnp.zeros(
                (y_pad, 128), jnp.float32
            )
        return carry

    lax.fori_loop(0, plan.lane_tiles * x_len, clear, 0)

    def deposit(source, number, start, base):
        for lead in range(0, block_atoms, COPIES):
            places, rows = [], []
            for k in range(COPIES):
                code = codes[source, start + lead + k].astype(jnp.int32) - base
                charge = codes[source, tile_atoms + start + lead + k]
                place = pl.ds(lax.shift_right_logical(code, 7), 1)
                hit = jnp.where(lane_ids == (code & 127), charge, 0.0)
                places.append(place)
                rows.append(added[k][place, :] + hit)
            for k in range(COPIES):
                added[k][places[k], :] = rows[k]

    owned_blocks(plan, codes, first_code, n_blocks, block_atoms, deposit)

    def transform(step, carry):
        start = step * slabs
        count = slabs * y_pad
        pieces = []
        for tile in range(plan.lane_tiles):
            low = tile * 128
            width = min(128, grid - low)
            piece = density[pl.ds(start, slabs), :, low : low + width]
            if y_pad == y_len:
                piece = piece.reshape(count, width)
            else:
                rows = jnp.zeros((y_pad - y_len, width), jnp.float32)
                piece = jnp.concatenate([piece[0], rows], axis=0)
            if width < 128:
                rest = jnp.zeros((count, 128 - width), jnp.float32)
                piece = jnp.concatenate([piece, rest], axis=1)
            place = pl.ds(pl.multiple_of(tile * planes + start * y_pad, 8), count)
            for copy in added:
                piece = piece + copy[place, :]
            pieces.append(piece)
        lines = right_apply(jnp.concatenate(pieces, axis=1), z_table[...])
        lines = lines.reshape(slabs, y_pad, lane_count)
        for slab in range(slabs):
            x = start + slab
            for tile in range(plan.lane_tiles):
                heads[tile, pl.ds(x, 1), :] = lines[slab, 0:1, tile * 128 : tile * 128 + 128]
            spectrum[x] = left_apply(y_table[...], lines[slab])

        @pl.when(step == 0)
        def _():
            stack[2 * y_pad : 3 * y_pad, :] = lines[0]

        return carry

    chunked_loop(x_len // slabs, 3, transform, 0)
    stack[3 * y_pad :, :] = jnp.zeros((stack.shape[0] - 3 * y_pad, lane_count), jnp.float32)
    for tile in range(plan.lane_tiles):
        lanes = slice(tile * 128, tile * 128 + 128)
        near_weight = edge_y[0]
        far_weight = edge_y[1]

        def eliminate(step, carry):
            factor, value = carry
            x = step + 1
            factor = inverse(diagonal[:, lanes] - factor)
            value = (spectrum[x, :, lanes] + value) * factor
            factors[x] = factor
            solved[x] = value
            return factor, value

        def substitute(step, value):
            x = x_len - 1 - step
            value = solved[x] + factors[x] * value
            near_row = jnp.sum(value * near_weight, axis=0, keepdims=True)
            far_row = jnp.sum(value * far_weight, axis=0, keepdims=True)
            edge_rows[0, pl.ds(x, 1), :] = near_row + heads[tile, pl.ds(x, 1), :]
            edge_rows[1, pl.ds(x, 1), :] = far_row
            return value

        zero = jnp.zeros((y_pad, 128), jnp.float32)
        chunked_loop(x_len - 1, 5, eliminate, (zero, zero))
        stack[y_pad : 2 * y_pad, lanes] = solved[x_len - 1]
        stack[0:y_pad, lanes] = chunked_loop(x_len - 1, 5, substitute, zero)
        for side in range(2):
            row = 3 * y_pad + side * x_pad
            stack[row + 1 : row + x_len, lanes] = edge_rows[side, 1:x_len, :]
    turned[...] = right_apply(jnp.transpose(stack[...]), interface[...])
    total = plan.parts * plan.modes
    for mode in range(grid):
        message[mode] = turned[mode : mode + 1, :]
    if total > grid:
        message[grid:total] = jnp.zeros((total - grid, 1, 2 * plan.half), jnp.float32)


def interface_kernel(
    plan,
    first_mode,
    stiff_z,
    incoming,
    gather,
    scatter,
    along_y,
    along_x,
    along_y_back,
    along_x_back,
    expand,
    expand_back,
    stiff_x,
    stiff_y,
    outgoing,
    rows,
    folded_y,
    folded_x,
    lines,
):
    grid, half, parts, modes = plan.grid, plan.half, plan.parts, plan.modes
    kx_pad, j_pad, n_gx, n_gy = plan.kx_pad, plan.j_pad, plan.n_gx, plan.n_gy
    lane_count = plan.lanes
    groups = grid // n_gx

    def collect(source, carry):
        for mode in range(modes):
            both = incoming[source * modes + mode]
            rows[mode, pl.ds(source, 1), :] = both[:, :half]
            rows[mode, pl.ds(parts + source, 1), :] = both[:, half:]
        return carry

    lax.fori_loop(0, parts, collect, 0)
    for mode in range(modes):
        lines[mode] = left_apply(gather[...], rows[mode])
    base = n_gy * kx_pad
    y_slots = [slice(j * kx_pad, (j + 1) * kx_pad) for j in range(n_gy)]
    x_slots = [slice(base + i * j_pad, base + (i + 1) * j_pad) for i in range(n_gx)]

    def side_by_side(slots, count):
        return jnp.concatenate(
            [lines[:, slot, :].reshape(modes * count, half) for slot in slots], axis=1
        )

    folded_y[...] = right_apply(side_by_side(y_slots, kx_pad), along_y[...]).reshape(
        modes, kx_pad, lane_count
    )
    folded_x[...] = right_apply(side_by_side(x_slots, j_pad), along_x[...]).reshape(
        modes, j_pad, lane_count
    )

    def solve(mode, carry):
        across = folded_x[mode, :, :grid]
        high = across.astype(jnp.bfloat16).astype(jnp.float32)
        across = jnp.concatenate([high, high, across - high], axis=0)
        spread = dot(across, expand[...], ((0,), (0,)))
        number = spread.reshape(groups, kx_pad, lane_count) + folded_y[mode][None]
        bottom = stiff_x[...] + (stiff_y[...] + stiff_z[first_mode[0] + mode])
        value = number * inverse(bottom).reshape(groups, kx_pad, lane_count)
        folded_y[mode] = jnp.sum(value, axis=0)
        value = value_triple(value.reshape(grid, lane_count), 1)
        folded_x[mode, :, :grid] = dot(expand_back[...], value, ((1,), (1,)))
        return carry

    chunked_loop(modes, 3, solve, 0)
    all_y = right_apply(folded_y[...].reshape(modes * kx_pad, lane_count), along_y_back[...])
    for j, slot in enumerate(y_slots):
        lines[:, slot, :] = all_y[:, j * half : (j + 1) * half].reshape(modes, kx_pad, half)
    all_x = right_apply(folded_x[...].reshape(modes * j_pad, lane_count), along_x_back[...])
    for i, slot in enumerate(x_slots):
        lines[:, slot, :] = all_x[:, i * half : (i + 1) * half].reshape(modes, j_pad, half)
    for mode in range(modes):
        rows[mode] = left_apply(scatter[...], lines[mode])

    def distribute(target, carry):
        for mode in range(modes):
            outgoing[target * modes + mode, :, :half] = rows[mode, pl.ds(target, 1), :]
            outgoing[target * modes + mode, :, half:] = rows[mode, pl.ds(parts + target, 1), :]
        return carry

    lax.fori_loop(0, parts, distribute, 0)


def backward_kernel(
    plan,
    n_blocks,
    block_atoms,
    codes,
    first_code,
    spectrum,
    message,
    z_table,
    y_table,
    diagonal,
    edge_y,
    interface,
    potential,
    values,
    lookup,
    work,
    solved,
    factors,
    stack,
    heads,
    edge_rows,
    turned,
    picked,
):
    x_len, y_len, y_pad, x_pad = plan.x_len, plan.y_len, plan.y_pad, plan.x_pad
    grid, lane_count, planes = plan.grid, plan.lanes, plan.planes
    slabs = slab_count(plan)
    for mode in range(grid):
        turned[mode : mode + 1, :] = message[mode]
    if lane_count > grid:
        turned[grid:, :] = jnp.zeros((lane_count - grid, turned.shape[1]), jnp.float32)
    stack[...] = dot(interface[...], value_triple(turned[...], 1), ((1,), (1,)))
    for tile in range(plan.lane_tiles):
        lanes = slice(tile * 128, tile * 128 + 128)
        near_weight = edge_y[0]
        far_weight = edge_y[1]
        heads[tile] = stack[3 * y_pad : 3 * y_pad + x_pad, lanes]
        edge_rows[...] = stack[3 * y_pad + x_pad : 3 * y_pad + 2 * x_pad, lanes]

        def eliminate(step, carry):
            factor, value = carry
            x = step + 1
            factor = inverse(diagonal[:, lanes] - factor)
            load = spectrum[x, :, lanes] + near_weight * heads[tile, pl.ds(x, 1), :]
            load = load + far_weight * edge_rows[pl.ds(x, 1), :]
            value = (load + value) * factor
            factors[x] = factor
            solved[x] = value
            return factor, value

        def substitute(step, value):
            x = x_len - 1 - step
            value = solved[x] + factors[x] * value
            work[x, :, lanes] = value
            return value

        zero = jnp.zeros((y_pad, 128), jnp.float32)
        chunked_loop(x_len - 1, 5, eliminate, (zero, stack[0:y_pad, lanes]))
        chunked_loop(x_len - 1, 5, substitute, stack[y_pad : 2 * y_pad, lanes])
    work[0] = jnp.zeros((y_pad, lane_count), jnp.float32)

    def transform(step, carry):
        start = step * slabs
        for slab in range(slabs):
            x = start + slab
            work[x] = left_apply(y_table[...], work[x])
            for tile in range(plan.lane_tiles):
                lanes = slice(tile * 128, tile * 128 + 128)
                work[x, 0:1, lanes] = heads[tile, pl.ds(x, 1), :]

        @pl.when(step == 0)
        def _():
            work[0] = stack[2 * y_pad : 3 * y_pad, :]

        lines = work[pl.ds(start, slabs)].reshape(slabs * y_pad, lane_count)
        lines = right_apply(lines, z_table[...])
        for tile in range(plan.lane_tiles):
            low = tile * 128
            place = pl.ds(pl.multiple_of(tile * planes + start * y_pad, 8), slabs * y_pad)
            lookup[place, :] = lines[:, low : low + 128]
        lines = lines.reshape(slabs, y_pad, lane_count)
        potential[pl.ds(start, slabs)] = lines[:, :y_len, :grid]
        return carry

    chunked_loop(x_len // slabs, 3, transform, 0)
    values[...] = jnp.zeros(values.shape, jnp.float32)
    lane_ids = lax.broadcasted_iota(jnp.int32, (1, 128), 1)
    shape = (block_atoms, 128)
    own_lane = lax.broadcasted_iota(jnp.int32, shape, 0) == lax.broadcasted_iota(
        jnp.int32, shape, 1
    )

    def sample(source, number, start, base):
        for atom in range(block_atoms):
            code = codes[source, start + atom].astype(jnp.int32) - base
            row = lookup[pl.ds(lax.shift_right_logical(code, 7), 1), :]
            picked[atom : atom + 1, :] = jnp.where(lane_ids == (code & 127), row, 0.0)
        found = jnp.sum(picked[...], axis=1, keepdims=True)
        found = jnp.sum(jnp.where(own_lane, found, 0.0), axis=0, keepdims=True)
        values[pl.ds(source * n_blocks + number, 1), :] = found

    owned_blocks(plan, codes, first_code, n_blocks, block_atoms, sample)


def pair_kernel(
    n_blocks, block_atoms, listed, listing, low, middle, high, forces, table, columns, results
):
    tile_atoms = n_blocks * block_atoms
    sides = (low, middle, high)
    for step_x in range(3):
        for step_y in range(3):
            table[step_x * 3 + step_y, 0:5, :] = sides[step_y][step_x]
    columns[0:8, :] = table[4]
    columns[5:, :] = jnp.zeros((columns.shape[0] - 5, tile_atoms), jnp.float32)
    results[...] = jnp.transpose(columns[...])
    lane_ids = lax.broadcasted_iota(jnp.int32, (block_atoms, 128), 1)

    def block(number, carry):
        place = pl.ds(pl.multiple_of(number * block_atoms, block_atoms), block_atoms)
        own = results[place, :]
        mine = [jnp.broadcast_to(own[:, k : k + 1], (block_atoms, 128)) for k in range(5)]
        zero = jnp.zeros((block_atoms, 128), jnp.float32)

        def tile(slot, sums):
            force_x, force_y, force_z = sums
            which = listing[number, slot]
            shift_x = (which // 3 - 1).astype(jnp.float32)
            shift_y = (which % 3 - 1).astype(jnp.float32)
            for start in range(0, tile_atoms, 128):
                lanes = slice(start, start + 128)
                sep_x = mine[0] - (table[which, 0:1, lanes] + shift_x)
                sep_y = mine[1] - (table[which, 1:2, lanes] + shift_y)
                sep_z = mine[2] - table[which, 2:3, lanes]
                reach = mine[4] + table[which, 4:5, lanes]
                root = lax.rsqrt(sep_x * sep_x + sep_y * sep_y + sep_z * sep_z + reach * reach)
                strength = table[which, 3:4, lanes] * root * root * root
                force_x = force_x + strength * sep_x
                force_y = force_y + strength * sep_y
                force_z = force_z + strength * sep_z
            return force_x, force_y, force_z

        sums = lax.fori_loop(0, listed, tile, (zero, zero, zero))
        out = zero
        for axis in range(3):
            force = mine[3] * jnp.sum(sums[axis], axis=1, keepdims=True)
            out = jnp.where(lane_ids == axis, force, out)
        results[place, :] = out
        return carry

    lax.fori_loop(0, n_blocks, block, 0)
    columns[...] = jnp.transpose(results[...])
    forces[...] = columns[0:3, :]


VMEM = pl.BlockSpec(memory_space=pltpu.VMEM)
SMEM = pl.BlockSpec(memory_space=pltpu.SMEM)


def shaped(*shape):
    return jax.ShapeDtypeStruct(shape, jnp.float32)


def buffer(*shape):
    return pltpu.VMEM(shape, jnp.float32)


def limit(mib):
    return pltpu.CompilerParams(vmem_limit_bytes=mib * MIB)


def solve_poisson(plan, density, codes, first_code, n_blocks, block_atoms):
    x_len, y_len, grid = density.shape
    y_pad, x_pad, half, lanes = plan.y_pad, plan.x_pad, plan.half, plan.lanes
    total = plan.parts * plan.modes
    z_table = table_triple(plan.z_matrix(), 0)
    y_table = table_triple(plan.y_matrix(), 1)
    diagonal = f32(plan.diagonal())
    edge_y = f32(plan.edge_weights())
    interface = plan.interface_table()
    shared = [
        buffer(x_len, y_pad, 128),
        buffer(x_len, y_pad, 128),
        buffer(plan.stack_rows, lanes),
        buffer(plan.lane_tiles, x_pad, 128),
    ]
    spectrum, message = pl.pallas_call(
        functools.partial(forward_kernel, plan, n_blocks, block_atoms),
        out_shape=(shaped(x_len, y_pad, lanes), shaped(total, 1, 2 * half)),
        in_specs=[SMEM] * 2 + [VMEM] * 6,
        out_specs=(VMEM, VMEM),
        scratch_shapes=[buffer(plan.lane_tiles * plan.planes, 128)] * COPIES
        + shared
        + [buffer(2, x_pad, 128), buffer(lanes, 2 * half)],
        compiler_params=limit(44),
        name="forward_solve",
    )(
        codes,
        first_code,
        density,
        z_table,
        y_table,
        diagonal,
        edge_y,
        table_triple(interface, 0),
    )
    incoming = lax.all_to_all(message, ("gx", "gy"), split_axis=0, concat_axis=0, tiled=True)
    gather = plan.gather_table()
    along_y, along_x = plan.line_tables()
    expand = plan.expand_table()
    position = lax.axis_index("gx") * plan.n_gy + lax.axis_index("gy")
    first_mode = (position * plan.modes).astype(jnp.int32).reshape(1)
    stiff = stiffness(grid, grid)
    padded_z = np.zeros(total)
    padded_z[:grid] = stiff
    padded_y = np.zeros((1, lanes))
    padded_y[0, :grid] = stiff
    outgoing = pl.pallas_call(
        functools.partial(interface_kernel, plan),
        out_shape=shaped(total, 1, 2 * half),
        in_specs=[SMEM] * 2 + [VMEM] * 11,
        out_specs=VMEM,
        scratch_shapes=[
            buffer(plan.modes, 2 * plan.parts, half),
            buffer(plan.modes, plan.kx_pad, lanes),
            buffer(plan.modes, plan.j_pad, lanes),
            buffer(plan.modes, gather.shape[0], half),
        ],
        compiler_params=limit(40),
        name="interface_solve",
    )(
        first_mode,
        f32((padded_z + SCREENING) * grid),
        incoming,
        table_triple(gather, 1),
        table_triple(gather.T, 1),
        table_triple(along_y, 0),
        table_triple(along_x, 0),
        table_triple(along_y.reshape(-1, lanes).T, 0),
        table_triple(along_x.reshape(-1, lanes).T, 0),
        f32(table_triple(expand, 0)),
        table_triple(expand, 1),
        f32(stiff[:, None] * grid),
        f32(padded_y * grid),
    )
    returned = lax.all_to_all(outgoing, ("gx", "gy"), split_axis=0, concat_axis=0, tiled=True)
    return pl.pallas_call(
        functools.partial(backward_kernel, plan, n_blocks, block_atoms),
        out_shape=(shaped(x_len, y_len, grid), shaped(plan.n_gx * n_blocks, 128)),
        in_specs=[SMEM] * 2 + [VMEM] * 7,
        out_specs=(VMEM, VMEM),
        scratch_shapes=[
            buffer(plan.lane_tiles * plan.planes, 128),
            buffer(x_len, y_pad, lanes),
        ]
        + shared
        + [buffer(x_pad, 128), buffer(lanes, 2 * half), buffer(block_atoms, 128)],
        compiler_params=limit(36),
        name="backward_solve",
    )(
        codes,
        first_code,
        spectrum,
        returned,
        z_table,
        y_table,
        diagonal,
        edge_y,
        table_triple(interface, 1),
    )


def shifted(block, axis, step):
    count = lax.axis_size(axis)
    return lax.ppermute(block, axis, [(i, (i + step) % count) for i in range(count)])


def body(
    qm_density,
    mm_coords,
    mm_charge,
    mm_types,
    type_radius,
    mm_cells,
    block_counts,
    block_owner,
    neighbour_tiles,
):
    n_blocks = block_counts.shape[2]
    tile_atoms = mm_charge.shape[2]
    block_atoms = tile_atoms // n_blocks
    x_local, local_y_rows, grid_len = qm_density.shape
    n_gx = lax.axis_size("gx")
    plan = Plan(x_local, local_y_rows, grid_len, n_gx, lax.axis_size("gy"))
    atoms = jnp.arange(tile_atoms, dtype=jnp.int32)
    per_atom = jnp.repeat(
        jnp.stack([block_counts.reshape(n_blocks), block_owner.reshape(n_blocks)]),
        block_atoms,
        axis=1,
    )
    live = (atoms % block_atoms < per_atom[0]).astype(jnp.float32)
    charge_live = mm_charge.reshape(tile_atoms) * live
    cells = mm_cells.reshape(tile_atoms)
    line, depth = cells // grid_len, cells % grid_len
    plane = (line // local_y_rows) * plan.y_pad + line % local_y_rows
    code = ((depth // 128) * plan.planes + plane) * 128 + depth % 128
    code = (per_atom[1] * plan.span + code).astype(jnp.float32)
    payload = jnp.concatenate([code, charge_live]).reshape(1, 2 * tile_atoms)
    type_count = type_radius.shape[0]
    type_match = mm_types.reshape(1, tile_atoms) == jnp.arange(type_count)[:, None]
    atom_radius = jnp.sum(jnp.where(type_match, type_radius[:, None], 0.0), axis=0)
    atom_rows = jnp.concatenate(
        [mm_coords.reshape(3, tile_atoms), charge_live[None, :], atom_radius[None, :]], axis=0
    )[None]
    copies = jnp.broadcast_to(payload[None], (n_gx, 1, 2 * tile_atoms))
    codes = lax.all_to_all(copies, "gx", split_axis=0, concat_axis=0, tiled=True)
    codes = codes.reshape(n_gx, 2 * tile_atoms)
    first_code = (lax.axis_index("gx") * plan.span).astype(jnp.int32).reshape(1)
    triple = jnp.concatenate(
        [shifted(atom_rows, "gx", 1), atom_rows, shifted(atom_rows, "gx", -1)], axis=0
    )
    below, above = shifted(triple, "gy", 1), shifted(triple, "gy", -1)
    listed = neighbour_tiles.shape[3]
    pair_force = pl.pallas_call(
        functools.partial(pair_kernel, n_blocks, block_atoms, listed),
        out_shape=shaped(3, tile_atoms),
        in_specs=[SMEM] + [VMEM] * 3,
        out_specs=VMEM,
        scratch_shapes=[
            buffer(9, 8, tile_atoms),
            buffer(128, tile_atoms),
            buffer(tile_atoms, 128),
        ],
        compiler_params=limit(16),
        cost_estimate=pl.CostEstimate(
            flops=21 * listed * tile_atoms * tile_atoms,
            bytes_accessed=4 * 50 * tile_atoms,
            transcendentals=listed * tile_atoms * tile_atoms,
        ),
        name="pair_forces",
    )(neighbour_tiles.reshape(n_blocks, listed), below, triple, above)
    potential, values = solve_poisson(
        plan, qm_density, codes, first_code, n_blocks, block_atoms
    )
    values = lax.all_to_all(values, "gx", split_axis=0, concat_axis=0, tiled=True)
    sampled = jnp.sum(values.reshape(n_gx, n_blocks, 128), axis=0)[:, :block_atoms]
    mm_potential = (sampled.reshape(tile_atoms) * live).reshape(1, 1, tile_atoms)
    return (potential, mm_potential, pair_force.reshape(1, 1, 3, tile_atoms))


def solution(mesh):
    placed = (
        P("gx", "gy", None),
        P("gx", "gy", None, None),
        P("gx", "gy", None),
        P("gx", "gy", None),
        P(),
        P("gx", "gy", None),
        P("gx", "gy", None),
        P("gx", "gy", None, None),
        P("gx", "gy", None, None),
    )
    return jax.shard_map(
        body,
        mesh=mesh,
        in_specs=placed,
        out_specs=(P("gx", "gy", None), P("gx", "gy", None), P("gx", "gy", None, None)),
        check_vma=False,
    )
```

```python
import functools

import jax
import jax.numpy as jnp
import ml_dtypes
import numpy as np
from jax import lax
from jax.experimental import pallas as pl
from jax.experimental.pallas import tpu as pltpu
from jax.sharding import PartitionSpec as P

SCREENING = 0.003
HIGH_ACCURACY = lax.Precision.HIGHEST
COPIES = 4
VMEM_MIB = 60
MIB = 1024 * 1024


def round_up(value, unit):
    return -(-value // unit) * unit


def sine_matrix(length):
    nodes = np.arange(length, dtype=np.float64)
    return np.sqrt(2.0 / length) * np.sin(np.pi * np.outer(nodes, nodes) / length)


def cas_matrix(length):
    nodes = np.arange(length)
    angle = 2.0 * np.pi * (np.outer(nodes, nodes) % length) / length
    return np.cos(angle) + np.sin(angle)


def stiffness(count, length):
    return 4.0 * np.sin(np.pi * np.arange(count) / length) ** 2


def split_pair(matrix):
    full = np.asarray(matrix, np.float32)
    high = full.astype(ml_dtypes.bfloat16)
    low = (full - high.astype(np.float32)).astype(ml_dtypes.bfloat16)
    return high, low


def table_triple(matrix, axis):
    high, low = split_pair(matrix)
    return np.concatenate([high, low, high], axis=axis)


def f32(table):
    return np.asarray(table, np.float32)


class Plan:
    def __init__(self, x_len, y_len, grid, n_gx, n_gy):
        self.x_len, self.y_len, self.grid = x_len, y_len, grid
        self.n_gx, self.n_gy = n_gx, n_gy
        self.y_pad = round_up(y_len, 8)
        self.x_pad = round_up(x_len, 8)
        self.lanes = round_up(grid, 128)
        self.lane_tiles = self.lanes // 128
        self.planes = x_len * self.y_pad
        self.span = self.lane_tiles * self.planes * 128
        self.parts = n_gx * n_gy
        self.modes = -(-grid // self.parts)
        self.half = round_up(y_len + x_len, 128)
        self.kx_pad = round_up(n_gx, 8)
        self.j_pad = round_up(n_gy, 8)
        self.stack_rows = round_up(3 * self.y_pad + 2 * self.x_pad, 128)

    def y_matrix(self):
        out = np.zeros((self.y_pad, self.y_pad))
        out[: self.y_len, : self.y_len] = sine_matrix(self.y_len)
        return out

    def z_matrix(self):
        out = np.zeros((self.lanes, self.lanes))
        out[: self.grid, : self.grid] = cas_matrix(self.grid) / np.sqrt(self.grid)
        return out

    def diagonal(self):
        z_part = np.zeros(self.lanes)
        z_part[: self.grid] = stiffness(self.grid, self.grid)
        y_part = stiffness(self.y_pad, 2 * self.y_len)
        return 2.0 + y_part[:, None] + z_part[None, :] + SCREENING

    def edge_weights(self):
        sine_y = self.y_matrix()
        both = np.stack([sine_y[1], sine_y[self.y_len - 1]])
        return np.broadcast_to(both[:, :, None], (2, self.y_pad, 128))

    def interface_table(self):
        x_len, y_len, half = self.x_len, self.y_len, self.half
        y_pad, x_pad = self.y_pad, self.x_pad
        sine_y = sine_matrix(y_len)
        out = np.zeros((self.stack_rows, 2 * half))
        out[:y_len, :y_len] = sine_y
        row = y_pad
        out[row : row + y_len, half : half + y_len] = sine_y
        row += y_pad
        out[row : row + y_len, :y_len] = np.eye(y_len)
        row += y_pad
        out[row + 1 : row + x_len, y_len + 1 : y_len + x_len] = np.eye(x_len - 1)
        row += x_pad
        far = half + y_len
        out[row + 1 : row + x_len, far + 1 : far + x_len] = np.eye(x_len - 1)
        return out

    def gather_table(self):
        n_gx, n_gy, parts = self.n_gx, self.n_gy, self.parts
        cas_x = cas_matrix(n_gx)
        out = np.zeros((n_gy * self.kx_pad + n_gx * self.j_pad, 2 * parts))
        for i in range(n_gx):
            for j in range(n_gy):
                col = i * n_gy + j
                base = j * self.kx_pad
                out[base : base + n_gx, col] = cas_x[:, i]
                out[base : base + n_gx, parts + col] = cas_x[:, (i + 1) % n_gx]
                base = n_gy * self.kx_pad + i * self.j_pad
                out[base + j, col] = 1.0
                out[base + (j + 1) % n_gy, parts + col] = 1.0
        return out

    def line_tables(self):
        scaled = cas_matrix(self.grid) / np.sqrt(self.grid)
        along_y = np.zeros((self.n_gy, self.half, self.lanes))
        along_x = np.zeros((self.n_gx, self.half, self.lanes))
        y_len, x_len, grid = self.y_len, self.x_len, self.grid
        for j in range(self.n_gy):
            along_y[j, :y_len, :grid] = scaled[j * y_len : (j + 1) * y_len]
        for i in range(self.n_gx):
            along_x[i, y_len : y_len + x_len, :grid] = scaled[i * x_len : (i + 1) * x_len]
        return along_y.reshape(-1, self.lanes), along_x.reshape(-1, self.lanes)

    def expand_table(self):
        ratio = self.grid // self.n_gy
        full = cas_matrix(self.grid)
        out = np.zeros((self.j_pad, self.lanes))
        for j in range(self.n_gy):
            out[j, : self.grid] = full[(j * ratio) % self.grid]
        return out


def dot(a, b, dims=((1,), (0,)), precision=None):
    return lax.dot_general(
        a, b, (dims, ((), ())), precision=precision, preferred_element_type=jnp.float32
    )


def value_triple(value, axis):
    high = value.astype(jnp.bfloat16).astype(jnp.float32)
    return jnp.concatenate([high, high, value - high], axis=axis).astype(jnp.bfloat16)


def left_apply(table, value):
    return dot(table, value_triple(value, 0))


def right_apply(value, table):
    return dot(value_triple(value, 1), table)


def slab_count(plan):
    if plan.y_pad != plan.y_len:
        return 1
    return max(count for count in (4, 3, 2, 1) if plan.x_len % count == 0)


def inverse(value):
    guess = pl.reciprocal(value, approx=True)
    guess = guess * (2.0 - value * guess)
    return guess * (2.0 - value * guess)


def start_copies(pairs, sems):
    copies = [
        pltpu.make_async_copy(source, target, sems.at[k])
        for k, (source, target) in enumerate(pairs)
    ]
    for copy in copies:
        copy.start()
    return copies


def list_owned(plan, places, blocks, n_blocks, block_atoms):
    rows = plan.lane_tiles * plan.planes

    def tile(source, count):
        for number in range(n_blocks):
            lead = places[source, number * block_atoms]
            blocks[count] = source * n_blocks + number
            count = count + jnp.where((lead >= 0) & (lead < rows), 1, 0)
        return count

    return lax.fori_loop(0, plan.n_gx, tile, 0)


def chunked_loop(count, unroll, body, init):
    while count % unroll:
        unroll -= 1

    def group(step, carry):
        for k in range(unroll):
            carry = body(step * unroll + k, carry)
        return carry

    return lax.fori_loop(0, count // unroll, group, init)


def forward_kernel(
    plan,
    n_blocks,
    block_atoms,
    first_code,
    codes_hbm,
    density_hbm,
    z_table_hbm,
    y_table_hbm,
    diagonal_hbm,
    edge_y_hbm,
    interface_hbm,
    spectrum_hbm,
    places_hbm,
    message,
    *scratch,
):
    added = scratch[:COPIES]
    solved, factors, stack, heads, edge_rows, turned = scratch[COPIES : COPIES + 6]
    codes, density, z_table, y_table, diagonal, edge_y, interface = scratch[COPIES + 6 : COPIES + 13]
    spectrum, place_rows, places, charges, blocks, sems = scratch[COPIES + 13 :]
    x_len, y_len, y_pad, x_pad = plan.x_len, plan.y_len, plan.y_pad, plan.x_pad
    grid, lane_count, planes = plan.grid, plan.lanes, plan.planes
    slabs = slab_count(plan)
    tile_atoms = n_blocks * block_atoms
    lane_ids = lax.broadcasted_iota(jnp.int32, (1, 128), 1)
    loads = start_copies(
        [
            (codes_hbm, codes),
            (codes_hbm.at[:, pl.ds(tile_atoms, tile_atoms)], charges),
            (density_hbm, density),
            (z_table_hbm, z_table),
            (y_table_hbm, y_table),
            (diagonal_hbm, diagonal),
            (edge_y_hbm, edge_y),
            (interface_hbm, interface),
        ],
        sems,
    )
    loads[0].wait()
    code = codes[:, :tile_atoms].astype(jnp.int32) - first_code[0]
    place_rows[:, :tile_atoms] = lax.shift_right_arithmetic(code, 7)
    place_rows[:, tile_atoms:] = code & 127
    place_copies = [
        pltpu.make_async_copy(place_rows, places, sems.at[8]),
        pltpu.make_async_copy(place_rows, places_hbm, sems.at[9]),
    ]
    for copy in place_copies:
        copy.start()

    def clear(step, carry):
        for copy in added:
            copy[pl.ds(pl.multiple_of(step * y_pad, 8), y_pad), :] = jnp.zeros(
                (y_pad, 128), jnp.float32
            )
        return carry

    chunked_loop(plan.lane_tiles * x_len, 4, clear, 0)
    loads[1].wait()
    place_copies[0].wait()
    count = list_owned(plan, places, blocks, n_blocks, block_atoms)

    def deposit(slot, carry):
        block = blocks[slot]
        source = block // n_blocks
        start = (block - source * n_blocks) * block_atoms
        for lead in range(0, block_atoms, COPIES):
            rows = [pl.ds(places[source, start + lead + k], 1) for k in range(COPIES)]
            sums = []
            for k in range(COPIES):
                lane = places[source, start + lead + k + tile_atoms]
                charge = charges[source, start + lead + k]
                sums.append(added[k][rows[k], :] + jnp.where(lane_ids == lane, charge, 0.0))
            for k in range(COPIES):
                added[k][rows[k], :] = sums[k]
        return carry

    lax.fori_loop(0, count, deposit, 0)
    for copy in loads[2:5]:
        copy.wait()

    def transform(step, carry):
        start = step * slabs
        count = slabs * y_pad
        pieces = []
        for tile in range(plan.lane_tiles):
            low = tile * 128
            width = min(128, grid - low)
            piece = density[pl.ds(start, slabs), :, low : low + width]
            if y_pad == y_len:
                piece = piece.reshape(count, width)
            else:
                rows = jnp.zeros((y_pad - y_len, width), jnp.float32)
                piece = jnp.concatenate([piece[0], rows], axis=0)
            if width < 128:
                rest = jnp.zeros((count, 128 - width), jnp.float32)
                piece = jnp.concatenate([piece, rest], axis=1)
            place = pl.ds(pl.multiple_of(tile * planes + start * y_pad, 8), count)
            for copy in added:
                piece = piece + copy[place, :]
            pieces.append(piece)
        lines = right_apply(jnp.concatenate(pieces, axis=1), z_table[...])
        lines = lines.reshape(slabs, y_pad, lane_count)
        for slab in range(slabs):
            x = start + slab
            for tile in range(plan.lane_tiles):
                heads[tile, pl.ds(x, 1), :] = lines[slab, 0:1, tile * 128 : tile * 128 + 128]
            spectrum[x] = left_apply(y_table[...], lines[slab])

        @pl.when(step == 0)
        def _():
            stack[2 * y_pad : 3 * y_pad, :] = lines[0]

        return carry

    chunked_loop(x_len // slabs, 3, transform, 0)
    spectrum_copy = pltpu.make_async_copy(spectrum, spectrum_hbm, sems.at[10])
    spectrum_copy.start()
    for copy in loads[5:8]:
        copy.wait()
    stack[3 * y_pad :, :] = jnp.zeros((stack.shape[0] - 3 * y_pad, lane_count), jnp.float32)
    for tile in range(plan.lane_tiles):
        lanes = slice(tile * 128, tile * 128 + 128)
        near_weight = edge_y[0]
        far_weight = edge_y[1]

        def eliminate(step, carry):
            factor, value = carry
            x = step + 1
            factor = inverse(diagonal[:, lanes] - factor)
            value = (spectrum[x, :, lanes] + value) * factor
            factors[x] = factor
            solved[x] = value
            return factor, value

        def substitute(step, value):
            x = x_len - 1 - step
            value = solved[x] + factors[x] * value
            near_row = jnp.sum(value * near_weight, axis=0, keepdims=True)
            far_row = jnp.sum(value * far_weight, axis=0, keepdims=True)
            edge_rows[0, pl.ds(x, 1), :] = near_row + heads[tile, pl.ds(x, 1), :]
            edge_rows[1, pl.ds(x, 1), :] = far_row
            return value

        zero = jnp.zeros((y_pad, 128), jnp.float32)
        chunked_loop(x_len - 1, 5, eliminate, (zero, zero))
        stack[y_pad : 2 * y_pad, lanes] = solved[x_len - 1]
        stack[0:y_pad, lanes] = chunked_loop(x_len - 1, 5, substitute, zero)
        for side in range(2):
            row = 3 * y_pad + side * x_pad
            stack[row + 1 : row + x_len, lanes] = edge_rows[side, 1:x_len, :]
    turned[...] = right_apply(jnp.transpose(stack[...]), interface[...])
    total = plan.parts * plan.modes
    for mode in range(grid):
        message[mode] = turned[mode : mode + 1, :]
    if total > grid:
        message[grid:total] = jnp.zeros((total - grid, 1, 2 * plan.half), jnp.float32)
    spectrum_copy.wait()
    place_copies[1].wait()


def interface_kernel(
    plan,
    first_mode,
    stiff_z,
    earlier_hbm,
    incoming_hbm,
    gather_hbm,
    along_y_hbm,
    along_x_hbm,
    expand_hbm,
    expand_back_hbm,
    stiff_x_hbm,
    stiff_y_hbm,
    along_y_back_hbm,
    along_x_back_hbm,
    scatter_hbm,
    outgoing,
    rows,
    folded_y,
    folded_x,
    lines,
    incoming,
    gather,
    along_y,
    along_x,
    expand,
    expand_back,
    stiff_x,
    stiff_y,
    along_y_back,
    along_x_back,
    scatter,
    sems,
):
    loads = start_copies(
        [
            (incoming_hbm, incoming),
            (gather_hbm, gather),
            (along_y_hbm, along_y),
            (along_x_hbm, along_x),
            (expand_hbm, expand),
            (expand_back_hbm, expand_back),
            (stiff_x_hbm, stiff_x),
            (stiff_y_hbm, stiff_y),
            (along_y_back_hbm, along_y_back),
            (along_x_back_hbm, along_x_back),
            (scatter_hbm, scatter),
        ],
        sems,
    )
    grid, half, parts, modes = plan.grid, plan.half, plan.parts, plan.modes
    kx_pad, j_pad, n_gx, n_gy = plan.kx_pad, plan.j_pad, plan.n_gx, plan.n_gy
    lane_count = plan.lanes
    groups = grid // n_gx

    def collect(source, carry):
        for mode in range(modes):
            both = incoming[source * modes + mode]
            rows[mode, pl.ds(source, 1), :] = both[:, :half]
            rows[mode, pl.ds(parts + source, 1), :] = both[:, half:]
        return carry

    loads[0].wait()
    lax.fori_loop(0, parts, collect, 0)
    loads[1].wait()
    for mode in range(modes):
        lines[mode] = left_apply(gather[...], rows[mode])
    base = n_gy * kx_pad
    y_slots = [slice(j * kx_pad, (j + 1) * kx_pad) for j in range(n_gy)]
    x_slots = [slice(base + i * j_pad, base + (i + 1) * j_pad) for i in range(n_gx)]

    def side_by_side(slots, count):
        return jnp.concatenate(
            [lines[:, slot, :].reshape(modes * count, half) for slot in slots], axis=1
        )

    loads[2].wait()
    loads[3].wait()
    folded_y[...] = right_apply(side_by_side(y_slots, kx_pad), along_y[...]).reshape(
        modes, kx_pad, lane_count
    )
    folded_x[...] = right_apply(side_by_side(x_slots, j_pad), along_x[...]).reshape(
        modes, j_pad, lane_count
    )

    def solve(mode, carry):
        across = folded_x[mode, :, :grid]
        high = across.astype(jnp.bfloat16).astype(jnp.float32)
        across = jnp.concatenate([high, high, across - high], axis=0)
        spread = dot(across, expand[...], ((0,), (0,)))
        number = spread.reshape(groups, kx_pad, lane_count) + folded_y[mode][None]
        bottom = stiff_x[...] + (stiff_y[...] + stiff_z[first_mode[0] + mode])
        value = number * inverse(bottom).reshape(groups, kx_pad, lane_count)
        folded_y[mode] = jnp.sum(value, axis=0)
        value = value_triple(value.reshape(grid, lane_count), 1)
        folded_x[mode, :, :grid] = dot(expand_back[...], value, ((1,), (1,)))
        return carry

    for copy in loads[4:8]:
        copy.wait()
    chunked_loop(modes, 3, solve, 0)
    for copy in loads[8:]:
        copy.wait()
    all_y = right_apply(folded_y[...].reshape(modes * kx_pad, lane_count), along_y_back[...])
    for j, slot in enumerate(y_slots):
        lines[:, slot, :] = all_y[:, j * half : (j + 1) * half].reshape(modes, kx_pad, half)
    all_x = right_apply(folded_x[...].reshape(modes * j_pad, lane_count), along_x_back[...])
    for i, slot in enumerate(x_slots):
        lines[:, slot, :] = all_x[:, i * half : (i + 1) * half].reshape(modes, j_pad, half)
    for mode in range(modes):
        rows[mode] = left_apply(scatter[...], lines[mode])

    def distribute(target, carry):
        for mode in range(modes):
            outgoing[target * modes + mode, :, :half] = rows[mode, pl.ds(target, 1), :]
            outgoing[target * modes + mode, :, half:] = rows[mode, pl.ds(parts + target, 1), :]
        return carry

    lax.fori_loop(0, parts, distribute, 0)


def backward_kernel(
    plan,
    n_blocks,
    block_atoms,
    places_hbm,
    message_hbm,
    interface_hbm,
    diagonal_hbm,
    edge_y_hbm,
    spectrum_hbm,
    y_table_hbm,
    z_table_hbm,
    potential_hbm,
    values,
    lookup,
    work,
    solved,
    factors,
    stack,
    heads,
    edge_rows,
    turned,
    picked,
    potential,
    places,
    message,
    interface,
    diagonal,
    edge_y,
    spectrum,
    y_table,
    z_table,
    blocks,
    sems,
):
    x_len, y_len, y_pad, x_pad = plan.x_len, plan.y_len, plan.y_pad, plan.x_pad
    grid, lane_count, planes = plan.grid, plan.lanes, plan.planes
    slabs = slab_count(plan)
    tile_atoms = n_blocks * block_atoms
    loads = start_copies(
        [
            (message_hbm, message),
            (interface_hbm, interface),
            (places_hbm, places),
            (diagonal_hbm, diagonal),
            (edge_y_hbm, edge_y),
            (spectrum_hbm, spectrum),
            (y_table_hbm, y_table),
            (z_table_hbm, z_table),
        ],
        sems,
    )
    loads[0].wait()
    for mode in range(grid):
        turned[mode : mode + 1, :] = message[mode]
    if lane_count > grid:
        turned[grid:, :] = jnp.zeros((lane_count - grid, turned.shape[1]), jnp.float32)
    loads[1].wait()
    stack[...] = dot(interface[...], value_triple(turned[...], 1), ((1,), (1,)))
    loads[2].wait()
    count = list_owned(plan, places, blocks, n_blocks, block_atoms)
    for copy in loads[3:]:
        copy.wait()
    for tile in range(plan.lane_tiles):
        lanes = slice(tile * 128, tile * 128 + 128)
        near_weight = edge_y[0]
        far_weight = edge_y[1]
        heads[tile] = stack[3 * y_pad : 3 * y_pad + x_pad, lanes]
        edge_rows[...] = stack[3 * y_pad + x_pad : 3 * y_pad + 2 * x_pad, lanes]

        def eliminate(step, carry):
            factor, value = carry
            x = step + 1
            factor = inverse(diagonal[:, lanes] - factor)
            load = spectrum[x, :, lanes] + near_weight * heads[tile, pl.ds(x, 1), :]
            load = load + far_weight * edge_rows[pl.ds(x, 1), :]
            value = (load + value) * factor
            factors[x] = factor
            solved[x] = value
            return factor, value

        def substitute(step, value):
            x = x_len - 1 - step
            value = solved[x] + factors[x] * value
            work[x, :, lanes] = value
            return value

        zero = jnp.zeros((y_pad, 128), jnp.float32)
        chunked_loop(x_len - 1, 5, eliminate, (zero, stack[0:y_pad, lanes]))
        chunked_loop(x_len - 1, 5, substitute, stack[y_pad : 2 * y_pad, lanes])
    work[0] = jnp.zeros((y_pad, lane_count), jnp.float32)

    def transform(step, carry):
        start = step * slabs
        for slab in range(slabs):
            x = start + slab
            work[x] = left_apply(y_table[...], work[x])
            for tile in range(plan.lane_tiles):
                lanes = slice(tile * 128, tile * 128 + 128)
                work[x, 0:1, lanes] = heads[tile, pl.ds(x, 1), :]

        @pl.when(step == 0)
        def _():
            work[0] = stack[2 * y_pad : 3 * y_pad, :]

        lines = work[pl.ds(start, slabs)].reshape(slabs * y_pad, lane_count)
        lines = right_apply(lines, z_table[...])
        for tile in range(plan.lane_tiles):
            low = tile * 128
            place = pl.ds(pl.multiple_of(tile * planes + start * y_pad, 8), slabs * y_pad)
            lookup[place, :] = lines[:, low : low + 128]
        lines = lines.reshape(slabs, y_pad, lane_count)
        potential[pl.ds(start, slabs)] = lines[:, :y_len, :grid]
        return carry

    chunked_loop(x_len // slabs, 3, transform, 0)
    potential_copy = pltpu.make_async_copy(potential, potential_hbm, sems.at[8])
    potential_copy.start()
    values[...] = jnp.zeros(values.shape, jnp.float32)
    lane_ids = lax.broadcasted_iota(jnp.int32, (1, 128), 1)
    shape = (block_atoms, 128)
    own_lane = lax.broadcasted_iota(jnp.int32, shape, 0) == lax.broadcasted_iota(
        jnp.int32, shape, 1
    )

    def sample(slot, carry):
        block = blocks[slot]
        source = block // n_blocks
        start = (block - source * n_blocks) * block_atoms
        for atom in range(block_atoms):
            row = lookup[pl.ds(places[source, start + atom], 1), :]
            lane = places[source, start + atom + tile_atoms]
            picked[atom : atom + 1, :] = jnp.where(lane_ids == lane, row, 0.0)
        found = jnp.sum(picked[...], axis=1, keepdims=True)
        found = jnp.sum(jnp.where(own_lane, found, 0.0), axis=0, keepdims=True)
        values[pl.ds(block, 1), :] = found
        return carry

    lax.fori_loop(0, count, sample, 0)
    potential_copy.wait()


def prepare_kernel(
    plan, n_blocks, block_atoms, counts, owners, type_radius, coords, charge, types, cells,
    copies, atom_rows,
):
    tile_atoms = n_blocks * block_atoms
    lane = lax.broadcasted_iota(jnp.int32, (1, 128), 1)
    slot = lane // block_atoms
    atom = lane - slot * block_atoms
    per_row = 128 // block_atoms
    for start in range(0, tile_atoms, 128):
        lanes = slice(start, start + 128)
        first = start // block_atoms
        count = jnp.full((1, 128), counts[0, first], jnp.int32)
        owner = jnp.full((1, 128), owners[0, first], jnp.int32)
        for k in range(1, per_row):
            count = jnp.where(slot >= k, counts[0, first + k], count)
            owner = jnp.where(slot >= k, owners[0, first + k], owner)
        live = jnp.where(atom < count, charge[0, :, lanes], 0.0)
        cell = cells[0, :, lanes]
        line = jnp.floor((cell.astype(jnp.float32) + 0.5) * (1.0 / plan.grid)).astype(jnp.int32)
        depth = cell - line * plan.grid
        x = jnp.floor((line.astype(jnp.float32) + 0.5) * (1.0 / plan.y_len)).astype(jnp.int32)
        plane = x * plan.y_pad + (line - x * plan.y_len)
        code = ((depth >> 7) * plan.planes + plane) * 128 + (depth & 127)
        code = (owner * plan.span + code).astype(jnp.float32)
        for target in range(plan.n_gx):
            copies[target, :, lanes] = code
            copies[target, :, tile_atoms + start : tile_atoms + start + 128] = live
        radius = jnp.zeros((1, 128), jnp.float32)
        for kind in range(type_radius.shape[0]):
            radius = jnp.where(types[0, :, lanes] == kind, type_radius[kind], radius)
        atom_rows[0, 0:3, lanes] = coords[0, 0, :, lanes]
        atom_rows[0, 3:4, lanes] = live
        atom_rows[0, 4:5, lanes] = radius


def pair_kernel(
    n_blocks, block_atoms, listed, listing, low, middle, high, forces, table, columns, results
):
    tile_atoms = n_blocks * block_atoms
    sides = (low, middle, high)
    for step_x in range(3):
        for step_y in range(3):
            rows = sides[step_y][step_x]
            shifts = (step_x - 1.0, step_y - 1.0, 0.0, 0.0, 0.0)
            for k in range(5):
                row = rows[k : k + 1, :]
                if shifts[k]:
                    row = row + shifts[k]
                table[step_x * 3 + step_y, k] = jnp.broadcast_to(row, (8, tile_atoms))
    columns[0:5, :] = middle[1]
    columns[5:, :] = jnp.zeros((columns.shape[0] - 5, tile_atoms), jnp.float32)
    results[...] = jnp.transpose(columns[...])
    lane_ids = lax.broadcasted_iota(jnp.int32, (block_atoms, 128), 1)
    groups = block_atoms // 8

    def block(number, carry):
        place = pl.ds(pl.multiple_of(number * block_atoms, block_atoms), block_atoms)
        own = results[place, :]
        mine = [
            jnp.broadcast_to(own[:, k : k + 1], (block_atoms, 128)).reshape(groups, 8, 128)
            for k in range(5)
        ]
        zero = jnp.zeros((groups, 8, 128), jnp.float32)

        def tile(slot, sums):
            force_x, force_y, force_z = sums
            which = listing[number, slot]
            for start in range(0, tile_atoms, 128):
                lanes = slice(start, start + 128)
                other = [table[which, k, :, lanes][None] for k in range(5)]
                sep_x = mine[0] - other[0]
                sep_y = mine[1] - other[1]
                sep_z = mine[2] - other[2]
                reach = mine[4] + other[4]
                root = lax.rsqrt(sep_x * sep_x + sep_y * sep_y + sep_z * sep_z + reach * reach)
                strength = other[3] * root * (root * root)
                force_x = force_x + strength * sep_x
                force_y = force_y + strength * sep_y
                force_z = force_z + strength * sep_z
            return force_x, force_y, force_z

        sums = lax.fori_loop(0, listed, tile, (zero, zero, zero))
        out = jnp.zeros((block_atoms, 128), jnp.float32)
        for axis in range(3):
            total = sums[axis].reshape(block_atoms, 128)
            force = own[:, 3:4] * jnp.sum(total, axis=1, keepdims=True)
            out = jnp.where(lane_ids == axis, force, out)
        results[place, :] = out
        return carry

    lax.fori_loop(0, n_blocks, block, 0)
    columns[...] = jnp.transpose(results[...])
    forces[...] = columns[0:3, :]


VMEM = pl.BlockSpec(memory_space=pltpu.VMEM)
SMEM = pl.BlockSpec(memory_space=pltpu.SMEM)
HBM = pl.BlockSpec(memory_space=pl.ANY)


def shaped(*shape):
    return jax.ShapeDtypeStruct(shape, jnp.float32)


def buffer(*shape):
    return pltpu.VMEM(shape, jnp.float32)


def like(table):
    return pltpu.VMEM(table.shape, table.dtype)


def limit(mib):
    return pltpu.CompilerParams(vmem_limit_bytes=mib * MIB)


def solve_poisson(plan, density, codes, first_code, n_blocks, block_atoms, earlier):
    x_len, y_len, grid = density.shape
    y_pad, x_pad, half, lanes = plan.y_pad, plan.x_pad, plan.half, plan.lanes
    total = plan.parts * plan.modes
    z_table = table_triple(plan.z_matrix(), 0)
    y_table = table_triple(plan.y_matrix(), 1)
    diagonal = f32(plan.diagonal())
    edge_y = f32(plan.edge_weights())
    interface = table_triple(plan.interface_table(), 0)
    interface_back = table_triple(plan.interface_table(), 1)
    n_rows, tile_atoms = codes.shape[0], n_blocks * block_atoms
    shared = [
        buffer(x_len, y_pad, 128),
        buffer(x_len, y_pad, 128),
        buffer(plan.stack_rows, lanes),
        buffer(plan.lane_tiles, x_pad, 128),
    ]
    spectrum, places, message = pl.pallas_call(
        functools.partial(forward_kernel, plan, n_blocks, block_atoms),
        out_shape=(
            shaped(x_len, y_pad, lanes),
            jax.ShapeDtypeStruct((n_rows, 2 * tile_atoms), jnp.int32),
            shaped(total, 1, 2 * half),
        ),
        in_specs=[SMEM] + [HBM] * 7,
        out_specs=(HBM, HBM, VMEM),
        scratch_shapes=[buffer(plan.lane_tiles * plan.planes, 128)] * COPIES
        + shared
        + [
            buffer(2, x_pad, 128),
            buffer(lanes, 2 * half),
            buffer(n_rows, 2 * tile_atoms),
            buffer(x_len, y_len, grid),
            like(z_table),
            like(y_table),
            like(diagonal),
            like(edge_y),
            like(interface),
            buffer(x_len, y_pad, lanes),
            pltpu.VMEM((n_rows, 2 * tile_atoms), jnp.int32),
            pltpu.SMEM((n_rows, 2 * tile_atoms), jnp.int32),
            pltpu.SMEM((n_rows, tile_atoms), jnp.float32),
            pltpu.SMEM((n_rows * n_blocks,), jnp.int32),
            pltpu.SemaphoreType.DMA((11,)),
        ],
        compiler_params=limit(VMEM_MIB),
        name="forward_solve",
    )(first_code, codes, density, z_table, y_table, diagonal, edge_y, interface)
    incoming = lax.all_to_all(message, ("gx", "gy"), split_axis=0, concat_axis=0, tiled=True)
    gather = plan.gather_table()
    along_y, along_x = plan.line_tables()
    expand = plan.expand_table()
    position = lax.axis_index("gx") * plan.n_gy + lax.axis_index("gy")
    first_mode = (position * plan.modes).astype(jnp.int32).reshape(1)
    stiff = stiffness(grid, grid)
    padded_z = np.zeros(total)
    padded_z[:grid] = stiff
    padded_y = np.zeros((1, lanes))
    padded_y[0, :grid] = stiff
    tables = [
        table_triple(gather, 1),
        table_triple(along_y, 0),
        table_triple(along_x, 0),
        f32(table_triple(expand, 0)),
        table_triple(expand, 1),
        f32(stiff[:, None] * grid),
        f32(padded_y * grid),
        table_triple(along_y.T, 0),
        table_triple(along_x.T, 0),
        table_triple(gather.T, 1),
    ]
    outgoing = pl.pallas_call(
        functools.partial(interface_kernel, plan),
        out_shape=shaped(total, 1, 2 * half),
        in_specs=[SMEM] * 2 + [HBM] * 12,
        out_specs=VMEM,
        scratch_shapes=[
            buffer(plan.modes, 2 * plan.parts, half),
            buffer(plan.modes, plan.kx_pad, lanes),
            buffer(plan.modes, plan.j_pad, lanes),
            buffer(plan.modes, gather.shape[0], half),
            buffer(total, 1, 2 * half),
            *[like(table) for table in tables],
            pltpu.SemaphoreType.DMA((11,)),
        ],
        compiler_params=limit(VMEM_MIB),
        name="interface_solve",
    )(first_mode, f32((padded_z + SCREENING) * grid), earlier, incoming, *tables)
    returned = lax.all_to_all(outgoing, ("gx", "gy"), split_axis=0, concat_axis=0, tiled=True)
    return pl.pallas_call(
        functools.partial(backward_kernel, plan, n_blocks, block_atoms),
        out_shape=(shaped(x_len, y_len, grid), shaped(plan.n_gx * n_blocks, 128)),
        in_specs=[HBM] * 8,
        out_specs=(HBM, VMEM),
        scratch_shapes=[
            buffer(plan.lane_tiles * plan.planes, 128),
            buffer(x_len, y_pad, lanes),
        ]
        + shared
        + [
            buffer(x_pad, 128),
            buffer(lanes, 2 * half),
            buffer(block_atoms, 128),
            buffer(x_len, y_len, grid),
            pltpu.SMEM((n_rows, 2 * tile_atoms), jnp.int32),
            buffer(total, 1, 2 * half),
            like(interface_back),
            like(diagonal),
            like(edge_y),
            buffer(x_len, y_pad, lanes),
            like(y_table),
            like(z_table),
            pltpu.SMEM((n_rows * n_blocks,), jnp.int32),
            pltpu.SemaphoreType.DMA((9,)),
        ],
        compiler_params=limit(VMEM_MIB),
        name="backward_solve",
    )(places, returned, interface_back, diagonal, edge_y, spectrum, y_table, z_table)


def shifted(block, axis, step):
    count = lax.axis_size(axis)
    return lax.ppermute(block, axis, [(i, (i + step) % count) for i in range(count)])


def body(
    qm_density,
    mm_coords,
    mm_charge,
    mm_types,
    type_radius,
    mm_cells,
    block_counts,
    block_owner,
    neighbour_tiles,
):
    n_blocks = block_counts.shape[2]
    tile_atoms = mm_charge.shape[2]
    block_atoms = tile_atoms // n_blocks
    x_local, local_y_rows, grid_len = qm_density.shape
    n_gx = lax.axis_size("gx")
    plan = Plan(x_local, local_y_rows, grid_len, n_gx, lax.axis_size("gy"))
    copies, atom_rows = pl.pallas_call(
        functools.partial(prepare_kernel, plan, n_blocks, block_atoms),
        out_shape=(shaped(n_gx, 1, 2 * tile_atoms), shaped(1, 5, tile_atoms)),
        in_specs=[SMEM] * 3 + [VMEM] * 4,
        out_specs=(VMEM, VMEM),
        compiler_params=limit(VMEM_MIB),
        name="prepare_atoms",
    )(
        block_counts.reshape(1, n_blocks),
        block_owner.reshape(1, n_blocks),
        type_radius,
        mm_coords,
        mm_charge,
        mm_types,
        mm_cells,
    )
    codes = lax.all_to_all(copies, "gx", split_axis=0, concat_axis=0, tiled=True)
    codes = codes.reshape(n_gx, 2 * tile_atoms)
    first_code = (lax.axis_index("gx") * plan.span).astype(jnp.int32).reshape(1)
    triple = jnp.concatenate(
        [shifted(atom_rows, "gx", 1), atom_rows, shifted(atom_rows, "gx", -1)], axis=0
    )
    below, above = shifted(triple, "gy", 1), shifted(triple, "gy", -1)
    listed = neighbour_tiles.shape[3]
    pair_force = pl.pallas_call(
        functools.partial(pair_kernel, n_blocks, block_atoms, listed),
        out_shape=shaped(3, tile_atoms),
        in_specs=[SMEM] + [VMEM] * 3,
        out_specs=VMEM,
        scratch_shapes=[
            buffer(9, 5, 8, tile_atoms),
            buffer(128, tile_atoms),
            buffer(tile_atoms, 128),
        ],
        compiler_params=limit(VMEM_MIB),
        cost_estimate=pl.CostEstimate(
            flops=21 * listed * tile_atoms * tile_atoms,
            bytes_accessed=4 * 50 * tile_atoms,
            transcendentals=listed * tile_atoms * tile_atoms,
        ),
        name="pair_forces",
    )(neighbour_tiles.reshape(n_blocks, listed), below, triple, above)
    potential, values = solve_poisson(
        plan, qm_density, codes, first_code, n_blocks, block_atoms, pair_force
    )
    values = lax.all_to_all(values, "gx", split_axis=0, concat_axis=0, tiled=True)
    sampled = jnp.sum(values.reshape(n_gx, n_blocks, 128), axis=0)[:, :block_atoms]
    lanes = jnp.arange(block_atoms, dtype=jnp.int32)
    live = lanes[None, :] < block_counts.reshape(n_blocks, 1)
    mm_potential = jnp.where(live, sampled, 0.0).reshape(1, 1, tile_atoms)
    return (potential, mm_potential, pair_force.reshape(1, 1, 3, tile_atoms))


def solution(mesh):
    placed = (
        P("gx", "gy", None),
        P("gx", "gy", None, None),
        P("gx", "gy", None),
        P("gx", "gy", None),
        P(),
        P("gx", "gy", None),
        P("gx", "gy", None),
        P("gx", "gy", None, None),
        P("gx", "gy", None, None),
    )
    return jax.shard_map(
        body,
        mesh=mesh,
        in_specs=placed,
        out_specs=(P("gx", "gy", None), P("gx", "gy", None), P("gx", "gy", None, None)),
        check_vma=False,
    )
```

```python
import functools

import jax
import jax.numpy as jnp
import ml_dtypes
import numpy as np
from jax import lax
from jax.experimental import pallas as pl
from jax.experimental.pallas import tpu as pltpu
from jax.sharding import PartitionSpec as P

SCREENING = 0.003
HIGH_ACCURACY = lax.Precision.HIGHEST
VMEM_MIB = 60
MIB = 1024 * 1024


def round_up(value, unit):
    return -(-value // unit) * unit


def sine_matrix(length):
    nodes = np.arange(length, dtype=np.float64)
    return np.sqrt(2.0 / length) * np.sin(np.pi * np.outer(nodes, nodes) / length)


def cas_matrix(length):
    nodes = np.arange(length)
    angle = 2.0 * np.pi * (np.outer(nodes, nodes) % length) / length
    return np.cos(angle) + np.sin(angle)


def stiffness(count, length):
    return 4.0 * np.sin(np.pi * np.arange(count) / length) ** 2


def split_pair(matrix):
    full = np.asarray(matrix, np.float32)
    high = full.astype(ml_dtypes.bfloat16)
    low = (full - high.astype(np.float32)).astype(ml_dtypes.bfloat16)
    return high, low


def table_triple(matrix, axis):
    high, low = split_pair(matrix)
    return np.concatenate([high, low, high], axis=axis)


def f32(table):
    return np.asarray(table, np.float32)


class Plan:
    def __init__(self, x_len, y_len, grid, n_gx, n_gy):
        self.x_len, self.y_len, self.grid = x_len, y_len, grid
        self.n_gx, self.n_gy = n_gx, n_gy
        self.y_pad = round_up(y_len, 8)
        self.x_pad = round_up(x_len, 8)
        self.lanes = round_up(grid, 128)
        self.lane_tiles = self.lanes // 128
        self.planes = x_len * self.y_pad
        self.span = self.lane_tiles * self.planes * 128
        self.parts = n_gx * n_gy
        self.modes = -(-grid // self.parts)
        self.half = round_up(y_len + x_len, 128)
        self.kx_pad = round_up(n_gx, 8)
        self.j_pad = round_up(n_gy, 8)
        self.stack_rows = round_up(3 * self.y_pad + 2 * self.x_pad, 128)

    def y_matrix(self):
        out = np.zeros((self.y_pad, self.y_pad))
        out[: self.y_len, : self.y_len] = sine_matrix(self.y_len)
        return out

    def z_matrix(self):
        out = np.zeros((self.lanes, self.lanes))
        out[: self.grid, : self.grid] = cas_matrix(self.grid) / np.sqrt(self.grid)
        return out

    def diagonal(self):
        z_part = np.zeros(self.lanes)
        z_part[: self.grid] = stiffness(self.grid, self.grid)
        y_part = stiffness(self.y_pad, 2 * self.y_len)
        return 2.0 + y_part[:, None] + z_part[None, :] + SCREENING

    def edge_weights(self):
        sine_y = self.y_matrix()
        both = np.stack([sine_y[1], sine_y[self.y_len - 1]])
        return np.broadcast_to(both[:, :, None], (2, self.y_pad, 128))

    def interface_table(self):
        x_len, y_len, half = self.x_len, self.y_len, self.half
        y_pad, x_pad = self.y_pad, self.x_pad
        sine_y = sine_matrix(y_len)
        out = np.zeros((self.stack_rows, 2 * half))
        out[:y_len, :y_len] = sine_y
        row = y_pad
        out[row : row + y_len, half : half + y_len] = sine_y
        row += y_pad
        out[row : row + y_len, :y_len] = np.eye(y_len)
        row += y_pad
        out[row + 1 : row + x_len, y_len + 1 : y_len + x_len] = np.eye(x_len - 1)
        row += x_pad
        far = half + y_len
        out[row + 1 : row + x_len, far + 1 : far + x_len] = np.eye(x_len - 1)
        return out

    def gather_table(self):
        n_gx, n_gy, parts = self.n_gx, self.n_gy, self.parts
        cas_x = cas_matrix(n_gx)
        out = np.zeros((n_gy * self.kx_pad + n_gx * self.j_pad, 2 * parts))
        for i in range(n_gx):
            for j in range(n_gy):
                col = i * n_gy + j
                base = j * self.kx_pad
                out[base : base + n_gx, col] = cas_x[:, i]
                out[base : base + n_gx, parts + col] = cas_x[:, (i + 1) % n_gx]
                base = n_gy * self.kx_pad + i * self.j_pad
                out[base + j, col] = 1.0
                out[base + (j + 1) % n_gy, parts + col] = 1.0
        return out

    def line_tables(self):
        scaled = cas_matrix(self.grid) / np.sqrt(self.grid)
        along_y = np.zeros((self.n_gy, self.half, self.lanes))
        along_x = np.zeros((self.n_gx, self.half, self.lanes))
        y_len, x_len, grid = self.y_len, self.x_len, self.grid
        for j in range(self.n_gy):
            along_y[j, :y_len, :grid] = scaled[j * y_len : (j + 1) * y_len]
        for i in range(self.n_gx):
            along_x[i, y_len : y_len + x_len, :grid] = scaled[i * x_len : (i + 1) * x_len]
        return along_y.reshape(-1, self.lanes), along_x.reshape(-1, self.lanes)

    def expand_table(self):
        ratio = self.grid // self.n_gy
        full = cas_matrix(self.grid)
        out = np.zeros((self.j_pad, self.lanes))
        for j in range(self.n_gy):
            out[j, : self.grid] = full[(j * ratio) % self.grid]
        return out


def dot(a, b, dims=((1,), (0,)), precision=None):
    return lax.dot_general(
        a, b, (dims, ((), ())), precision=precision, preferred_element_type=jnp.float32
    )


def value_triple(value, axis):
    high = value.astype(jnp.bfloat16).astype(jnp.float32)
    return jnp.concatenate([high, high, value - high], axis=axis).astype(jnp.bfloat16)


def split_table(source, target, axis):
    value = source[...]
    high = value.astype(jnp.bfloat16).astype(jnp.float32)
    parts = jnp.concatenate([high, value - high, high], axis=axis)
    target[...] = parts.astype(jnp.bfloat16)


def left_apply(table, value):
    return dot(table, value_triple(value, 0))


def right_apply(value, table):
    return dot(value_triple(value, 1), table)


def slab_count(plan):
    if plan.y_pad != plan.y_len:
        return 1
    return max(count for count in (4, 3, 2, 1) if plan.x_len % count == 0)


def inverse(value):
    guess = pl.reciprocal(value, approx=True)
    guess = guess * (2.0 - value * guess)
    return guess * (2.0 - value * guess)


def start_copies(pairs, sems):
    copies = [
        pltpu.make_async_copy(source, target, sems.at[k])
        for k, (source, target) in enumerate(pairs)
    ]
    for copy in copies:
        copy.start()
    return copies


def list_owned(plan, places, blocks, n_blocks, block_atoms):
    rows = plan.lane_tiles * plan.planes

    def tile(source, count):
        for number in range(n_blocks):
            lead = places[source, number * block_atoms]
            blocks[count] = source * n_blocks + number
            count = count + jnp.where((lead >= 0) & (lead < rows), 1, 0)
        return count

    return lax.fori_loop(0, plan.n_gx, tile, 0)


def chunked_loop(count, unroll, body, init):
    while count % unroll:
        unroll -= 1

    def group(step, carry):
        for k in range(unroll):
            carry = body(step * unroll + k, carry)
        return carry

    return lax.fori_loop(0, count // unroll, group, init)


def mark_places(plan, codes, first_code, place_rows, tile_atoms, block_atoms):
    lane = lax.broadcasted_iota(jnp.int32, (codes.shape[0], 128), 1) % block_atoms
    for start in range(0, tile_atoms, 128):
        lanes = slice(start, start + 128)
        code = codes[:, lanes].astype(jnp.int32) - first_code
        place = lax.shift_right_arithmetic(code, 7)
        shared = jnp.zeros_like(place)
        for step in range(1, block_atoms):
            same = (pltpu.roll(place, step, 1) == place) & (lane >= step)
            shared = jnp.where(same, 1, shared)
        step = block_atoms // 2
        while step:
            shared = shared | pltpu.roll(shared, 128 - step, 1)
            step //= 2
        place_rows[:, lanes] = place
        mark = jnp.where(lane == 0, shared * 128, 0)
        place_rows[:, tile_atoms + start : tile_atoms + start + 128] = (code & 127) + mark


def forward_kernel(
    plan,
    n_blocks,
    block_atoms,
    first_code,
    *refs,
):
    (
        codes_hbm,
        density_hbm,
        z_full_hbm,
        y_table_hbm,
        diagonal_hbm,
        edge_y_hbm,
        interface_hbm,
        _,
        _,
        spectrum_hbm,
        places_hbm,
        message,
        added,
        solved,
        factors,
        stack,
        heads,
        edge_rows,
        turned,
        codes_in,
        codes,
        density,
        z_full,
        z_table,
        y_table,
        diagonal,
        edge_y,
        interface_full,
        interface,
        spectrum,
        place_rows,
        charge_rows,
        places,
        charges,
        blocks,
        sems,
    ) = refs
    x_len, y_len, y_pad, x_pad = plan.x_len, plan.y_len, plan.y_pad, plan.x_pad
    grid, lane_count, planes = plan.grid, plan.lanes, plan.planes
    slabs = slab_count(plan)
    tile_atoms = n_blocks * block_atoms
    lane_ids = lax.broadcasted_iota(jnp.int32, (1, 128), 1)
    loads = start_copies(
        [
            (codes_hbm, codes_in),
            (density_hbm, density),
            (z_full_hbm, z_full),
            (y_table_hbm, y_table),
            (diagonal_hbm, diagonal),
            (edge_y_hbm, edge_y),
            (interface_hbm, interface_full),
        ],
        sems,
    )
    loads[0].wait()
    for source in range(plan.n_gx):
        codes[source : source + 1, :] = codes_in[source, :, :tile_atoms]
        charge_rows[source : source + 1, :] = codes_in[source, :, tile_atoms:]
    charge_copy = pltpu.make_async_copy(charge_rows, charges, sems.at[7])
    charge_copy.start()
    mark_places(plan, codes, first_code[0], place_rows, tile_atoms, block_atoms)
    place_copies = [
        pltpu.make_async_copy(place_rows, places, sems.at[8]),
        pltpu.make_async_copy(place_rows, places_hbm, sems.at[9]),
    ]
    for copy in place_copies:
        copy.start()

    def clear(step, carry):
        place = pl.ds(pl.multiple_of(step * y_pad, 8), y_pad)
        added[place, :] = jnp.zeros((y_pad, 128), jnp.float32)
        return carry

    chunked_loop(plan.lane_tiles * x_len, 4, clear, 0)
    loads[2].wait()
    split_table(z_full, z_table, 0)
    charge_copy.wait()
    place_copies[0].wait()
    count = list_owned(plan, places, blocks, n_blocks, block_atoms)

    def deposit(slot, carry):
        block = blocks[slot]
        source = block // n_blocks
        start = (block - source * n_blocks) * block_atoms
        lead = places[source, start + tile_atoms]

        def row_of(k):
            return pl.ds(places[source, start + k], 1)

        def raised(k):
            lane = places[source, start + k + tile_atoms] & 127
            hit = jnp.where(lane_ids == lane, charges[source, start + k], 0.0)
            return added[row_of(k), :] + hit

        @pl.when(lead < 128)
        def _():
            rows = [raised(k) for k in range(block_atoms)]
            for k in range(block_atoms):
                added[row_of(k), :] = rows[k]

        @pl.when(lead >= 128)
        def _():
            for k in range(block_atoms):
                added[row_of(k), :] = raised(k)

        return carry

    lax.fori_loop(0, count, deposit, 0)
    loads[1].wait()
    loads[3].wait()

    def transform(step, carry):
        start = step * slabs
        count = slabs * y_pad
        pieces = []
        for tile in range(plan.lane_tiles):
            low = tile * 128
            width = min(128, grid - low)
            piece = density[pl.ds(start, slabs), :, low : low + width]
            if y_pad == y_len:
                piece = piece.reshape(count, width)
            else:
                rows = jnp.zeros((y_pad - y_len, width), jnp.float32)
                piece = jnp.concatenate([piece[0], rows], axis=0)
            if width < 128:
                rest = jnp.zeros((count, 128 - width), jnp.float32)
                piece = jnp.concatenate([piece, rest], axis=1)
            place = pl.ds(pl.multiple_of(tile * planes + start * y_pad, 8), count)
            pieces.append(piece + added[place, :])
        lines = right_apply(jnp.concatenate(pieces, axis=1), z_table[...])
        lines = lines.reshape(slabs, y_pad, lane_count)
        for slab in range(slabs):
            x = start + slab
            for tile in range(plan.lane_tiles):
                heads[tile, pl.ds(x, 1), :] = lines[slab, 0:1, tile * 128 : tile * 128 + 128]
            spectrum[x] = left_apply(y_table[...], lines[slab])

        @pl.when(step == 0)
        def _():
            stack[2 * y_pad : 3 * y_pad, :] = lines[0]

        return carry

    chunked_loop(x_len // slabs, 3, transform, 0)
    spectrum_copy = pltpu.make_async_copy(spectrum, spectrum_hbm, sems.at[10])
    spectrum_copy.start()
    for copy in loads[4:]:
        copy.wait()
    split_table(interface_full, interface, 0)
    stack[3 * y_pad :, :] = jnp.zeros((stack.shape[0] - 3 * y_pad, lane_count), jnp.float32)
    for tile in range(plan.lane_tiles):
        lanes = slice(tile * 128, tile * 128 + 128)
        near_weight = edge_y[0]
        far_weight = edge_y[1]

        def eliminate(step, carry):
            factor, value = carry
            x = step + 1
            factor = inverse(diagonal[:, lanes] - factor)
            value = (spectrum[x, :, lanes] + value) * factor
            factors[x] = factor
            solved[x] = value
            return factor, value

        def substitute(step, value):
            x = x_len - 1 - step
            value = solved[x] + factors[x] * value
            near_row = jnp.sum(value * near_weight, axis=0, keepdims=True)
            far_row = jnp.sum(value * far_weight, axis=0, keepdims=True)
            edge_rows[0, pl.ds(x, 1), :] = near_row + heads[tile, pl.ds(x, 1), :]
            edge_rows[1, pl.ds(x, 1), :] = far_row
            return value

        zero = jnp.zeros((y_pad, 128), jnp.float32)
        chunked_loop(x_len - 1, 5, eliminate, (zero, zero))
        stack[y_pad : 2 * y_pad, lanes] = solved[x_len - 1]
        stack[0:y_pad, lanes] = chunked_loop(x_len - 1, 5, substitute, zero)
        for side in range(2):
            row = 3 * y_pad + side * x_pad
            stack[row + 1 : row + x_len, lanes] = edge_rows[side, 1:x_len, :]
    turned[...] = right_apply(jnp.transpose(stack[...]), interface[...])
    total = plan.parts * plan.modes
    for mode in range(grid):
        message[mode] = turned[mode : mode + 1, :]
    if total > grid:
        message[grid:total] = jnp.zeros((total - grid, 1, 2 * plan.half), jnp.float32)
    spectrum_copy.wait()
    place_copies[1].wait()


def interface_kernel(
    plan,
    first_mode,
    stiff_z,
    _,
    incoming_hbm,
    gather_hbm,
    along_y_hbm,
    along_x_hbm,
    expand_hbm,
    expand_back_hbm,
    stiff_x_hbm,
    stiff_y_hbm,
    scatter_hbm,
    outgoing,
    rows,
    folded_y,
    folded_x,
    lines,
    incoming,
    gather,
    along_y_full,
    along_x_full,
    expand,
    expand_back,
    stiff_x,
    stiff_y,
    scatter,
    along_y,
    along_x,
    along_y_back,
    along_x_back,
    sems,
):
    loads = start_copies(
        [
            (incoming_hbm, incoming),
            (gather_hbm, gather),
            (along_y_hbm, along_y_full),
            (along_x_hbm, along_x_full),
            (expand_hbm, expand),
            (expand_back_hbm, expand_back),
            (stiff_x_hbm, stiff_x),
            (stiff_y_hbm, stiff_y),
            (scatter_hbm, scatter),
        ],
        sems,
    )
    grid, half, parts, modes = plan.grid, plan.half, plan.parts, plan.modes
    kx_pad, j_pad, n_gx, n_gy = plan.kx_pad, plan.j_pad, plan.n_gx, plan.n_gy
    lane_count = plan.lanes
    groups = grid // n_gx

    def collect(source, carry):
        for mode in range(modes):
            both = incoming[source * modes + mode]
            rows[mode, pl.ds(source, 1), :] = both[:, :half]
            rows[mode, pl.ds(parts + source, 1), :] = both[:, half:]
        return carry

    loads[0].wait()
    lax.fori_loop(0, parts, collect, 0)
    loads[1].wait()
    for mode in range(modes):
        lines[mode] = left_apply(gather[...], rows[mode])
    base = n_gy * kx_pad
    y_slots = [slice(j * kx_pad, (j + 1) * kx_pad) for j in range(n_gy)]
    x_slots = [slice(base + i * j_pad, base + (i + 1) * j_pad) for i in range(n_gx)]

    def side_by_side(slots, count):
        return jnp.concatenate(
            [lines[:, slot, :].reshape(modes * count, half) for slot in slots], axis=1
        )

    loads[2].wait()
    split_table(along_y_full, along_y, 0)
    loads[3].wait()
    split_table(along_x_full, along_x, 0)
    folded_y[...] = right_apply(side_by_side(y_slots, kx_pad), along_y[...]).reshape(
        modes, kx_pad, lane_count
    )
    folded_x[...] = right_apply(side_by_side(x_slots, j_pad), along_x[...]).reshape(
        modes, j_pad, lane_count
    )

    def solve(mode, carry):
        across = folded_x[mode, :, :grid]
        high = across.astype(jnp.bfloat16).astype(jnp.float32)
        across = jnp.concatenate([high, high, across - high], axis=0)
        spread = dot(across, expand[...], ((0,), (0,)))
        number = spread.reshape(groups, kx_pad, lane_count) + folded_y[mode][None]
        bottom = stiff_x[...] + (stiff_y[...] + stiff_z[first_mode[0] + mode])
        value = number * inverse(bottom).reshape(groups, kx_pad, lane_count)
        folded_y[mode] = jnp.sum(value, axis=0)
        value = value_triple(value.reshape(grid, lane_count), 1)
        folded_x[mode, :, :grid] = dot(expand_back[...], value, ((1,), (1,)))
        return carry

    for copy in loads[4:8]:
        copy.wait()
    chunked_loop(modes, 3, solve, 0)
    loads[8].wait()
    split_table(along_y_full, along_y_back, 1)
    split_table(along_x_full, along_x_back, 1)
    all_y = folded_y[...].reshape(modes * kx_pad, lane_count)
    all_y = dot(value_triple(all_y, 1), along_y_back[...], ((1,), (1,)))
    for j, slot in enumerate(y_slots):
        lines[:, slot, :] = all_y[:, j * half : (j + 1) * half].reshape(modes, kx_pad, half)
    all_x = folded_x[...].reshape(modes * j_pad, lane_count)
    all_x = dot(value_triple(all_x, 1), along_x_back[...], ((1,), (1,)))
    for i, slot in enumerate(x_slots):
        lines[:, slot, :] = all_x[:, i * half : (i + 1) * half].reshape(modes, j_pad, half)
    for mode in range(modes):
        rows[mode] = left_apply(scatter[...], lines[mode])

    def distribute(target, carry):
        for mode in range(modes):
            outgoing[target * modes + mode, :, :half] = rows[mode, pl.ds(target, 1), :]
            outgoing[target * modes + mode, :, half:] = rows[mode, pl.ds(parts + target, 1), :]
        return carry

    lax.fori_loop(0, parts, distribute, 0)


def backward_kernel(
    plan,
    n_blocks,
    block_atoms,
    places_hbm,
    message_hbm,
    interface_hbm,
    diagonal_hbm,
    edge_y_hbm,
    spectrum_hbm,
    y_table_hbm,
    z_full_hbm,
    _,
    potential_hbm,
    values,
    lookup,
    work,
    solved,
    factors,
    stack,
    heads,
    edge_rows,
    turned,
    picked,
    potential,
    places,
    message,
    interface_full,
    interface,
    diagonal,
    edge_y,
    spectrum,
    y_table,
    z_full,
    z_table,
    blocks,
    sems,
):
    x_len, y_len, y_pad, x_pad = plan.x_len, plan.y_len, plan.y_pad, plan.x_pad
    grid, lane_count, planes = plan.grid, plan.lanes, plan.planes
    slabs = slab_count(plan)
    tile_atoms = n_blocks * block_atoms
    loads = start_copies(
        [
            (message_hbm, message),
            (interface_hbm, interface_full),
            (places_hbm, places),
            (diagonal_hbm, diagonal),
            (edge_y_hbm, edge_y),
            (spectrum_hbm, spectrum),
            (y_table_hbm, y_table),
            (z_full_hbm, z_full),
        ],
        sems,
    )
    loads[0].wait()
    for mode in range(grid):
        turned[mode : mode + 1, :] = message[mode]
    if lane_count > grid:
        turned[grid:, :] = jnp.zeros((lane_count - grid, turned.shape[1]), jnp.float32)
    loads[1].wait()
    split_table(interface_full, interface, 1)
    stack[...] = dot(interface[...], value_triple(turned[...], 1), ((1,), (1,)))
    loads[2].wait()
    count = list_owned(plan, places, blocks, n_blocks, block_atoms)
    for copy in loads[3:]:
        copy.wait()
    split_table(z_full, z_table, 0)
    for tile in range(plan.lane_tiles):
        lanes = slice(tile * 128, tile * 128 + 128)
        near_weight = edge_y[0]
        far_weight = edge_y[1]
        heads[tile] = stack[3 * y_pad : 3 * y_pad + x_pad, lanes]
        edge_rows[...] = stack[3 * y_pad + x_pad : 3 * y_pad + 2 * x_pad, lanes]

        def eliminate(step, carry):
            factor, value = carry
            x = step + 1
            factor = inverse(diagonal[:, lanes] - factor)
            load = spectrum[x, :, lanes] + near_weight * heads[tile, pl.ds(x, 1), :]
            load = load + far_weight * edge_rows[pl.ds(x, 1), :]
            value = (load + value) * factor
            factors[x] = factor
            solved[x] = value
            return factor, value

        def substitute(step, value):
            x = x_len - 1 - step
            value = solved[x] + factors[x] * value
            work[x, :, lanes] = value
            return value

        zero = jnp.zeros((y_pad, 128), jnp.float32)
        chunked_loop(x_len - 1, 5, eliminate, (zero, stack[0:y_pad, lanes]))
        chunked_loop(x_len - 1, 5, substitute, stack[y_pad : 2 * y_pad, lanes])
    work[0] = jnp.zeros((y_pad, lane_count), jnp.float32)

    def transform(step, carry):
        start = step * slabs
        for slab in range(slabs):
            x = start + slab
            work[x] = left_apply(y_table[...], work[x])
            for tile in range(plan.lane_tiles):
                lanes = slice(tile * 128, tile * 128 + 128)
                work[x, 0:1, lanes] = heads[tile, pl.ds(x, 1), :]

        @pl.when(step == 0)
        def _():
            work[0] = stack[2 * y_pad : 3 * y_pad, :]

        lines = work[pl.ds(start, slabs)].reshape(slabs * y_pad, lane_count)
        lines = right_apply(lines, z_table[...])
        for tile in range(plan.lane_tiles):
            low = tile * 128
            place = pl.ds(pl.multiple_of(tile * planes + start * y_pad, 8), slabs * y_pad)
            lookup[place, :] = lines[:, low : low + 128]
        lines = lines.reshape(slabs, y_pad, lane_count)
        potential[pl.ds(start, slabs)] = lines[:, :y_len, :grid]
        return carry

    chunked_loop(x_len // slabs, 3, transform, 0)
    potential_copy = pltpu.make_async_copy(potential, potential_hbm, sems.at[8])
    potential_copy.start()
    values[...] = jnp.zeros(values.shape, jnp.float32)
    lane_ids = lax.broadcasted_iota(jnp.int32, (1, 128), 1)
    shape = (block_atoms, 128)
    own_lane = lax.broadcasted_iota(jnp.int32, shape, 0) == lax.broadcasted_iota(
        jnp.int32, shape, 1
    )

    def sample(slot, carry):
        block = blocks[slot]
        source = block // n_blocks
        start = (block - source * n_blocks) * block_atoms
        for first in range(0, block_atoms, 16):
            rows = []
            for atom in range(first, first + 16):
                row = lookup[pl.ds(places[source, start + atom], 1), :]
                lane = places[source, start + atom + tile_atoms] & 127
                rows.append(jnp.where(lane_ids == lane, row, 0.0))
            for k in range(16):
                picked[first + k : first + k + 1, :] = rows[k]
        found = jnp.sum(picked[...], axis=1, keepdims=True)
        found = jnp.sum(jnp.where(own_lane, found, 0.0), axis=0, keepdims=True)
        values[pl.ds(block, 1), :] = found
        return carry

    lax.fori_loop(0, count, sample, 0)
    potential_copy.wait()


def prepare_kernel(
    plan, n_blocks, block_atoms, counts, owners, type_radius, coords, charge, types, cells,
    copies, atom_rows,
):
    tile_atoms = n_blocks * block_atoms
    lane = lax.broadcasted_iota(jnp.int32, (1, 128), 1)
    slot = lane // block_atoms
    atom = lane - slot * block_atoms
    per_row = 128 // block_atoms
    for start in range(0, tile_atoms, 128):
        lanes = slice(start, start + 128)
        first = start // block_atoms
        count = jnp.full((1, 128), counts[0, first], jnp.int32)
        owner = jnp.full((1, 128), owners[0, first], jnp.int32)
        for k in range(1, per_row):
            count = jnp.where(slot >= k, counts[0, first + k], count)
            owner = jnp.where(slot >= k, owners[0, first + k], owner)
        live = jnp.where(atom < count, charge[0, :, lanes], 0.0)
        cell = cells[0, :, lanes]
        line = jnp.floor((cell.astype(jnp.float32) + 0.5) * (1.0 / plan.grid)).astype(jnp.int32)
        depth = cell - line * plan.grid
        x = jnp.floor((line.astype(jnp.float32) + 0.5) * (1.0 / plan.y_len)).astype(jnp.int32)
        plane = x * plan.y_pad + (line - x * plan.y_len)
        code = ((depth >> 7) * plan.planes + plane) * 128 + (depth & 127)
        code = (owner * plan.span + code).astype(jnp.float32)
        for target in range(plan.n_gx):
            copies[target, :, lanes] = code
            copies[target, :, tile_atoms + start : tile_atoms + start + 128] = live
        radius = jnp.zeros((1, 128), jnp.float32)
        for kind in range(type_radius.shape[0]):
            radius = jnp.where(types[0, :, lanes] == kind, type_radius[kind], radius)
        atom_rows[0, 0:3, lanes] = coords[0, :, 0, lanes]
        atom_rows[0, 3:4, lanes] = live
        atom_rows[0, 4:5, lanes] = radius


def pair_kernel(
    n_blocks, block_atoms, listed, part, n_parts, listing, low, middle, high, earlier, forces,
    table, columns, results,
):
    tile_atoms = n_blocks * block_atoms
    part_atoms = tile_atoms // n_parts
    first = part * part_atoms
    sides = (low, middle, high)
    for step_x in range(3):
        for step_y in range(3):
            rows = sides[step_y][step_x]
            shifts = (step_x - 1.0, step_y - 1.0, 0.0, 0.0, 0.0)
            for k in range(5):
                row = rows[k : k + 1, :]
                if shifts[k]:
                    row = row + shifts[k]
                table[step_x * 3 + step_y, k] = jnp.broadcast_to(row, (8, tile_atoms))
    columns[0:5, :] = middle[1, :, first : first + part_atoms]
    columns[5:, :] = jnp.zeros((columns.shape[0] - 5, part_atoms), jnp.float32)
    results[...] = jnp.transpose(columns[...])
    lane_ids = lax.broadcasted_iota(jnp.int32, (16, 128), 1)

    def group(number, carry):
        place = pl.ds(pl.multiple_of(number * 16, 16), 16)
        block = (first + number * 16) // block_atoms
        own = results[place, :]
        mine = [
            jnp.broadcast_to(own[:, k : k + 1], (16, 128)).reshape(2, 8, 128)
            for k in (0, 1, 2, 4)
        ]
        force_x = force_y = force_z = jnp.zeros((2, 8, 128), jnp.float32)
        for slot in range(listed):
            which = listing[0, slot, 0, block]
            for start in range(0, tile_atoms, 128):
                lanes = slice(start, start + 128)
                sep_x = mine[0] - table[which, 0, :, lanes][None]
                sep_y = mine[1] - table[which, 1, :, lanes][None]
                sep_z = mine[2] - table[which, 2, :, lanes][None]
                reach = mine[3] + table[which, 4, :, lanes][None]
                root = lax.rsqrt(sep_x * sep_x + sep_y * sep_y + sep_z * sep_z + reach * reach)
                strength = table[which, 3, :, lanes][None] * root * (root * root)
                force_x = force_x + strength * sep_x
                force_y = force_y + strength * sep_y
                force_z = force_z + strength * sep_z
        out = jnp.zeros((16, 128), jnp.float32)
        for axis, total in enumerate((force_x, force_y, force_z)):
            force = own[:, 3:4] * jnp.sum(total.reshape(16, 128), axis=1, keepdims=True)
            out = jnp.where(lane_ids == axis, force, out)
        results[place, :] = out
        return carry

    lax.fori_loop(0, part_atoms // 16, group, 0)
    columns[...] = jnp.transpose(results[...])
    if first:
        for axis in range(3):
            forces[axis, :, :first] = earlier[axis, :, :first]
    for axis in range(3):
        forces[axis, :, first : first + part_atoms] = columns[axis : axis + 1, :]


VMEM = pl.BlockSpec(memory_space=pltpu.VMEM)
SMEM = pl.BlockSpec(memory_space=pltpu.SMEM)
HBM = pl.BlockSpec(memory_space=pl.ANY)


def shaped(*shape):
    return jax.ShapeDtypeStruct(shape, jnp.float32)


def buffer(*shape):
    return pltpu.VMEM(shape, jnp.float32)


def like(table):
    return pltpu.VMEM(table.shape, table.dtype)


def limit(mib):
    return pltpu.CompilerParams(vmem_limit_bytes=mib * MIB)


def solve_poisson(plan, density, codes, first_code, n_blocks, block_atoms, neighbours, pair_part):
    x_len, y_len, grid = density.shape
    y_pad, x_pad, half, lanes = plan.y_pad, plan.x_pad, plan.half, plan.lanes
    total = plan.parts * plan.modes
    z_full = f32(plan.z_matrix())
    y_table = table_triple(plan.y_matrix(), 1)
    diagonal = f32(plan.diagonal())
    edge_y = f32(plan.edge_weights())
    interface = f32(plan.interface_table())
    bf16 = jnp.bfloat16
    n_rows, tile_atoms = codes.shape[0], n_blocks * block_atoms
    shared = [
        buffer(x_len, y_pad, 128),
        buffer(x_len, y_pad, 128),
        buffer(plan.stack_rows, lanes),
        buffer(plan.lane_tiles, x_pad, 128),
    ]
    spectrum, places, message = pl.pallas_call(
        functools.partial(forward_kernel, plan, n_blocks, block_atoms),
        out_shape=(
            shaped(x_len, y_pad, lanes),
            jax.ShapeDtypeStruct((n_rows, 2 * tile_atoms), jnp.int32),
            shaped(total, 1, 2 * half),
        ),
        in_specs=[SMEM] + [HBM] * 9,
        out_specs=(HBM, HBM, VMEM),
        scratch_shapes=[buffer(plan.lane_tiles * plan.planes, 128)]
        + shared
        + [
            buffer(2, x_pad, 128),
            buffer(lanes, 2 * half),
            buffer(n_rows, 1, 2 * tile_atoms),
            buffer(n_rows, tile_atoms),
            buffer(x_len, y_len, grid),
            like(z_full),
            pltpu.VMEM((3 * lanes, lanes), bf16),
            like(y_table),
            like(diagonal),
            like(edge_y),
            like(interface),
            pltpu.VMEM((3 * plan.stack_rows, 2 * half), bf16),
            buffer(x_len, y_pad, lanes),
            pltpu.VMEM((n_rows, 2 * tile_atoms), jnp.int32),
            buffer(n_rows, tile_atoms),
            pltpu.SMEM((n_rows, 2 * tile_atoms), jnp.int32),
            pltpu.SMEM((n_rows, tile_atoms), jnp.float32),
            pltpu.SMEM((n_rows * n_blocks,), jnp.int32),
            pltpu.SemaphoreType.DMA((11,)),
        ],
        compiler_params=limit(VMEM_MIB),
        name="forward_solve",
    )(first_code, codes, density, z_full, y_table, diagonal, edge_y, interface, *neighbours)
    first_pairs = pair_part(0, None)
    incoming = lax.all_to_all(message, ("gx", "gy"), split_axis=0, concat_axis=0, tiled=True)
    gather = plan.gather_table()
    along_y, along_x = plan.line_tables()
    expand = plan.expand_table()
    position = lax.axis_index("gx") * plan.n_gy + lax.axis_index("gy")
    first_mode = (position * plan.modes).astype(jnp.int32).reshape(1)
    stiff = stiffness(grid, grid)
    padded_z = np.zeros(total)
    padded_z[:grid] = stiff
    padded_y = np.zeros((1, lanes))
    padded_y[0, :grid] = stiff
    tables = [
        table_triple(gather, 1),
        f32(along_y),
        f32(along_x),
        f32(table_triple(expand, 0)),
        table_triple(expand, 1),
        f32(stiff[:, None] * grid),
        f32(padded_y * grid),
        table_triple(gather.T, 1),
    ]
    outgoing = pl.pallas_call(
        functools.partial(interface_kernel, plan),
        out_shape=shaped(total, 1, 2 * half),
        in_specs=[SMEM] * 2 + [HBM] * 10,
        out_specs=VMEM,
        scratch_shapes=[
            buffer(plan.modes, 2 * plan.parts, half),
            buffer(plan.modes, plan.kx_pad, lanes),
            buffer(plan.modes, plan.j_pad, lanes),
            buffer(plan.modes, gather.shape[0], half),
            buffer(total, 1, 2 * half),
            *[like(table) for table in tables],
            pltpu.VMEM((3 * along_y.shape[0], lanes), bf16),
            pltpu.VMEM((3 * along_x.shape[0], lanes), bf16),
            pltpu.VMEM((along_y.shape[0], 3 * lanes), bf16),
            pltpu.VMEM((along_x.shape[0], 3 * lanes), bf16),
            pltpu.SemaphoreType.DMA((9,)),
        ],
        compiler_params=limit(VMEM_MIB),
        name="interface_solve",
    )(first_mode, f32((padded_z + SCREENING) * grid), first_pairs, incoming, *tables)
    returned = lax.all_to_all(outgoing, ("gx", "gy"), split_axis=0, concat_axis=0, tiled=True)
    pair_force = pair_part(1, first_pairs)
    potential, values = pl.pallas_call(
        functools.partial(backward_kernel, plan, n_blocks, block_atoms),
        out_shape=(shaped(x_len, y_len, grid), shaped(plan.n_gx * n_blocks, 128)),
        in_specs=[HBM] * 9,
        out_specs=(HBM, VMEM),
        scratch_shapes=[
            buffer(plan.lane_tiles * plan.planes, 128),
            buffer(x_len, y_pad, lanes),
        ]
        + shared
        + [
            buffer(x_pad, 128),
            buffer(lanes, 2 * half),
            buffer(block_atoms, 128),
            buffer(x_len, y_len, grid),
            pltpu.SMEM((n_rows, 2 * tile_atoms), jnp.int32),
            buffer(total, 1, 2 * half),
            like(interface),
            pltpu.VMEM((plan.stack_rows, 6 * half), bf16),
            like(diagonal),
            like(edge_y),
            buffer(x_len, y_pad, lanes),
            like(y_table),
            like(z_full),
            pltpu.VMEM((3 * lanes, lanes), bf16),
            pltpu.SMEM((n_rows * n_blocks,), jnp.int32),
            pltpu.SemaphoreType.DMA((9,)),
        ],
        compiler_params=limit(VMEM_MIB),
        name="backward_solve",
    )(places, returned, interface, diagonal, edge_y, spectrum, y_table, z_full, pair_force)
    return potential, values, pair_force


def shifted(block, axis, step):
    count = lax.axis_size(axis)
    return lax.ppermute(block, axis, [(i, (i + step) % count) for i in range(count)])


def body(
    qm_density,
    mm_coords,
    mm_charge,
    mm_types,
    type_radius,
    mm_cells,
    block_counts,
    block_owner,
    neighbour_tiles,
):
    n_blocks = block_counts.shape[2]
    tile_atoms = mm_charge.shape[2]
    block_atoms = tile_atoms // n_blocks
    x_local, local_y_rows, grid_len = qm_density.shape
    n_gx = lax.axis_size("gx")
    plan = Plan(x_local, local_y_rows, grid_len, n_gx, lax.axis_size("gy"))
    copies, atom_rows = pl.pallas_call(
        functools.partial(prepare_kernel, plan, n_blocks, block_atoms),
        out_shape=(shaped(n_gx, 1, 2 * tile_atoms), shaped(1, 5, tile_atoms)),
        in_specs=[SMEM] * 3 + [VMEM] * 4,
        out_specs=(VMEM, VMEM),
        compiler_params=limit(VMEM_MIB),
        name="prepare_atoms",
    )(
        block_counts.reshape(1, n_blocks),
        block_owner.reshape(1, n_blocks),
        type_radius,
        mm_coords.transpose(0, 2, 1, 3),
        mm_charge,
        mm_types,
        mm_cells,
    )
    codes = lax.all_to_all(copies, "gx", split_axis=0, concat_axis=0, tiled=True)
    first_code = (lax.axis_index("gx") * plan.span).astype(jnp.int32).reshape(1)
    triple = jnp.concatenate(
        [shifted(atom_rows, "gx", 1), atom_rows, shifted(atom_rows, "gx", -1)], axis=0
    )
    below, above = shifted(triple, "gy", 1), shifted(triple, "gy", -1)
    listed = neighbour_tiles.shape[3]
    listing = neighbour_tiles.transpose(0, 3, 1, 2)

    def pair_part(part, earlier):
        if earlier is None:
            earlier = jnp.zeros((3, 1, 128), jnp.float32)
        return pl.pallas_call(
            functools.partial(pair_kernel, n_blocks, block_atoms, listed, part, 2),
            out_shape=shaped(3, 1, (part + 1) * tile_atoms // 2),
            in_specs=[SMEM] + [VMEM] * 4,
            out_specs=VMEM,
            scratch_shapes=[
                buffer(9, 5, 8, tile_atoms),
                buffer(128, tile_atoms // 2),
                buffer(tile_atoms // 2, 128),
            ],
            compiler_params=limit(VMEM_MIB),
            cost_estimate=pl.CostEstimate(
                flops=10 * listed * tile_atoms * tile_atoms,
                bytes_accessed=4 * 50 * tile_atoms,
                transcendentals=listed * tile_atoms * tile_atoms // 2,
            ),
            name="pair_forces",
        )(listing, below, triple, above, earlier)

    potential, values, pair_force = solve_poisson(
        plan, qm_density, codes, first_code, n_blocks, block_atoms, (below, above), pair_part
    )
    values = lax.all_to_all(values, "gx", split_axis=0, concat_axis=0, tiled=True)
    sampled = jnp.sum(values.reshape(n_gx, n_blocks, 128), axis=0)[:, :block_atoms]
    lanes = jnp.arange(block_atoms, dtype=jnp.int32)
    live = lanes[None, :] < block_counts.reshape(n_blocks, 1)
    mm_potential = jnp.where(live, sampled, 0.0).reshape(1, 1, tile_atoms)
    return (potential, mm_potential, pair_force[None].transpose(0, 2, 1, 3))


def solution(mesh):
    placed = (
        P("gx", "gy", None),
        P("gx", "gy", None, None),
        P("gx", "gy", None),
        P("gx", "gy", None),
        P(),
        P("gx", "gy", None),
        P("gx", "gy", None),
        P("gx", "gy", None, None),
        P("gx", "gy", None, None),
    )
    return jax.shard_map(
        body,
        mesh=mesh,
        in_specs=placed,
        out_specs=(P("gx", "gy", None), P("gx", "gy", None), P("gx", "gy", None, None)),
        check_vma=False,
    )
```

```python
import functools

import jax
import jax.numpy as jnp
import ml_dtypes
import numpy as np
from jax import lax
from jax.experimental import pallas as pl
from jax.experimental.pallas import tpu as pltpu
from jax.sharding import PartitionSpec as P

SCREENING = 0.003
HIGH_ACCURACY = lax.Precision.HIGHEST
VMEM_MIB = 60
BATCH = 8
MIB = 1024 * 1024


def round_up(value, unit):
    return -(-value // unit) * unit


def sine_matrix(length):
    nodes = np.arange(length, dtype=np.float64)
    return np.sqrt(2.0 / length) * np.sin(np.pi * np.outer(nodes, nodes) / length)


def cas_matrix(length):
    nodes = np.arange(length)
    angle = 2.0 * np.pi * (np.outer(nodes, nodes) % length) / length
    return np.cos(angle) + np.sin(angle)


def stiffness(count, length):
    return 4.0 * np.sin(np.pi * np.arange(count) / length) ** 2


def split_pair(matrix):
    full = np.asarray(matrix, np.float32)
    high = full.astype(ml_dtypes.bfloat16)
    low = (full - high.astype(np.float32)).astype(ml_dtypes.bfloat16)
    return high, low


def table_triple(matrix, axis):
    high, low = split_pair(matrix)
    return np.concatenate([high, low, high], axis=axis)


def f32(table):
    return np.asarray(table, np.float32)


class Plan:
    def __init__(self, x_len, y_len, grid, n_gx, n_gy):
        self.x_len, self.y_len, self.grid = x_len, y_len, grid
        self.n_gx, self.n_gy = n_gx, n_gy
        self.y_pad = round_up(y_len, 8)
        self.x_pad = round_up(x_len, 8)
        self.lanes = round_up(grid, 128)
        self.lane_tiles = self.lanes // 128
        self.planes = x_len * self.y_pad
        self.span = self.lane_tiles * self.planes * 128
        self.parts = n_gx * n_gy
        self.modes = -(-grid // self.parts)
        self.half = round_up(y_len + x_len, 128)
        self.kx_pad = round_up(n_gx, 8)
        self.j_pad = round_up(n_gy, 8)
        self.stack_rows = round_up(3 * self.y_pad + 2 * self.x_pad, 128)

    def y_matrix(self):
        out = np.zeros((self.y_pad, self.y_pad))
        out[: self.y_len, : self.y_len] = sine_matrix(self.y_len)
        return out

    def z_matrix(self):
        out = np.zeros((self.lanes, self.lanes))
        out[: self.grid, : self.grid] = cas_matrix(self.grid) / np.sqrt(self.grid)
        return out

    def diagonal(self):
        z_part = np.zeros(self.lanes)
        z_part[: self.grid] = stiffness(self.grid, self.grid)
        y_part = stiffness(self.y_pad, 2 * self.y_len)
        return 2.0 + y_part[:, None] + z_part[None, :] + SCREENING

    def edge_weights(self):
        sine_y = self.y_matrix()
        both = np.stack([sine_y[1], sine_y[self.y_len - 1]])
        return np.broadcast_to(both[:, :, None], (2, self.y_pad, 128))

    def interface_table(self):
        x_len, y_len, half = self.x_len, self.y_len, self.half
        y_pad, x_pad = self.y_pad, self.x_pad
        sine_y = sine_matrix(y_len)
        out = np.zeros((self.stack_rows, 2 * half))
        out[:y_len, :y_len] = sine_y
        row = y_pad
        out[row : row + y_len, half : half + y_len] = sine_y
        row += y_pad
        out[row : row + y_len, :y_len] = np.eye(y_len)
        row += y_pad
        out[row + 1 : row + x_len, y_len + 1 : y_len + x_len] = np.eye(x_len - 1)
        row += x_pad
        far = half + y_len
        out[row + 1 : row + x_len, far + 1 : far + x_len] = np.eye(x_len - 1)
        return out

    def gather_table(self):
        n_gx, n_gy, parts = self.n_gx, self.n_gy, self.parts
        cas_x = cas_matrix(n_gx)
        out = np.zeros((n_gy * self.kx_pad + n_gx * self.j_pad, 2 * parts))
        for i in range(n_gx):
            for j in range(n_gy):
                col = i * n_gy + j
                base = j * self.kx_pad
                out[base : base + n_gx, col] = cas_x[:, i]
                out[base : base + n_gx, parts + col] = cas_x[:, (i + 1) % n_gx]
                base = n_gy * self.kx_pad + i * self.j_pad
                out[base + j, col] = 1.0
                out[base + (j + 1) % n_gy, parts + col] = 1.0
        return out

    def line_tables(self):
        scaled = cas_matrix(self.grid) / np.sqrt(self.grid)
        along_y = np.zeros((self.n_gy, self.half, self.lanes))
        along_x = np.zeros((self.n_gx, self.half, self.lanes))
        y_len, x_len, grid = self.y_len, self.x_len, self.grid
        for j in range(self.n_gy):
            along_y[j, :y_len, :grid] = scaled[j * y_len : (j + 1) * y_len]
        for i in range(self.n_gx):
            along_x[i, y_len : y_len + x_len, :grid] = scaled[i * x_len : (i + 1) * x_len]
        return along_y.reshape(-1, self.lanes), along_x.reshape(-1, self.lanes)

    def expand_table(self):
        ratio = self.grid // self.n_gy
        full = cas_matrix(self.grid)
        out = np.zeros((self.j_pad, self.lanes))
        for j in range(self.n_gy):
            out[j, : self.grid] = full[(j * ratio) % self.grid]
        return out


def dot(a, b, dims=((1,), (0,)), precision=None):
    return lax.dot_general(
        a, b, (dims, ((), ())), precision=precision, preferred_element_type=jnp.float32
    )


def value_triple(value, axis):
    high = value.astype(jnp.bfloat16).astype(jnp.float32)
    return jnp.concatenate([high, high, value - high], axis=axis).astype(jnp.bfloat16)


def split_table(source, target, axis):
    value = source[...]
    high = value.astype(jnp.bfloat16).astype(jnp.float32)
    parts = jnp.concatenate([high, value - high, high], axis=axis)
    target[...] = parts.astype(jnp.bfloat16)


def left_apply(table, value):
    return dot(table, value_triple(value, 0))


def right_apply(value, table):
    return dot(value_triple(value, 1), table)


def slab_count(plan):
    if plan.y_pad != plan.y_len:
        return 1
    return max(count for count in (4, 3, 2, 1) if plan.x_len % count == 0)


def inverse(value):
    guess = pl.reciprocal(value, approx=True)
    guess = guess * (2.0 - value * guess)
    return guess * (2.0 - value * guess)


def start_copies(pairs, sems):
    copies = [
        pltpu.make_async_copy(source, target, sems.at[k])
        for k, (source, target) in enumerate(pairs)
    ]
    for copy in copies:
        copy.start()
    return copies


def list_owned(plan, places, blocks, block_count):
    def several(step, count):
        for k in range(8):
            number = step * 8 + k
            lead = places[number, 0]
            blocks[count] = number
            count = count + jnp.where((lead >= 0) & (lead < plan.span), 1, 0)
        return count

    return lax.fori_loop(0, block_count // 8, several, 0)


def chunked_loop(count, unroll, body, init):
    while count % unroll:
        unroll -= 1

    def group(step, carry):
        for k in range(unroll):
            carry = body(step * unroll + k, carry)
        return carry

    return lax.fori_loop(0, count // unroll, group, init)


def mark_places(codes, first_code, place_rows, block_atoms):
    lane = lax.broadcasted_iota(jnp.int32, codes.shape, 1)
    code = codes[...].astype(jnp.int32) - first_code
    place = lax.shift_right_arithmetic(code, 7)
    shared = jnp.zeros_like(place)
    for step in range(1, BATCH):
        same = (pltpu.roll(place, step, 1) == place) & (lane % BATCH >= step)
        shared = jnp.where(same & (lane < block_atoms), 1, shared)
    step = block_atoms // 2
    while step:
        shared = shared | pltpu.roll(shared, 128 - step, 1)
        step //= 2
    mark = pltpu.roll(shared, block_atoms, 1)
    place_rows[...] = jnp.where(lane == block_atoms, mark, code)


def forward_kernel(
    plan,
    n_blocks,
    block_atoms,
    first_code,
    *refs,
):
    (
        codes_hbm,
        density_hbm,
        z_full_hbm,
        y_table_hbm,
        diagonal_hbm,
        edge_y_hbm,
        interface_hbm,
        _,
        _,
        spectrum_hbm,
        places_hbm,
        message,
        added,
        solved,
        factors,
        stack,
        heads,
        edge_rows,
        turned,
        codes,
        density,
        z_full,
        z_table,
        y_table,
        diagonal,
        edge_y,
        interface_full,
        interface,
        spectrum,
        place_rows,
        places,
        blocks,
        sems,
    ) = refs
    x_len, y_len, y_pad, x_pad = plan.x_len, plan.y_len, plan.y_pad, plan.x_pad
    grid, lane_count, planes = plan.grid, plan.lanes, plan.planes
    slabs = slab_count(plan)
    lane_ids = lax.broadcasted_iota(jnp.int32, (1, 128), 1)
    loads = start_copies(
        [
            (codes_hbm, codes),
            (density_hbm, density),
            (z_full_hbm, z_full),
            (y_table_hbm, y_table),
            (diagonal_hbm, diagonal),
            (edge_y_hbm, edge_y),
            (interface_hbm, interface_full),
        ],
        sems,
    )
    loads[0].wait()
    mark_places(codes, first_code[0], place_rows, block_atoms)
    place_copies = [
        pltpu.make_async_copy(place_rows, places, sems.at[8]),
        pltpu.make_async_copy(place_rows, places_hbm, sems.at[9]),
    ]
    for copy in place_copies:
        copy.start()

    def clear(step, carry):
        place = pl.ds(pl.multiple_of(step * y_pad, 8), y_pad)
        added[place, :] = jnp.zeros((y_pad, 128), jnp.float32)
        return carry

    chunked_loop(plan.lane_tiles * x_len, 4, clear, 0)
    loads[2].wait()
    split_table(z_full, z_table, 0)
    place_copies[0].wait()
    count = list_owned(plan, places, blocks, plan.n_gx * n_blocks)

    def deposit(slot, carry):
        block = blocks[slot]
        row_codes = places.at[block]
        charge_row = codes[pl.ds(block, 1), :]

        def raised(code, k):
            charge = charge_row[:, block_atoms + k : block_atoms + k + 1]
            hit = jnp.where(lane_ids == (code & 127), charge, 0.0)
            return added[pl.ds(lax.shift_right_logical(code, 7), 1), :] + hit

        @pl.when(row_codes[block_atoms] == 0)
        def _():
            for start in range(0, block_atoms, BATCH):
                local = [row_codes[start + k] for k in range(BATCH)]
                rows = [raised(code, start + k) for k, code in enumerate(local)]
                for code, row in zip(local, rows):
                    added[pl.ds(lax.shift_right_logical(code, 7), 1), :] = row

        @pl.when(row_codes[block_atoms] != 0)
        def _():
            for k in range(block_atoms):
                code = row_codes[k]
                row = raised(code, k)
                added[pl.ds(lax.shift_right_logical(code, 7), 1), :] = row

        return carry

    lax.fori_loop(0, count, deposit, 0)
    loads[1].wait()
    loads[3].wait()

    def transform(step, carry):
        start = step * slabs
        count = slabs * y_pad
        pieces = []
        for tile in range(plan.lane_tiles):
            low = tile * 128
            width = min(128, grid - low)
            piece = density.at[pl.ds(start, slabs)][:, :, low : low + width]
            if y_pad == y_len:
                piece = piece.reshape(count, width)
            else:
                rows = jnp.zeros((y_pad - y_len, width), jnp.float32)
                piece = jnp.concatenate([piece[0], rows], axis=0)
            if width < 128:
                rest = jnp.zeros((count, 128 - width), jnp.float32)
                piece = jnp.concatenate([piece, rest], axis=1)
            place = pl.ds(pl.multiple_of(tile * planes + start * y_pad, 8), count)
            pieces.append(piece + added.at[place][...])
        lines = right_apply(jnp.concatenate(pieces, axis=1), z_table[...])
        lines = lines.reshape(slabs, y_pad, lane_count)
        for slab in range(slabs):
            x = start + slab
            for tile in range(plan.lane_tiles):
                heads[tile, pl.ds(x, 1), :] = lines[slab, 0:1, tile * 128 : tile * 128 + 128]
            spectrum.at[x][...] = left_apply(y_table[...], lines[slab])

        @pl.when(step == 0)
        def _():
            stack[2 * y_pad : 3 * y_pad, :] = lines[0]

        return carry

    chunked_loop(x_len // slabs, 3, transform, 0)
    spectrum_copy = pltpu.make_async_copy(spectrum, spectrum_hbm, sems.at[10])
    spectrum_copy.start()
    for copy in loads[4:]:
        copy.wait()
    split_table(interface_full, interface, 0)
    stack[3 * y_pad :, :] = jnp.zeros((stack.shape[0] - 3 * y_pad, lane_count), jnp.float32)
    for tile in range(plan.lane_tiles):
        lanes = slice(tile * 128, tile * 128 + 128)
        near_weight = edge_y[0]
        far_weight = edge_y[1]

        def eliminate(step, carry):
            factor, value = carry
            x = step + 1
            factor = inverse(diagonal[:, lanes] - factor)
            value = (spectrum.at[x][:, lanes] + value) * factor
            factors.at[x][...] = factor
            solved.at[x][...] = value
            return factor, value

        def substitute(step, value):
            x = x_len - 1 - step
            value = solved.at[x][...] + factors.at[x][...] * value
            near_row = jnp.sum(value * near_weight, axis=0, keepdims=True)
            far_row = jnp.sum(value * far_weight, axis=0, keepdims=True)
            edge_rows[0, pl.ds(x, 1), :] = near_row + heads[tile, pl.ds(x, 1), :]
            edge_rows[1, pl.ds(x, 1), :] = far_row
            return value

        zero = jnp.zeros((y_pad, 128), jnp.float32)
        chunked_loop(x_len - 1, 5, eliminate, (zero, zero))
        stack[y_pad : 2 * y_pad, lanes] = solved[x_len - 1]
        stack[0:y_pad, lanes] = chunked_loop(x_len - 1, 5, substitute, zero)
        for side in range(2):
            row = 3 * y_pad + side * x_pad
            stack[row + 1 : row + x_len, lanes] = edge_rows[side, 1:x_len, :]
    turned[...] = right_apply(jnp.transpose(stack[...]), interface[...])
    total = plan.parts * plan.modes
    for mode in range(grid):
        message[mode] = turned[mode : mode + 1, :]
    if total > grid:
        message[grid:total] = jnp.zeros((total - grid, 1, 2 * plan.half), jnp.float32)
    spectrum_copy.wait()
    place_copies[1].wait()


def interface_kernel(
    plan,
    first_mode,
    stiff_z,
    _,
    incoming_hbm,
    gather_hbm,
    along_y_hbm,
    along_x_hbm,
    expand_hbm,
    expand_back_hbm,
    stiff_x_hbm,
    stiff_y_hbm,
    scatter_hbm,
    outgoing,
    rows,
    folded_y,
    folded_x,
    lines,
    incoming,
    gather,
    along_y_full,
    along_x_full,
    expand,
    expand_back,
    stiff_x,
    stiff_y,
    scatter,
    along_y,
    along_x,
    along_y_back,
    along_x_back,
    sems,
):
    loads = start_copies(
        [
            (incoming_hbm, incoming),
            (gather_hbm, gather),
            (along_y_hbm, along_y_full),
            (along_x_hbm, along_x_full),
            (expand_hbm, expand),
            (expand_back_hbm, expand_back),
            (stiff_x_hbm, stiff_x),
            (stiff_y_hbm, stiff_y),
            (scatter_hbm, scatter),
        ],
        sems,
    )
    grid, half, parts, modes = plan.grid, plan.half, plan.parts, plan.modes
    kx_pad, j_pad, n_gx, n_gy = plan.kx_pad, plan.j_pad, plan.n_gx, plan.n_gy
    lane_count = plan.lanes
    groups = grid // n_gx

    def collect(source, carry):
        for mode in range(modes):
            both = incoming.at[source * modes + mode][...]
            rows[mode, pl.ds(source, 1), :] = both[:, :half]
            rows[mode, pl.ds(parts + source, 1), :] = both[:, half:]
        return carry

    loads[0].wait()
    lax.fori_loop(0, parts, collect, 0)
    loads[1].wait()
    for mode in range(modes):
        lines[mode] = left_apply(gather[...], rows[mode])
    base = n_gy * kx_pad
    y_slots = [slice(j * kx_pad, (j + 1) * kx_pad) for j in range(n_gy)]
    x_slots = [slice(base + i * j_pad, base + (i + 1) * j_pad) for i in range(n_gx)]

    def side_by_side(slots, count):
        return jnp.concatenate(
            [lines[:, slot, :].reshape(modes * count, half) for slot in slots], axis=1
        )

    loads[2].wait()
    split_table(along_y_full, along_y, 0)
    loads[3].wait()
    split_table(along_x_full, along_x, 0)
    folded_y[...] = right_apply(side_by_side(y_slots, kx_pad), along_y[...]).reshape(
        modes, kx_pad, lane_count
    )
    folded_x[...] = right_apply(side_by_side(x_slots, j_pad), along_x[...]).reshape(
        modes, j_pad, lane_count
    )

    def solve(mode, carry):
        across = folded_x[mode, :, :grid]
        high = across.astype(jnp.bfloat16).astype(jnp.float32)
        across = jnp.concatenate([high, high, across - high], axis=0)
        spread = dot(across, expand[...], ((0,), (0,)))
        number = spread.reshape(groups, kx_pad, lane_count) + folded_y[mode][None]
        bottom = stiff_x[...] + (stiff_y[...] + stiff_z[first_mode[0] + mode])
        value = number * inverse(bottom).reshape(groups, kx_pad, lane_count)
        folded_y[mode] = jnp.sum(value, axis=0)
        value = value_triple(value.reshape(grid, lane_count), 1)
        folded_x[mode, :, :grid] = dot(expand_back[...], value, ((1,), (1,)))
        return carry

    for copy in loads[4:8]:
        copy.wait()
    chunked_loop(modes, 3, solve, 0)
    loads[8].wait()
    split_table(along_y_full, along_y_back, 1)
    split_table(along_x_full, along_x_back, 1)
    all_y = folded_y[...].reshape(modes * kx_pad, lane_count)
    all_y = dot(value_triple(all_y, 1), along_y_back[...], ((1,), (1,)))
    for j, slot in enumerate(y_slots):
        lines[:, slot, :] = all_y[:, j * half : (j + 1) * half].reshape(modes, kx_pad, half)
    all_x = folded_x[...].reshape(modes * j_pad, lane_count)
    all_x = dot(value_triple(all_x, 1), along_x_back[...], ((1,), (1,)))
    for i, slot in enumerate(x_slots):
        lines[:, slot, :] = all_x[:, i * half : (i + 1) * half].reshape(modes, j_pad, half)
    for mode in range(modes):
        rows[mode] = left_apply(scatter[...], lines[mode])

    def distribute(target, carry):
        for mode in range(modes):
            outgoing[target * modes + mode, :, :half] = rows[mode, pl.ds(target, 1), :]
            outgoing[target * modes + mode, :, half:] = rows[mode, pl.ds(parts + target, 1), :]
        return carry

    lax.fori_loop(0, parts, distribute, 0)


def backward_kernel(
    plan,
    n_blocks,
    block_atoms,
    places_hbm,
    message_hbm,
    interface_hbm,
    diagonal_hbm,
    edge_y_hbm,
    spectrum_hbm,
    y_table_hbm,
    z_full_hbm,
    _,
    potential_hbm,
    values,
    lookup,
    work,
    solved,
    factors,
    stack,
    heads,
    edge_rows,
    turned,
    picked,
    potential,
    places,
    message,
    interface_full,
    interface,
    diagonal,
    edge_y,
    spectrum,
    y_table,
    z_full,
    z_table,
    blocks,
    sems,
):
    x_len, y_len, y_pad, x_pad = plan.x_len, plan.y_len, plan.y_pad, plan.x_pad
    grid, lane_count, planes = plan.grid, plan.lanes, plan.planes
    slabs = slab_count(plan)
    loads = start_copies(
        [
            (message_hbm, message),
            (interface_hbm, interface_full),
            (places_hbm, places),
            (diagonal_hbm, diagonal),
            (edge_y_hbm, edge_y),
            (spectrum_hbm, spectrum),
            (y_table_hbm, y_table),
            (z_full_hbm, z_full),
        ],
        sems,
    )
    loads[0].wait()
    for mode in range(grid):
        turned[mode : mode + 1, :] = message[mode]
    if lane_count > grid:
        turned[grid:, :] = jnp.zeros((lane_count - grid, turned.shape[1]), jnp.float32)
    loads[1].wait()
    split_table(interface_full, interface, 1)
    stack[...] = dot(interface[...], value_triple(turned[...], 1), ((1,), (1,)))
    loads[2].wait()
    count = list_owned(plan, places, blocks, plan.n_gx * n_blocks)
    for copy in loads[3:]:
        copy.wait()
    split_table(z_full, z_table, 0)
    for tile in range(plan.lane_tiles):
        lanes = slice(tile * 128, tile * 128 + 128)
        near_weight = edge_y[0]
        far_weight = edge_y[1]
        heads[tile] = stack[3 * y_pad : 3 * y_pad + x_pad, lanes]
        edge_rows[...] = stack[3 * y_pad + x_pad : 3 * y_pad + 2 * x_pad, lanes]

        def eliminate(step, carry):
            factor, value = carry
            x = step + 1
            factor = inverse(diagonal[:, lanes] - factor)
            load = spectrum.at[x][:, lanes] + near_weight * heads[tile, pl.ds(x, 1), :]
            load = load + far_weight * edge_rows[pl.ds(x, 1), :]
            value = (load + value) * factor
            factors.at[x][...] = factor
            solved.at[x][...] = value
            return factor, value

        def substitute(step, value):
            x = x_len - 1 - step
            value = solved.at[x][...] + factors.at[x][...] * value
            work.at[x][:, lanes] = value
            return value

        zero = jnp.zeros((y_pad, 128), jnp.float32)
        chunked_loop(x_len - 1, 5, eliminate, (zero, stack[0:y_pad, lanes]))
        chunked_loop(x_len - 1, 5, substitute, stack[y_pad : 2 * y_pad, lanes])
    work[0] = jnp.zeros((y_pad, lane_count), jnp.float32)

    def transform(step, carry):
        start = step * slabs
        for slab in range(slabs):
            x = start + slab
            slab_work = work.at[x]
            slab_work[...] = left_apply(y_table[...], slab_work[...])
            for tile in range(plan.lane_tiles):
                lanes = slice(tile * 128, tile * 128 + 128)
                slab_work[0:1, lanes] = heads[tile, pl.ds(x, 1), :]

        @pl.when(step == 0)
        def _():
            work[0] = stack[2 * y_pad : 3 * y_pad, :]

        lines = work.at[pl.ds(start, slabs)][...].reshape(slabs * y_pad, lane_count)
        lines = right_apply(lines, z_table[...])
        for tile in range(plan.lane_tiles):
            low = tile * 128
            place = pl.ds(pl.multiple_of(tile * planes + start * y_pad, 8), slabs * y_pad)
            lookup.at[place][...] = lines[:, low : low + 128]
        lines = lines.reshape(slabs, y_pad, lane_count)
        potential.at[pl.ds(start, slabs)][...] = lines[:, :y_len, :grid]
        return carry

    chunked_loop(x_len // slabs, 3, transform, 0)
    potential_copy = pltpu.make_async_copy(potential, potential_hbm, sems.at[8])
    potential_copy.start()
    values[...] = jnp.zeros(values.shape, jnp.float32)
    lane_ids = lax.broadcasted_iota(jnp.int32, (1, 128), 1)
    shape = (block_atoms, 128)
    own_lane = lax.broadcasted_iota(jnp.int32, shape, 0) == lax.broadcasted_iota(
        jnp.int32, shape, 1
    )

    def sample(slot, carry):
        block = blocks[slot]
        row_codes = places.at[block]
        for first in range(0, block_atoms, 16):
            rows = []
            for atom in range(first, first + 16):
                code = row_codes[atom]
                row = lookup[pl.ds(lax.shift_right_logical(code, 7), 1), :]
                rows.append(jnp.where(lane_ids == (code & 127), row, 0.0))
            for k in range(16):
                picked[first + k : first + k + 1, :] = rows[k]
        found = jnp.sum(picked[...], axis=1, keepdims=True)
        found = jnp.sum(jnp.where(own_lane, found, 0.0), axis=0, keepdims=True)
        values[pl.ds(block, 1), :] = found
        return carry

    lax.fori_loop(0, count, sample, 0)
    potential_copy.wait()


def prepare_kernel(
    plan, n_blocks, block_atoms, counts, owners, type_radius, coords, charge, types, cells,
    copies, atom_rows, payload,
):
    tile_atoms = n_blocks * block_atoms
    lane = lax.broadcasted_iota(jnp.int32, (1, 128), 1)
    slot = lane // block_atoms
    atom = lane - slot * block_atoms
    per_row = 128 // block_atoms
    for start in range(0, tile_atoms, 128):
        lanes = slice(start, start + 128)
        first = start // block_atoms
        count = jnp.full((1, 128), counts[0, first], jnp.int32)
        owner = jnp.full((1, 128), owners[0, first], jnp.int32)
        for k in range(1, per_row):
            count = jnp.where(slot >= k, counts[0, first + k], count)
            owner = jnp.where(slot >= k, owners[0, first + k], owner)
        live = jnp.where(atom < count, charge[0, :, lanes], 0.0)
        cell = cells[0, :, lanes]
        line = jnp.floor((cell.astype(jnp.float32) + 0.5) * (1.0 / plan.grid)).astype(jnp.int32)
        depth = cell - line * plan.grid
        x = jnp.floor((line.astype(jnp.float32) + 0.5) * (1.0 / plan.y_len)).astype(jnp.int32)
        plane = x * plan.y_pad + (line - x * plan.y_len)
        code = ((depth >> 7) * plan.planes + plane) * 128 + (depth & 127)
        code = (owner * plan.span + code).astype(jnp.float32)
        for k in range(per_row):
            shift = k * block_atoms
            row = pltpu.roll(code, (128 - shift) % 128, 1)
            charges = pltpu.roll(live, (128 + block_atoms - shift) % 128, 1)
            row = jnp.where(lane < block_atoms, row, charges)
            payload[first + k : first + k + 1, :] = jnp.where(lane < 2 * block_atoms, row, 0.0)
        radius = jnp.zeros((1, 128), jnp.float32)
        for kind in range(type_radius.shape[0]):
            radius = jnp.where(types[0, :, lanes] == kind, type_radius[kind], radius)
        atom_rows[0, 0:3, lanes] = coords[0, :, 0, lanes]
        atom_rows[0, 3:4, lanes] = live
        atom_rows[0, 4:5, lanes] = radius
    for target in range(plan.n_gx):
        copies[target * n_blocks : (target + 1) * n_blocks, :] = payload[...]


def pair_kernel(
    n_blocks, block_atoms, listed, first, part_atoms, listing, low, middle, high, earlier, forces,
    table, columns, results,
):
    tile_atoms = n_blocks * block_atoms
    sides = (low, middle, high)
    for step_x in range(3):
        for step_y in range(3):
            rows = sides[step_y][step_x]
            shifts = (step_x - 1.0, step_y - 1.0, 0.0, 0.0, 0.0)
            for k in range(5):
                row = rows[k : k + 1, :]
                if shifts[k]:
                    row = row + shifts[k]
                table[step_x * 3 + step_y, k] = jnp.broadcast_to(row, (8, tile_atoms))
    columns[0:5, :] = middle[1, :, first : first + part_atoms]
    columns[5:, :] = jnp.zeros((columns.shape[0] - 5, part_atoms), jnp.float32)
    results[...] = jnp.transpose(columns[...])
    lane_ids = lax.broadcasted_iota(jnp.int32, (block_atoms, 128), 1)
    groups = block_atoms // 8

    def group(number, carry):
        place = pl.ds(pl.multiple_of(number * block_atoms, block_atoms), block_atoms)
        block = first // block_atoms + number
        own = results[place, :]
        mine = [
            jnp.broadcast_to(own[:, k : k + 1], (block_atoms, 128)).reshape(groups, 8, 128)
            for k in (0, 1, 2, 4)
        ]
        force_x = force_y = force_z = jnp.zeros((groups, 8, 128), jnp.float32)
        for slot in range(listed):
            rows = table.at[listing[0, slot, 0, block]]
            for start in range(0, tile_atoms, 128):
                lanes = slice(start, start + 128)
                sep_x = mine[0] - rows[0, :, lanes][None]
                sep_y = mine[1] - rows[1, :, lanes][None]
                sep_z = mine[2] - rows[2, :, lanes][None]
                reach = mine[3] + rows[4, :, lanes][None]
                root = lax.rsqrt(sep_x * sep_x + sep_y * sep_y + sep_z * sep_z + reach * reach)
                strength = rows[3, :, lanes][None] * root * (root * root)
                force_x = force_x + strength * sep_x
                force_y = force_y + strength * sep_y
                force_z = force_z + strength * sep_z
        out = jnp.zeros((block_atoms, 128), jnp.float32)
        for axis, total in enumerate((force_x, force_y, force_z)):
            total = jnp.sum(total.reshape(block_atoms, 128), axis=1, keepdims=True)
            out = jnp.where(lane_ids == axis, own[:, 3:4] * total, out)
        results[place, :] = out
        return carry

    lax.fori_loop(0, part_atoms // block_atoms, group, 0)
    columns[...] = jnp.transpose(results[...])
    if first:
        for axis in range(3):
            forces[axis, :, :first] = earlier[axis, :, :first]
    for axis in range(3):
        forces[axis, :, first : first + part_atoms] = columns[axis : axis + 1, :]


VMEM = pl.BlockSpec(memory_space=pltpu.VMEM)
SMEM = pl.BlockSpec(memory_space=pltpu.SMEM)
HBM = pl.BlockSpec(memory_space=pl.ANY)


def shaped(*shape):
    return jax.ShapeDtypeStruct(shape, jnp.float32)


def buffer(*shape):
    return pltpu.VMEM(shape, jnp.float32)


def like(table):
    return pltpu.VMEM(table.shape, table.dtype)


def limit(mib):
    return pltpu.CompilerParams(vmem_limit_bytes=mib * MIB)


def solve_poisson(plan, density, codes, first_code, n_blocks, block_atoms, neighbours, pair_part):
    x_len, y_len, grid = density.shape
    y_pad, x_pad, half, lanes = plan.y_pad, plan.x_pad, plan.half, plan.lanes
    total = plan.parts * plan.modes
    z_full = f32(plan.z_matrix())
    y_table = table_triple(plan.y_matrix(), 1)
    diagonal = f32(plan.diagonal())
    edge_y = f32(plan.edge_weights())
    interface = f32(plan.interface_table())
    bf16 = jnp.bfloat16
    code_shape = codes.shape
    shared = [
        buffer(x_len, y_pad, 128),
        buffer(x_len, y_pad, 128),
        buffer(plan.stack_rows, lanes),
        buffer(plan.lane_tiles, x_pad, 128),
    ]
    spectrum, places, message = pl.pallas_call(
        functools.partial(forward_kernel, plan, n_blocks, block_atoms),
        out_shape=(
            shaped(x_len, y_pad, lanes),
            jax.ShapeDtypeStruct(code_shape, jnp.int32),
            shaped(total, 1, 2 * half),
        ),
        in_specs=[SMEM] + [HBM] * 9,
        out_specs=(HBM, HBM, VMEM),
        scratch_shapes=[buffer(plan.lane_tiles * plan.planes, 128)]
        + shared
        + [
            buffer(2, x_pad, 128),
            buffer(lanes, 2 * half),
            buffer(*code_shape),
            buffer(x_len, y_len, grid),
            like(z_full),
            pltpu.VMEM((3 * lanes, lanes), bf16),
            like(y_table),
            like(diagonal),
            like(edge_y),
            like(interface),
            pltpu.VMEM((3 * plan.stack_rows, 2 * half), bf16),
            buffer(x_len, y_pad, lanes),
            pltpu.VMEM(code_shape, jnp.int32),
            pltpu.SMEM(code_shape, jnp.int32),
            pltpu.SMEM((code_shape[0],), jnp.int32),
            pltpu.SemaphoreType.DMA((11,)),
        ],
        compiler_params=limit(VMEM_MIB),
        name="forward_solve",
    )(first_code, codes, density, z_full, y_table, diagonal, edge_y, interface, *neighbours)
    half_tile = n_blocks * block_atoms // 2
    first_pairs = pair_part(0, half_tile, None)
    incoming = lax.all_to_all(message, ("gx", "gy"), split_axis=0, concat_axis=0, tiled=True)
    gather = plan.gather_table()
    along_y, along_x = plan.line_tables()
    expand = plan.expand_table()
    position = lax.axis_index("gx") * plan.n_gy + lax.axis_index("gy")
    first_mode = (position * plan.modes).astype(jnp.int32).reshape(1)
    stiff = stiffness(grid, grid)
    padded_z = np.zeros(total)
    padded_z[:grid] = stiff
    padded_y = np.zeros((1, lanes))
    padded_y[0, :grid] = stiff
    tables = [
        table_triple(gather, 1),
        f32(along_y),
        f32(along_x),
        f32(table_triple(expand, 0)),
        table_triple(expand, 1),
        f32(stiff[:, None] * grid),
        f32(padded_y * grid),
        table_triple(gather.T, 1),
    ]
    outgoing = pl.pallas_call(
        functools.partial(interface_kernel, plan),
        out_shape=shaped(total, 1, 2 * half),
        in_specs=[SMEM] * 2 + [HBM] * 10,
        out_specs=VMEM,
        scratch_shapes=[
            buffer(plan.modes, 2 * plan.parts, half),
            buffer(plan.modes, plan.kx_pad, lanes),
            buffer(plan.modes, plan.j_pad, lanes),
            buffer(plan.modes, gather.shape[0], half),
            buffer(total, 1, 2 * half),
            *[like(table) for table in tables],
            pltpu.VMEM((3 * along_y.shape[0], lanes), bf16),
            pltpu.VMEM((3 * along_x.shape[0], lanes), bf16),
            pltpu.VMEM((along_y.shape[0], 3 * lanes), bf16),
            pltpu.VMEM((along_x.shape[0], 3 * lanes), bf16),
            pltpu.SemaphoreType.DMA((9,)),
        ],
        compiler_params=limit(VMEM_MIB),
        name="interface_solve",
    )(first_mode, f32((padded_z + SCREENING) * grid), first_pairs, incoming, *tables)
    returned = lax.all_to_all(outgoing, ("gx", "gy"), split_axis=0, concat_axis=0, tiled=True)
    more_pairs = pair_part(half_tile, half_tile // 2, first_pairs)
    potential, values = pl.pallas_call(
        functools.partial(backward_kernel, plan, n_blocks, block_atoms),
        out_shape=(shaped(x_len, y_len, grid), shaped(plan.n_gx * n_blocks, 128)),
        in_specs=[HBM] * 9,
        out_specs=(HBM, VMEM),
        scratch_shapes=[
            buffer(plan.lane_tiles * plan.planes, 128),
            buffer(x_len, y_pad, lanes),
        ]
        + shared
        + [
            buffer(x_pad, 128),
            buffer(lanes, 2 * half),
            buffer(block_atoms, 128),
            buffer(x_len, y_len, grid),
            pltpu.SMEM(code_shape, jnp.int32),
            buffer(total, 1, 2 * half),
            like(interface),
            pltpu.VMEM((plan.stack_rows, 6 * half), bf16),
            like(diagonal),
            like(edge_y),
            buffer(x_len, y_pad, lanes),
            like(y_table),
            like(z_full),
            pltpu.VMEM((3 * lanes, lanes), bf16),
            pltpu.SMEM((code_shape[0],), jnp.int32),
            pltpu.SemaphoreType.DMA((9,)),
        ],
        compiler_params=limit(VMEM_MIB),
        name="backward_solve",
    )(places, returned, interface, diagonal, edge_y, spectrum, y_table, z_full, more_pairs)
    pair_force = pair_part(half_tile + half_tile // 2, half_tile // 2, more_pairs)
    return potential, values, pair_force


def shifted(block, axis, step):
    count = lax.axis_size(axis)
    return lax.ppermute(block, axis, [(i, (i + step) % count) for i in range(count)])


def body(
    qm_density,
    mm_coords,
    mm_charge,
    mm_types,
    type_radius,
    mm_cells,
    block_counts,
    block_owner,
    neighbour_tiles,
):
    n_blocks = block_counts.shape[2]
    tile_atoms = mm_charge.shape[2]
    block_atoms = tile_atoms // n_blocks
    x_local, local_y_rows, grid_len = qm_density.shape
    n_gx = lax.axis_size("gx")
    plan = Plan(x_local, local_y_rows, grid_len, n_gx, lax.axis_size("gy"))
    copies, atom_rows = pl.pallas_call(
        functools.partial(prepare_kernel, plan, n_blocks, block_atoms),
        out_shape=(shaped(n_gx * n_blocks, 128), shaped(1, 5, tile_atoms)),
        in_specs=[SMEM] * 3 + [VMEM] * 4,
        out_specs=(VMEM, VMEM),
        scratch_shapes=[buffer(n_blocks, 128)],
        compiler_params=limit(VMEM_MIB),
        name="prepare_atoms",
    )(
        block_counts.reshape(1, n_blocks),
        block_owner.reshape(1, n_blocks),
        type_radius,
        mm_coords.transpose(0, 2, 1, 3),
        mm_charge,
        mm_types,
        mm_cells,
    )
    codes = lax.all_to_all(copies, "gx", split_axis=0, concat_axis=0, tiled=True)
    first_code = (lax.axis_index("gx") * plan.span).astype(jnp.int32).reshape(1)
    triple = jnp.concatenate(
        [shifted(atom_rows, "gx", 1), atom_rows, shifted(atom_rows, "gx", -1)], axis=0
    )
    below, above = shifted(triple, "gy", 1), shifted(triple, "gy", -1)
    listed = neighbour_tiles.shape[3]
    listing = neighbour_tiles.transpose(0, 3, 1, 2)

    def pair_part(first, part_atoms, earlier):
        if earlier is None:
            earlier = jnp.zeros((3, 1, 128), jnp.float32)
        return pl.pallas_call(
            functools.partial(pair_kernel, n_blocks, block_atoms, listed, first, part_atoms),
            out_shape=shaped(3, 1, first + part_atoms),
            in_specs=[SMEM] + [VMEM] * 4,
            out_specs=VMEM,
            scratch_shapes=[
                buffer(9, 5, 8, tile_atoms),
                buffer(128, part_atoms),
                buffer(part_atoms, 128),
            ],
            compiler_params=limit(VMEM_MIB),
            cost_estimate=pl.CostEstimate(
                flops=21 * listed * tile_atoms * part_atoms,
                bytes_accessed=4 * 50 * tile_atoms,
                transcendentals=listed * tile_atoms * part_atoms,
            ),
            name="pair_forces",
        )(listing, below, triple, above, earlier)

    potential, values, pair_force = solve_poisson(
        plan, qm_density, codes, first_code, n_blocks, block_atoms, (below, above), pair_part
    )
    values = lax.all_to_all(values, "gx", split_axis=0, concat_axis=0, tiled=True)
    sampled = jnp.sum(values.reshape(n_gx, n_blocks, 128), axis=0)[:, :block_atoms]
    lanes = jnp.arange(block_atoms, dtype=jnp.int32)
    live = lanes[None, :] < block_counts.reshape(n_blocks, 1)
    mm_potential = jnp.where(live, sampled, 0.0).reshape(1, 1, tile_atoms)
    return (potential, mm_potential, pair_force[None].transpose(0, 2, 1, 3))


def solution(mesh):
    placed = (
        P("gx", "gy", None),
        P("gx", "gy", None, None),
        P("gx", "gy", None),
        P("gx", "gy", None),
        P(),
        P("gx", "gy", None),
        P("gx", "gy", None),
        P("gx", "gy", None, None),
        P("gx", "gy", None, None),
    )
    return jax.shard_map(
        body,
        mesh=mesh,
        in_specs=placed,
        out_specs=(P("gx", "gy", None), P("gx", "gy", None), P("gx", "gy", None, None)),
        check_vma=False,
    )
```

```python
import functools

import jax
import jax.numpy as jnp
import ml_dtypes
import numpy as np
from jax import lax
from jax.experimental import pallas as pl
from jax.experimental.pallas import tpu as pltpu
from jax.sharding import PartitionSpec as P

SCREENING = 0.003
HIGH_ACCURACY = lax.Precision.HIGHEST
VMEM_MIB = 60
BATCH = 16
MIB = 1024 * 1024


def round_up(value, unit):
    return -(-value // unit) * unit


def sine_matrix(length):
    nodes = np.arange(length, dtype=np.float64)
    return np.sqrt(2.0 / length) * np.sin(np.pi * np.outer(nodes, nodes) / length)


def cas_matrix(length):
    nodes = np.arange(length)
    angle = 2.0 * np.pi * (np.outer(nodes, nodes) % length) / length
    return np.cos(angle) + np.sin(angle)


def stiffness(count, length):
    return 4.0 * np.sin(np.pi * np.arange(count) / length) ** 2


def split_pair(matrix):
    full = np.asarray(matrix, np.float32)
    high = full.astype(ml_dtypes.bfloat16)
    low = (full - high.astype(np.float32)).astype(ml_dtypes.bfloat16)
    return high, low


def table_triple(matrix, axis):
    high, low = split_pair(matrix)
    return np.concatenate([high, low, high], axis=axis)


def f32(table):
    return np.asarray(table, np.float32)


class Plan:
    def __init__(self, x_len, y_len, grid, n_gx, n_gy):
        self.x_len, self.y_len, self.grid = x_len, y_len, grid
        self.n_gx, self.n_gy = n_gx, n_gy
        self.y_pad = round_up(y_len, 8)
        self.x_pad = round_up(x_len, 8)
        self.lanes = round_up(grid, 128)
        self.lane_tiles = self.lanes // 128
        self.planes = x_len * self.y_pad
        self.span = self.lane_tiles * self.planes * 128
        self.parts = n_gx * n_gy
        self.modes = -(-grid // self.parts)
        self.half = round_up(y_len + x_len, 128)
        self.kx_pad = round_up(n_gx, 8)
        self.j_pad = round_up(n_gy, 8)
        self.stack_rows = round_up(3 * self.y_pad + 2 * self.x_pad, 128)

    def y_matrix(self):
        out = np.zeros((self.y_pad, self.y_pad))
        out[: self.y_len, : self.y_len] = sine_matrix(self.y_len)
        return out

    def z_matrix(self):
        out = np.zeros((self.lanes, self.lanes))
        out[: self.grid, : self.grid] = cas_matrix(self.grid) / np.sqrt(self.grid)
        return out

    def elimination_factors(self):
        z_part = np.zeros(self.lanes)
        z_part[: self.grid] = stiffness(self.grid, self.grid)
        y_part = stiffness(self.y_pad, 2 * self.y_len)
        diagonal = 2.0 + y_part[:, None] + z_part[None, :] + SCREENING
        out = np.zeros((self.x_len, self.y_pad, self.lanes))
        for x in range(1, self.x_len):
            out[x] = 1.0 / (diagonal - out[x - 1])
        return out

    def edge_weights(self):
        sine_y = self.y_matrix()
        both = np.stack([sine_y[1], sine_y[self.y_len - 1]])
        return np.broadcast_to(both[:, :, None], (2, self.y_pad, 128))

    def interface_table(self):
        x_len, y_len, half = self.x_len, self.y_len, self.half
        y_pad, x_pad = self.y_pad, self.x_pad
        sine_y = sine_matrix(y_len)
        out = np.zeros((self.stack_rows, 2 * half))
        out[:y_len, :y_len] = sine_y
        row = y_pad
        out[row : row + y_len, half : half + y_len] = sine_y
        row += y_pad
        out[row : row + y_len, :y_len] = np.eye(y_len)
        row += y_pad
        out[row + 1 : row + x_len, y_len + 1 : y_len + x_len] = np.eye(x_len - 1)
        row += x_pad
        far = half + y_len
        out[row + 1 : row + x_len, far + 1 : far + x_len] = np.eye(x_len - 1)
        return out

    def gather_table(self):
        n_gx, n_gy, parts = self.n_gx, self.n_gy, self.parts
        cas_x = cas_matrix(n_gx)
        out = np.zeros((n_gy * self.kx_pad + n_gx * self.j_pad, 2 * parts))
        for i in range(n_gx):
            for j in range(n_gy):
                col = i * n_gy + j
                base = j * self.kx_pad
                out[base : base + n_gx, col] = cas_x[:, i]
                out[base : base + n_gx, parts + col] = cas_x[:, (i + 1) % n_gx]
                base = n_gy * self.kx_pad + i * self.j_pad
                out[base + j, col] = 1.0
                out[base + (j + 1) % n_gy, parts + col] = 1.0
        return out

    def line_tables(self):
        scaled = cas_matrix(self.grid) / np.sqrt(self.grid)
        along_y = np.zeros((self.n_gy, self.half, self.lanes))
        along_x = np.zeros((self.n_gx, self.half, self.lanes))
        y_len, x_len, grid = self.y_len, self.x_len, self.grid
        for j in range(self.n_gy):
            along_y[j, :y_len, :grid] = scaled[j * y_len : (j + 1) * y_len]
        for i in range(self.n_gx):
            along_x[i, y_len : y_len + x_len, :grid] = scaled[i * x_len : (i + 1) * x_len]
        return along_y.reshape(-1, self.lanes), along_x.reshape(-1, self.lanes)

    def expand_table(self):
        ratio = self.grid // self.n_gy
        full = cas_matrix(self.grid)
        out = np.zeros((self.j_pad, self.lanes))
        for j in range(self.n_gy):
            out[j, : self.grid] = full[(j * ratio) % self.grid]
        return np.where(np.abs(out - np.round(out)) < 1e-9, np.round(out), out)


def dot(a, b, dims=((1,), (0,)), precision=None):
    return lax.dot_general(
        a, b, (dims, ((), ())), precision=precision, preferred_element_type=jnp.float32
    )


def value_parts(value, axis, count):
    high = value.astype(jnp.bfloat16).astype(jnp.float32)
    return jnp.concatenate([high] * (count - 1) + [value - high], axis=axis)


def table_parts(matrix, axis):
    high, low = split_pair(matrix)
    if low.astype(np.float32).any():
        return np.concatenate([high, low, high], axis=axis)
    return np.concatenate([high, high], axis=axis)


def value_triple(value, axis):
    high = value.astype(jnp.bfloat16).astype(jnp.float32)
    return jnp.concatenate([high, high, value - high], axis=axis).astype(jnp.bfloat16)


def split_table(source, target, axis):
    value = source[...]
    high = value.astype(jnp.bfloat16).astype(jnp.float32)
    parts = jnp.concatenate([high, value - high, high], axis=axis)
    target[...] = parts.astype(jnp.bfloat16)


def left_apply(table, value):
    return dot(table, value_triple(value, 0))


def right_apply(value, table):
    return dot(value_triple(value, 1), table)


def slab_count(plan):
    if plan.y_pad != plan.y_len:
        return 1
    return max(count for count in (4, 3, 2, 1) if plan.x_len % count == 0)


def inverse(value):
    guess = pl.reciprocal(value, approx=True)
    guess = guess * (2.0 - value * guess)
    return guess * (2.0 - value * guess)


def start_copies(pairs, sems):
    copies = [
        pltpu.make_async_copy(source, target, sems.at[k])
        for k, (source, target) in enumerate(pairs)
    ]
    for copy in copies:
        copy.start()
    return copies


def list_owned(plan, places, blocks, block_count):
    def several(step, count):
        for k in range(8):
            number = step * 8 + k
            lead = places[number, 0]
            blocks[count] = number
            count = count + jnp.where((lead >= 0) & (lead < plan.span), 1, 0)
        return count

    return lax.fori_loop(0, block_count // 8, several, 0)


def chunked_loop(count, unroll, body, init):
    while count % unroll:
        unroll -= 1

    def group(step, carry):
        for k in range(unroll):
            carry = body(step * unroll + k, carry)
        return carry

    return lax.fori_loop(0, count // unroll, group, init)


def mark_places(codes, first_code, place_rows, block_atoms):
    lane = lax.broadcasted_iota(jnp.int32, codes.shape, 1)
    code = codes[...].astype(jnp.int32) - first_code
    place = lax.shift_right_arithmetic(code, 7)
    shared = jnp.zeros_like(place)
    for step in range(1, BATCH):
        same = (pltpu.roll(place, step, 1) == place) & (lane % BATCH >= step)
        shared = jnp.where(same & (lane < block_atoms), 1, shared)
    step = block_atoms // 2
    while step:
        shared = shared | pltpu.roll(shared, 128 - step, 1)
        step //= 2
    mark = pltpu.roll(shared, block_atoms, 1)
    place_rows[...] = jnp.where(lane == block_atoms, mark, code)


def forward_kernel(
    plan,
    n_blocks,
    block_atoms,
    first_code,
    *refs,
):
    (
        codes_hbm,
        density_hbm,
        z_full_hbm,
        y_table_hbm,
        factors_hbm,
        edge_y_hbm,
        interface_hbm,
        _,
        _,
        spectrum_hbm,
        places_hbm,
        message,
        added,
        solved,
        stack,
        heads,
        edge_rows,
        turned,
        codes,
        density,
        z_full,
        z_table,
        y_table,
        factors,
        edge_y,
        interface_full,
        interface,
        spectrum,
        place_rows,
        places,
        blocks,
        sems,
    ) = refs
    x_len, y_len, y_pad, x_pad = plan.x_len, plan.y_len, plan.y_pad, plan.x_pad
    grid, lane_count, planes = plan.grid, plan.lanes, plan.planes
    slabs = slab_count(plan)
    lane_ids = lax.broadcasted_iota(jnp.int32, (1, 128), 1)
    loads = start_copies(
        [
            (codes_hbm, codes),
            (density_hbm, density),
            (z_full_hbm, z_full),
            (y_table_hbm, y_table),
            (factors_hbm, factors),
            (edge_y_hbm, edge_y),
            (interface_hbm, interface_full),
        ],
        sems,
    )
    loads[0].wait()
    mark_places(codes, first_code[0], place_rows, block_atoms)
    place_copies = [
        pltpu.make_async_copy(place_rows, places, sems.at[8]),
        pltpu.make_async_copy(place_rows, places_hbm, sems.at[9]),
    ]
    for copy in place_copies:
        copy.start()

    def clear(step, carry):
        place = pl.ds(pl.multiple_of(step * y_pad, 8), y_pad)
        added[place, :] = jnp.zeros((y_pad, 128), jnp.float32)
        return carry

    chunked_loop(plan.lane_tiles * x_len, 4, clear, 0)
    loads[2].wait()
    split_table(z_full, z_table, 0)
    place_copies[0].wait()
    count = list_owned(plan, places, blocks, plan.n_gx * n_blocks)

    def deposit(slot, carry):
        block = blocks[slot]
        row_codes = places.at[block]
        charge_row = codes[pl.ds(block, 1), :]

        def raised(code, k):
            charge = charge_row[:, block_atoms + k : block_atoms + k + 1]
            hit = jnp.where(lane_ids == (code & 127), charge, 0.0)
            return added[pl.ds(lax.shift_right_logical(code, 7), 1), :] + hit

        @pl.when(row_codes[block_atoms] == 0)
        def _():
            for start in range(0, block_atoms, BATCH):
                local = [row_codes[start + k] for k in range(BATCH)]
                rows = [raised(code, start + k) for k, code in enumerate(local)]
                for code, row in zip(local, rows):
                    added[pl.ds(lax.shift_right_logical(code, 7), 1), :] = row

        @pl.when(row_codes[block_atoms] != 0)
        def _():
            for k in range(block_atoms):
                code = row_codes[k]
                row = raised(code, k)
                added[pl.ds(lax.shift_right_logical(code, 7), 1), :] = row

        return carry

    lax.fori_loop(0, count, deposit, 0)
    loads[1].wait()
    loads[3].wait()

    def transform(step, carry):
        start = step * slabs
        count = slabs * y_pad
        pieces = []
        for tile in range(plan.lane_tiles):
            low = tile * 128
            width = min(128, grid - low)
            piece = density.at[pl.ds(start, slabs)][:, :, low : low + width]
            if y_pad == y_len:
                piece = piece.reshape(count, width)
            else:
                rows = jnp.zeros((y_pad - y_len, width), jnp.float32)
                piece = jnp.concatenate([piece[0], rows], axis=0)
            if width < 128:
                rest = jnp.zeros((count, 128 - width), jnp.float32)
                piece = jnp.concatenate([piece, rest], axis=1)
            place = pl.ds(pl.multiple_of(tile * planes + start * y_pad, 8), count)
            pieces.append(piece + added.at[place][...])
        lines = right_apply(jnp.concatenate(pieces, axis=1), z_table[...])
        lines = lines.reshape(slabs, y_pad, lane_count)
        for slab in range(slabs):
            x = start + slab
            for tile in range(plan.lane_tiles):
                heads[tile, pl.ds(x, 1), :] = lines[slab, 0:1, tile * 128 : tile * 128 + 128]
            spectrum.at[x][...] = left_apply(y_table[...], lines[slab])

        @pl.when(step == 0)
        def _():
            stack[2 * y_pad : 3 * y_pad, :] = lines[0]

        return carry

    chunked_loop(x_len // slabs, 3, transform, 0)
    spectrum_copy = pltpu.make_async_copy(spectrum, spectrum_hbm, sems.at[10])
    spectrum_copy.start()
    for copy in loads[4:]:
        copy.wait()
    split_table(interface_full, interface, 0)
    stack[3 * y_pad :, :] = jnp.zeros((stack.shape[0] - 3 * y_pad, lane_count), jnp.float32)
    for tile in range(plan.lane_tiles):
        lanes = slice(tile * 128, tile * 128 + 128)
        near_weight = edge_y[0]
        far_weight = edge_y[1]

        def eliminate(step, carry):
            x = step + 1
            value = (spectrum.at[x][:, lanes] + carry) * factors.at[x][:, lanes]
            solved.at[x][...] = value
            return value

        def substitute(step, value):
            x = x_len - 1 - step
            value = solved.at[x][...] + factors.at[x][:, lanes] * value
            near_row = jnp.sum(value * near_weight, axis=0, keepdims=True)
            far_row = jnp.sum(value * far_weight, axis=0, keepdims=True)
            edge_rows[0, pl.ds(x, 1), :] = near_row + heads[tile, pl.ds(x, 1), :]
            edge_rows[1, pl.ds(x, 1), :] = far_row
            return value

        zero = jnp.zeros((y_pad, 128), jnp.float32)
        chunked_loop(x_len - 1, 5, eliminate, zero)
        stack[y_pad : 2 * y_pad, lanes] = solved[x_len - 1]
        stack[0:y_pad, lanes] = chunked_loop(x_len - 1, 5, substitute, zero)
        for side in range(2):
            row = 3 * y_pad + side * x_pad
            stack[row + 1 : row + x_len, lanes] = edge_rows[side, 1:x_len, :]
    turned[...] = right_apply(jnp.transpose(stack[...]), interface[...])
    total = plan.parts * plan.modes
    for mode in range(grid):
        message[mode] = turned[mode : mode + 1, :]
    if total > grid:
        message[grid:total] = jnp.zeros((total - grid, 1, 2 * plan.half), jnp.float32)
    spectrum_copy.wait()
    place_copies[1].wait()


def interface_kernel(
    plan,
    first_mode,
    stiff_z,
    _,
    incoming_hbm,
    gather_hbm,
    along_y_hbm,
    along_x_hbm,
    expand_hbm,
    expand_back_hbm,
    stiff_x_hbm,
    stiff_y_hbm,
    scatter_hbm,
    outgoing,
    rows,
    folded_y,
    folded_x,
    lines,
    incoming,
    gather,
    along_y_full,
    along_x_full,
    expand,
    expand_back,
    stiff_x,
    stiff_y,
    scatter,
    along_y,
    along_x,
    along_y_back,
    along_x_back,
    sems,
):
    loads = start_copies(
        [
            (incoming_hbm, incoming),
            (gather_hbm, gather),
            (along_y_hbm, along_y_full),
            (along_x_hbm, along_x_full),
            (expand_hbm, expand),
            (expand_back_hbm, expand_back),
            (stiff_x_hbm, stiff_x),
            (stiff_y_hbm, stiff_y),
            (scatter_hbm, scatter),
        ],
        sems,
    )
    grid, half, parts, modes = plan.grid, plan.half, plan.parts, plan.modes
    kx_pad, j_pad, n_gx, n_gy = plan.kx_pad, plan.j_pad, plan.n_gx, plan.n_gy
    lane_count = plan.lanes
    groups = grid // n_gx

    def collect(source, carry):
        for mode in range(modes):
            both = incoming.at[source * modes + mode][...]
            rows[mode, pl.ds(source, 1), :] = both[:, :half]
            rows[mode, pl.ds(parts + source, 1), :] = both[:, half:]
        return carry

    loads[0].wait()
    lax.fori_loop(0, parts, collect, 0)
    loads[1].wait()
    for mode in range(modes):
        lines[mode] = left_apply(gather[...], rows[mode])
    base = n_gy * kx_pad
    y_slots = [slice(j * kx_pad, (j + 1) * kx_pad) for j in range(n_gy)]
    x_slots = [slice(base + i * j_pad, base + (i + 1) * j_pad) for i in range(n_gx)]

    def side_by_side(slots, count):
        return jnp.concatenate(
            [lines[:, slot, :].reshape(modes * count, half) for slot in slots], axis=1
        )

    loads[2].wait()
    split_table(along_y_full, along_y, 0)
    loads[3].wait()
    split_table(along_x_full, along_x, 0)
    folded_y[...] = right_apply(side_by_side(y_slots, kx_pad), along_y[...]).reshape(
        modes, kx_pad, lane_count
    )
    folded_x[...] = right_apply(side_by_side(x_slots, j_pad), along_x[...]).reshape(
        modes, j_pad, lane_count
    )

    def solve(mode, carry):
        across = value_parts(folded_x[mode, :, :grid], 0, expand.shape[0] // j_pad)
        spread = dot(across, expand[...], ((0,), (0,)))
        number = spread.reshape(groups, kx_pad, lane_count) + folded_y[mode][None]
        bottom = stiff_x[...] + (stiff_y[...] + stiff_z[first_mode[0] + mode])
        value = number * inverse(bottom).reshape(groups, kx_pad, lane_count)
        folded_y[mode] = jnp.sum(value, axis=0)
        value = value_parts(value.reshape(grid, lane_count), 1, expand.shape[0] // j_pad)
        value = value.astype(jnp.bfloat16)
        folded_x[mode, :, :grid] = dot(expand_back[...], value, ((1,), (1,)))
        return carry

    for copy in loads[4:8]:
        copy.wait()
    chunked_loop(modes, 3, solve, 0)
    loads[8].wait()
    split_table(along_y_full, along_y_back, 1)
    split_table(along_x_full, along_x_back, 1)
    all_y = folded_y[...].reshape(modes * kx_pad, lane_count)
    all_y = dot(value_triple(all_y, 1), along_y_back[...], ((1,), (1,)))
    for j, slot in enumerate(y_slots):
        lines[:, slot, :] = all_y[:, j * half : (j + 1) * half].reshape(modes, kx_pad, half)
    all_x = folded_x[...].reshape(modes * j_pad, lane_count)
    all_x = dot(value_triple(all_x, 1), along_x_back[...], ((1,), (1,)))
    for i, slot in enumerate(x_slots):
        lines[:, slot, :] = all_x[:, i * half : (i + 1) * half].reshape(modes, j_pad, half)
    for mode in range(modes):
        rows[mode] = left_apply(scatter[...], lines[mode])

    def distribute(target, carry):
        for mode in range(modes):
            outgoing[target * modes + mode, :, :half] = rows[mode, pl.ds(target, 1), :]
            outgoing[target * modes + mode, :, half:] = rows[mode, pl.ds(parts + target, 1), :]
        return carry

    lax.fori_loop(0, parts, distribute, 0)


def backward_kernel(
    plan,
    n_blocks,
    block_atoms,
    places_hbm,
    message_hbm,
    interface_hbm,
    factors_hbm,
    edge_y_hbm,
    spectrum_hbm,
    y_table_hbm,
    z_full_hbm,
    _,
    potential_hbm,
    values,
    lookup,
    work,
    solved,
    stack,
    heads,
    edge_rows,
    turned,
    picked,
    potential,
    places,
    message,
    interface_full,
    interface,
    factors,
    edge_y,
    spectrum,
    y_table,
    z_full,
    z_table,
    blocks,
    sems,
):
    x_len, y_len, y_pad, x_pad = plan.x_len, plan.y_len, plan.y_pad, plan.x_pad
    grid, lane_count, planes = plan.grid, plan.lanes, plan.planes
    slabs = slab_count(plan)
    loads = start_copies(
        [
            (message_hbm, message),
            (interface_hbm, interface_full),
            (places_hbm, places),
            (factors_hbm, factors),
            (edge_y_hbm, edge_y),
            (spectrum_hbm, spectrum),
            (y_table_hbm, y_table),
            (z_full_hbm, z_full),
        ],
        sems,
    )
    loads[0].wait()
    for mode in range(grid):
        turned[mode : mode + 1, :] = message[mode]
    if lane_count > grid:
        turned[grid:, :] = jnp.zeros((lane_count - grid, turned.shape[1]), jnp.float32)
    loads[1].wait()
    split_table(interface_full, interface, 1)
    stack[...] = dot(interface[...], value_triple(turned[...], 1), ((1,), (1,)))
    loads[2].wait()
    count = list_owned(plan, places, blocks, plan.n_gx * n_blocks)
    for copy in loads[3:]:
        copy.wait()
    split_table(z_full, z_table, 0)
    for tile in range(plan.lane_tiles):
        lanes = slice(tile * 128, tile * 128 + 128)
        near_weight = edge_y[0]
        far_weight = edge_y[1]
        heads[tile] = stack[3 * y_pad : 3 * y_pad + x_pad, lanes]
        edge_rows[...] = stack[3 * y_pad + x_pad : 3 * y_pad + 2 * x_pad, lanes]

        def eliminate(step, carry):
            x = step + 1
            load = spectrum.at[x][:, lanes] + near_weight * heads[tile, pl.ds(x, 1), :]
            load = load + far_weight * edge_rows[pl.ds(x, 1), :]
            value = (load + carry) * factors.at[x][:, lanes]
            solved.at[x][...] = value
            return value

        def substitute(step, value):
            x = x_len - 1 - step
            value = solved.at[x][...] + factors.at[x][:, lanes] * value
            work.at[x][:, lanes] = value
            return value

        chunked_loop(x_len - 1, 5, eliminate, stack[0:y_pad, lanes])
        chunked_loop(x_len - 1, 5, substitute, stack[y_pad : 2 * y_pad, lanes])
    work[0] = jnp.zeros((y_pad, lane_count), jnp.float32)

    def transform(step, carry):
        start = step * slabs
        for slab in range(slabs):
            x = start + slab
            slab_work = work.at[x]
            slab_work[...] = left_apply(y_table[...], slab_work[...])
            for tile in range(plan.lane_tiles):
                lanes = slice(tile * 128, tile * 128 + 128)
                slab_work[0:1, lanes] = heads[tile, pl.ds(x, 1), :]

        @pl.when(step == 0)
        def _():
            work[0] = stack[2 * y_pad : 3 * y_pad, :]

        lines = work.at[pl.ds(start, slabs)][...].reshape(slabs * y_pad, lane_count)
        lines = right_apply(lines, z_table[...])
        for tile in range(plan.lane_tiles):
            low = tile * 128
            place = pl.ds(pl.multiple_of(tile * planes + start * y_pad, 8), slabs * y_pad)
            lookup.at[place][...] = lines[:, low : low + 128]
        lines = lines.reshape(slabs, y_pad, lane_count)
        potential.at[pl.ds(start, slabs)][...] = lines[:, :y_len, :grid]
        return carry

    chunked_loop(x_len // slabs, 3, transform, 0)
    potential_copy = pltpu.make_async_copy(potential, potential_hbm, sems.at[8])
    potential_copy.start()
    values[...] = jnp.zeros(values.shape, jnp.float32)
    lane_ids = lax.broadcasted_iota(jnp.int32, (1, 128), 1)
    shape = (block_atoms, 128)
    own_lane = lax.broadcasted_iota(jnp.int32, shape, 0) == lax.broadcasted_iota(
        jnp.int32, shape, 1
    )

    def reduce_rows(rows, block):
        found = jnp.sum(rows, axis=1, keepdims=True)
        found = jnp.sum(jnp.where(own_lane, found, 0.0), axis=0, keepdims=True)
        values[pl.ds(block, 1), :] = found

    def sample(slot, before):
        block = blocks[slot]
        row_codes = places.at[block]
        rows_before = picked[...]
        for first in range(0, block_atoms, 16):
            rows = []
            for atom in range(first, first + 16):
                code = row_codes[atom]
                row = lookup[pl.ds(lax.shift_right_logical(code, 7), 1), :]
                rows.append(jnp.where(lane_ids == (code & 127), row, 0.0))
            for k in range(16):
                picked[first + k : first + k + 1, :] = rows[k]
        reduce_rows(rows_before, before)
        return block

    picked[...] = jnp.zeros(picked.shape, jnp.float32)
    last = lax.fori_loop(0, count, sample, blocks[0])

    @pl.when(count > 0)
    def _():
        reduce_rows(picked[...], last)

    potential_copy.wait()


def prepare_kernel(
    plan, n_blocks, block_atoms, counts, owners, type_radius, coords, charge, types, cells,
    copies, atom_rows, payload,
):
    tile_atoms = n_blocks * block_atoms
    lane = lax.broadcasted_iota(jnp.int32, (1, 128), 1)
    slot = lane // block_atoms
    atom = lane - slot * block_atoms
    per_row = 128 // block_atoms
    for start in range(0, tile_atoms, 128):
        lanes = slice(start, start + 128)
        first = start // block_atoms
        count = jnp.full((1, 128), counts[0, first], jnp.int32)
        owner = jnp.full((1, 128), owners[0, first], jnp.int32)
        for k in range(1, per_row):
            count = jnp.where(slot >= k, counts[0, first + k], count)
            owner = jnp.where(slot >= k, owners[0, first + k], owner)
        live = jnp.where(atom < count, charge[0, :, lanes], 0.0)
        cell = cells[0, :, lanes]
        line = jnp.floor((cell.astype(jnp.float32) + 0.5) * (1.0 / plan.grid)).astype(jnp.int32)
        depth = cell - line * plan.grid
        x = jnp.floor((line.astype(jnp.float32) + 0.5) * (1.0 / plan.y_len)).astype(jnp.int32)
        plane = x * plan.y_pad + (line - x * plan.y_len)
        code = ((depth >> 7) * plan.planes + plane) * 128 + (depth & 127)
        code = (owner * plan.span + code).astype(jnp.float32)
        for k in range(per_row):
            shift = k * block_atoms
            row = pltpu.roll(code, (128 - shift) % 128, 1)
            charges = pltpu.roll(live, (128 + block_atoms - shift) % 128, 1)
            row = jnp.where(lane < block_atoms, row, charges)
            payload[first + k : first + k + 1, :] = jnp.where(lane < 2 * block_atoms, row, 0.0)
        radius = jnp.zeros((1, 128), jnp.float32)
        for kind in range(type_radius.shape[0]):
            radius = jnp.where(types[0, :, lanes] == kind, type_radius[kind], radius)
        atom_rows[0, 0:3, lanes] = coords[0, :, 0, lanes]
        atom_rows[0, 3:4, lanes] = live
        atom_rows[0, 4:5, lanes] = radius
    for target in range(plan.n_gx):
        copies[target * n_blocks : (target + 1) * n_blocks, :] = payload[...]


def pair_kernel(
    n_blocks, block_atoms, listed, first, part_atoms, listing, low, middle, high, earlier, forces,
    table, columns, results,
):
    tile_atoms = n_blocks * block_atoms
    sides = (low, middle, high)
    for step_x in range(3):
        for step_y in range(3):
            rows = sides[step_y][step_x]
            shifts = (step_x - 1.0, step_y - 1.0, 0.0, 0.0, 0.0)
            for k in range(5):
                row = rows[k : k + 1, :]
                if shifts[k]:
                    row = row + shifts[k]
                table[step_x * 3 + step_y, k] = jnp.broadcast_to(row, (8, tile_atoms))
    columns[0:5, :] = middle[1, :, first : first + part_atoms]
    columns[5:, :] = jnp.zeros((columns.shape[0] - 5, part_atoms), jnp.float32)
    results[...] = jnp.transpose(columns[...])
    lane_ids = lax.broadcasted_iota(jnp.int32, (block_atoms, 128), 1)
    groups = block_atoms // 8

    def group(number, carry):
        place = pl.ds(pl.multiple_of(number * block_atoms, block_atoms), block_atoms)
        block = first // block_atoms + number
        own = results[place, :]
        mine = [
            jnp.broadcast_to(own[:, k : k + 1], (block_atoms, 128)).reshape(groups, 8, 128)
            for k in (0, 1, 2, 4)
        ]
        force_x = force_y = force_z = jnp.zeros((groups, 8, 128), jnp.float32)
        for slot in range(listed):
            rows = table.at[listing[0, slot, 0, block]]
            for start in range(0, tile_atoms, 128):
                lanes = slice(start, start + 128)
                sep_x = mine[0] - rows[0, :, lanes][None]
                sep_y = mine[1] - rows[1, :, lanes][None]
                sep_z = mine[2] - rows[2, :, lanes][None]
                reach = mine[3] + rows[4, :, lanes][None]
                root = lax.rsqrt(sep_x * sep_x + sep_y * sep_y + sep_z * sep_z + reach * reach)
                strength = rows[3, :, lanes][None] * root * (root * root)
                force_x = force_x + strength * sep_x
                force_y = force_y + strength * sep_y
                force_z = force_z + strength * sep_z
        out = jnp.zeros((block_atoms, 128), jnp.float32)
        for axis, total in enumerate((force_x, force_y, force_z)):
            total = jnp.sum(total.reshape(block_atoms, 128), axis=1, keepdims=True)
            out = jnp.where(lane_ids == axis, own[:, 3:4] * total, out)
        results[place, :] = out
        return carry

    lax.fori_loop(0, part_atoms // block_atoms, group, 0)
    columns[...] = jnp.transpose(results[...])
    if first:
        for axis in range(3):
            forces[axis, :, :first] = earlier[axis, :, :first]
    for axis in range(3):
        forces[axis, :, first : first + part_atoms] = columns[axis : axis + 1, :]


VMEM = pl.BlockSpec(memory_space=pltpu.VMEM)
SMEM = pl.BlockSpec(memory_space=pltpu.SMEM)
HBM = pl.BlockSpec(memory_space=pl.ANY)


def shaped(*shape):
    return jax.ShapeDtypeStruct(shape, jnp.float32)


def buffer(*shape):
    return pltpu.VMEM(shape, jnp.float32)


def like(table):
    return pltpu.VMEM(table.shape, table.dtype)


def limit(mib):
    return pltpu.CompilerParams(vmem_limit_bytes=mib * MIB)


def solve_poisson(plan, density, codes, first_code, n_blocks, block_atoms, neighbours, pair_part):
    x_len, y_len, grid = density.shape
    y_pad, x_pad, half, lanes = plan.y_pad, plan.x_pad, plan.half, plan.lanes
    total = plan.parts * plan.modes
    z_full = f32(plan.z_matrix())
    y_table = table_triple(plan.y_matrix(), 1)
    factors = f32(plan.elimination_factors())
    edge_y = f32(plan.edge_weights())
    interface = f32(plan.interface_table())
    bf16 = jnp.bfloat16
    code_shape = codes.shape
    shared = [
        buffer(x_len, y_pad, 128),
        buffer(plan.stack_rows, lanes),
        buffer(plan.lane_tiles, x_pad, 128),
    ]
    spectrum, places, message = pl.pallas_call(
        functools.partial(forward_kernel, plan, n_blocks, block_atoms),
        out_shape=(
            shaped(x_len, y_pad, lanes),
            jax.ShapeDtypeStruct(code_shape, jnp.int32),
            shaped(total, 1, 2 * half),
        ),
        in_specs=[SMEM] + [HBM] * 9,
        out_specs=(HBM, HBM, VMEM),
        scratch_shapes=[buffer(plan.lane_tiles * plan.planes, 128)]
        + shared
        + [
            buffer(2, x_pad, 128),
            buffer(lanes, 2 * half),
            buffer(*code_shape),
            buffer(x_len, y_len, grid),
            like(z_full),
            pltpu.VMEM((3 * lanes, lanes), bf16),
            like(y_table),
            like(factors),
            like(edge_y),
            like(interface),
            pltpu.VMEM((3 * plan.stack_rows, 2 * half), bf16),
            buffer(x_len, y_pad, lanes),
            pltpu.VMEM(code_shape, jnp.int32),
            pltpu.SMEM(code_shape, jnp.int32),
            pltpu.SMEM((code_shape[0],), jnp.int32),
            pltpu.SemaphoreType.DMA((11,)),
        ],
        compiler_params=limit(VMEM_MIB),
        name="forward_solve",
    )(first_code, codes, density, z_full, y_table, factors, edge_y, interface, *neighbours)
    eighth = n_blocks * block_atoms // 8
    first_pairs = pair_part(0, 4 * eighth, None)
    incoming = lax.all_to_all(message, ("gx", "gy"), split_axis=0, concat_axis=0, tiled=True)
    gather = plan.gather_table()
    along_y, along_x = plan.line_tables()
    expand = plan.expand_table()
    position = lax.axis_index("gx") * plan.n_gy + lax.axis_index("gy")
    first_mode = (position * plan.modes).astype(jnp.int32).reshape(1)
    stiff = stiffness(grid, grid)
    padded_z = np.zeros(total)
    padded_z[:grid] = stiff
    padded_y = np.zeros((1, lanes))
    padded_y[0, :grid] = stiff
    tables = [
        table_triple(gather, 1),
        f32(along_y),
        f32(along_x),
        f32(table_parts(expand, 0)),
        table_parts(expand, 1),
        f32(stiff[:, None] * grid),
        f32(padded_y * grid),
        table_triple(gather.T, 1),
    ]
    outgoing = pl.pallas_call(
        functools.partial(interface_kernel, plan),
        out_shape=shaped(total, 1, 2 * half),
        in_specs=[SMEM] * 2 + [HBM] * 10,
        out_specs=VMEM,
        scratch_shapes=[
            buffer(plan.modes, 2 * plan.parts, half),
            buffer(plan.modes, plan.kx_pad, lanes),
            buffer(plan.modes, plan.j_pad, lanes),
            buffer(plan.modes, gather.shape[0], half),
            buffer(total, 1, 2 * half),
            *[like(table) for table in tables],
            pltpu.VMEM((3 * along_y.shape[0], lanes), bf16),
            pltpu.VMEM((3 * along_x.shape[0], lanes), bf16),
            pltpu.VMEM((along_y.shape[0], 3 * lanes), bf16),
            pltpu.VMEM((along_x.shape[0], 3 * lanes), bf16),
            pltpu.SemaphoreType.DMA((9,)),
        ],
        compiler_params=limit(VMEM_MIB),
        name="interface_solve",
    )(first_mode, f32((padded_z + SCREENING) * grid), first_pairs, incoming, *tables)
    returned = lax.all_to_all(outgoing, ("gx", "gy"), split_axis=0, concat_axis=0, tiled=True)
    more_pairs = pair_part(4 * eighth, 3 * eighth, first_pairs)
    potential, values = pl.pallas_call(
        functools.partial(backward_kernel, plan, n_blocks, block_atoms),
        out_shape=(shaped(x_len, y_len, grid), shaped(plan.n_gx * n_blocks, 128)),
        in_specs=[HBM] * 9,
        out_specs=(HBM, VMEM),
        scratch_shapes=[
            buffer(plan.lane_tiles * plan.planes, 128),
            buffer(x_len, y_pad, lanes),
        ]
        + shared
        + [
            buffer(x_pad, 128),
            buffer(lanes, 2 * half),
            buffer(block_atoms, 128),
            buffer(x_len, y_len, grid),
            pltpu.SMEM(code_shape, jnp.int32),
            buffer(total, 1, 2 * half),
            like(interface),
            pltpu.VMEM((plan.stack_rows, 6 * half), bf16),
            like(factors),
            like(edge_y),
            buffer(x_len, y_pad, lanes),
            like(y_table),
            like(z_full),
            pltpu.VMEM((3 * lanes, lanes), bf16),
            pltpu.SMEM((code_shape[0],), jnp.int32),
            pltpu.SemaphoreType.DMA((9,)),
        ],
        compiler_params=limit(VMEM_MIB),
        name="backward_solve",
    )(places, returned, interface, factors, edge_y, spectrum, y_table, z_full, more_pairs)
    pair_force = pair_part(7 * eighth, eighth, more_pairs)
    return potential, values, pair_force


def shifted(block, axis, step):
    count = lax.axis_size(axis)
    return lax.ppermute(block, axis, [(i, (i + step) % count) for i in range(count)])


def body(
    qm_density,
    mm_coords,
    mm_charge,
    mm_types,
    type_radius,
    mm_cells,
    block_counts,
    block_owner,
    neighbour_tiles,
):
    n_blocks = block_counts.shape[2]
    tile_atoms = mm_charge.shape[2]
    block_atoms = tile_atoms // n_blocks
    x_local, local_y_rows, grid_len = qm_density.shape
    n_gx = lax.axis_size("gx")
    plan = Plan(x_local, local_y_rows, grid_len, n_gx, lax.axis_size("gy"))
    copies, atom_rows = pl.pallas_call(
        functools.partial(prepare_kernel, plan, n_blocks, block_atoms),
        out_shape=(shaped(n_gx * n_blocks, 128), shaped(1, 5, tile_atoms)),
        in_specs=[SMEM] * 3 + [VMEM] * 4,
        out_specs=(VMEM, VMEM),
        scratch_shapes=[buffer(n_blocks, 128)],
        compiler_params=limit(VMEM_MIB),
        name="prepare_atoms",
    )(
        block_counts.reshape(1, n_blocks),
        block_owner.reshape(1, n_blocks),
        type_radius,
        mm_coords.transpose(0, 2, 1, 3),
        mm_charge,
        mm_types,
        mm_cells,
    )
    codes = lax.all_to_all(copies, "gx", split_axis=0, concat_axis=0, tiled=True)
    first_code = (lax.axis_index("gx") * plan.span).astype(jnp.int32).reshape(1)
    triple = jnp.concatenate(
        [shifted(atom_rows, "gx", 1), atom_rows, shifted(atom_rows, "gx", -1)], axis=0
    )
    below, above = shifted(triple, "gy", 1), shifted(triple, "gy", -1)
    listed = neighbour_tiles.shape[3]
    listing = neighbour_tiles.transpose(0, 3, 1, 2)

    def pair_part(first, part_atoms, earlier):
        if earlier is None:
            earlier = jnp.zeros((3, 1, 128), jnp.float32)
        return pl.pallas_call(
            functools.partial(pair_kernel, n_blocks, block_atoms, listed, first, part_atoms),
            out_shape=shaped(3, 1, first + part_atoms),
            in_specs=[SMEM] + [VMEM] * 4,
            out_specs=VMEM,
            scratch_shapes=[
                buffer(9, 5, 8, tile_atoms),
                buffer(128, part_atoms),
                buffer(part_atoms, 128),
            ],
            compiler_params=limit(VMEM_MIB),
            cost_estimate=pl.CostEstimate(
                flops=21 * listed * tile_atoms * part_atoms,
                bytes_accessed=4 * 50 * tile_atoms,
                transcendentals=listed * tile_atoms * part_atoms,
            ),
            name="pair_forces",
        )(listing, below, triple, above, earlier)

    potential, values, pair_force = solve_poisson(
        plan, qm_density, codes, first_code, n_blocks, block_atoms, (below, above), pair_part
    )
    values = lax.all_to_all(values, "gx", split_axis=0, concat_axis=0, tiled=True)
    sampled = jnp.sum(values.reshape(n_gx, n_blocks, 128), axis=0)[:, :block_atoms]
    lanes = jnp.arange(block_atoms, dtype=jnp.int32)
    live = lanes[None, :] < block_counts.reshape(n_blocks, 1)
    mm_potential = jnp.where(live, sampled, 0.0).reshape(1, 1, tile_atoms)
    return (potential, mm_potential, pair_force[None].transpose(0, 2, 1, 3))


def solution(mesh):
    placed = (
        P("gx", "gy", None),
        P("gx", "gy", None, None),
        P("gx", "gy", None),
        P("gx", "gy", None),
        P(),
        P("gx", "gy", None),
        P("gx", "gy", None),
        P("gx", "gy", None, None),
        P("gx", "gy", None, None),
    )
    return jax.shard_map(
        body,
        mesh=mesh,
        in_specs=placed,
        out_specs=(P("gx", "gy", None), P("gx", "gy", None), P("gx", "gy", None, None)),
        check_vma=False,
    )
```

```python
import functools

import jax
import jax.numpy as jnp
import ml_dtypes
import numpy as np
from jax import lax
from jax.experimental import pallas as pl
from jax.experimental.pallas import tpu as pltpu
from jax.sharding import PartitionSpec as P

SCREENING = 0.003
HIGH_ACCURACY = lax.Precision.HIGHEST
VMEM_MIB = 60
BATCH = 16
MIB = 1024 * 1024


def round_up(value, unit):
    return -(-value // unit) * unit


def sine_matrix(length):
    nodes = np.arange(length, dtype=np.float64)
    return np.sqrt(2.0 / length) * np.sin(np.pi * np.outer(nodes, nodes) / length)


def cas_matrix(length):
    nodes = np.arange(length)
    angle = 2.0 * np.pi * (np.outer(nodes, nodes) % length) / length
    return np.cos(angle) + np.sin(angle)


def stiffness(count, length):
    return 4.0 * np.sin(np.pi * np.arange(count) / length) ** 2


def split_pair(matrix):
    full = np.asarray(matrix, np.float32)
    high = full.astype(ml_dtypes.bfloat16)
    low = (full - high.astype(np.float32)).astype(ml_dtypes.bfloat16)
    return high, low


def table_triple(matrix, axis):
    high, low = split_pair(matrix)
    return np.concatenate([high, low, high], axis=axis)


def f32(table):
    return np.asarray(table, np.float32)


class Plan:
    def __init__(self, x_len, y_len, grid, n_gx, n_gy):
        self.x_len, self.y_len, self.grid = x_len, y_len, grid
        self.n_gx, self.n_gy = n_gx, n_gy
        self.y_pad = round_up(y_len, 8)
        self.x_pad = round_up(x_len, 8)
        self.lanes = round_up(grid, 128)
        self.lane_tiles = self.lanes // 128
        self.planes = x_len * self.y_pad
        self.span = self.lane_tiles * self.planes * 128
        self.parts = n_gx * n_gy
        self.modes = -(-grid // self.parts)
        self.half = round_up(y_len + x_len, 128)
        self.kx_pad = round_up(n_gx, 8)
        self.j_pad = round_up(n_gy, 8)
        self.stack_rows = round_up(3 * self.y_pad + 2 * self.x_pad, 128)

    def y_matrix(self):
        out = np.zeros((self.y_pad, self.y_pad))
        out[: self.y_len, : self.y_len] = sine_matrix(self.y_len)
        return out

    def z_matrix(self):
        out = np.zeros((self.lanes, self.lanes))
        out[: self.grid, : self.grid] = cas_matrix(self.grid) / np.sqrt(self.grid)
        return out

    def elimination_factors(self):
        z_part = np.zeros(self.lanes)
        z_part[: self.grid] = stiffness(self.grid, self.grid)
        y_part = stiffness(self.y_pad, 2 * self.y_len)
        diagonal = 2.0 + y_part[:, None] + z_part[None, :] + SCREENING
        out = np.zeros((self.x_len, self.y_pad, self.lanes))
        for x in range(1, self.x_len):
            out[x] = 1.0 / (diagonal - out[x - 1])
        return out

    def edge_weights(self):
        sine_y = self.y_matrix()
        both = np.stack([sine_y[1], sine_y[self.y_len - 1]])
        return np.broadcast_to(both[:, :, None], (2, self.y_pad, 128))

    def interface_table(self):
        x_len, y_len, half = self.x_len, self.y_len, self.half
        y_pad, x_pad = self.y_pad, self.x_pad
        sine_y = sine_matrix(y_len)
        out = np.zeros((self.stack_rows, 2 * half))
        out[:y_len, :y_len] = sine_y
        row = y_pad
        out[row : row + y_len, half : half + y_len] = sine_y
        row += y_pad
        out[row : row + y_len, :y_len] = np.eye(y_len)
        row += y_pad
        out[row + 1 : row + x_len, y_len + 1 : y_len + x_len] = np.eye(x_len - 1)
        row += x_pad
        far = half + y_len
        out[row + 1 : row + x_len, far + 1 : far + x_len] = np.eye(x_len - 1)
        return out

    def gather_table(self):
        n_gx, n_gy, parts = self.n_gx, self.n_gy, self.parts
        cas_x = cas_matrix(n_gx)
        out = np.zeros((n_gy * self.kx_pad + n_gx * self.j_pad, 2 * parts))
        for i in range(n_gx):
            for j in range(n_gy):
                col = i * n_gy + j
                base = j * self.kx_pad
                out[base : base + n_gx, col] = cas_x[:, i]
                out[base : base + n_gx, parts + col] = cas_x[:, (i + 1) % n_gx]
                base = n_gy * self.kx_pad + i * self.j_pad
                out[base + j, col] = 1.0
                out[base + (j + 1) % n_gy, parts + col] = 1.0
        return out

    def line_tables(self):
        scaled = cas_matrix(self.grid) / np.sqrt(self.grid)
        along_y = np.zeros((self.n_gy, self.half, self.lanes))
        along_x = np.zeros((self.n_gx, self.half, self.lanes))
        y_len, x_len, grid = self.y_len, self.x_len, self.grid
        for j in range(self.n_gy):
            along_y[j, :y_len, :grid] = scaled[j * y_len : (j + 1) * y_len]
        for i in range(self.n_gx):
            along_x[i, y_len : y_len + x_len, :grid] = scaled[i * x_len : (i + 1) * x_len]
        return along_y.reshape(-1, self.lanes), along_x.reshape(-1, self.lanes)

    def expand_table(self):
        ratio = self.grid // self.n_gy
        full = cas_matrix(self.grid)
        out = np.zeros((self.j_pad, self.lanes))
        for j in range(self.n_gy):
            out[j, : self.grid] = full[(j * ratio) % self.grid]
        return np.where(np.abs(out - np.round(out)) < 1e-9, np.round(out), out)


def dot(a, b, dims=((1,), (0,)), precision=None):
    return lax.dot_general(
        a, b, (dims, ((), ())), precision=precision, preferred_element_type=jnp.float32
    )


def value_parts(value, axis, count):
    high = value.astype(jnp.bfloat16).astype(jnp.float32)
    return jnp.concatenate([high] * (count - 1) + [value - high], axis=axis)


def table_parts(matrix, axis):
    high, low = split_pair(matrix)
    if low.astype(np.float32).any():
        return np.concatenate([high, low, high], axis=axis)
    return np.concatenate([high, high], axis=axis)


def value_triple(value, axis):
    high = value.astype(jnp.bfloat16).astype(jnp.float32)
    return jnp.concatenate([high, high, value - high], axis=axis).astype(jnp.bfloat16)


def split_table(source, target, axis):
    value = source[...]
    high = value.astype(jnp.bfloat16).astype(jnp.float32)
    parts = jnp.concatenate([high, value - high, high], axis=axis)
    target[...] = parts.astype(jnp.bfloat16)


def left_apply(table, value):
    return dot(table, value_triple(value, 0))


def right_apply(value, table):
    return dot(value_triple(value, 1), table)


def slab_count(plan):
    if plan.y_pad != plan.y_len:
        return 1
    return max(count for count in (4, 3, 2, 1) if plan.x_len % count == 0)


def inverse(value):
    guess = pl.reciprocal(value, approx=True)
    guess = guess * (2.0 - value * guess)
    return guess * (2.0 - value * guess)


def start_copies(pairs, sems):
    copies = [
        pltpu.make_async_copy(source, target, sems.at[k])
        for k, (source, target) in enumerate(pairs)
    ]
    for copy in copies:
        copy.start()
    return copies


def list_owned(plan, places, blocks, block_count):
    def several(step, count):
        for k in range(8):
            number = step * 8 + k
            lead = places[number, 0]
            blocks[count] = number
            count = count + jnp.where((lead >= 0) & (lead < plan.span), 1, 0)
        return count

    return lax.fori_loop(0, block_count // 8, several, 0)


def chunked_loop(count, unroll, body, init):
    while count % unroll:
        unroll -= 1

    def group(step, carry):
        for k in range(unroll):
            carry = body(step * unroll + k, carry)
        return carry

    return lax.fori_loop(0, count // unroll, group, init)


def mark_places(codes, first_code, place_rows, block_atoms):
    lane = lax.broadcasted_iota(jnp.int32, codes.shape, 1)
    code = codes[...].astype(jnp.int32) - first_code
    place = lax.shift_right_arithmetic(code, 7)
    shared = jnp.zeros_like(place)
    for step in range(1, BATCH):
        same = (pltpu.roll(place, step, 1) == place) & (lane % BATCH >= step)
        shared = jnp.where(same & (lane < block_atoms), 1, shared)
    step = block_atoms // 2
    while step:
        shared = shared | pltpu.roll(shared, 128 - step, 1)
        step //= 2
    mark = pltpu.roll(shared, block_atoms, 1)
    place_rows[...] = jnp.where(lane == block_atoms, mark, code)


def forward_kernel(
    plan,
    n_blocks,
    block_atoms,
    first_code,
    *refs,
):
    (
        codes_hbm,
        density_hbm,
        z_full_hbm,
        y_table_hbm,
        factors_hbm,
        edge_y_hbm,
        interface_hbm,
        _,
        spectrum_hbm,
        places_hbm,
        message,
        added,
        solved,
        stack,
        heads,
        edge_rows,
        turned,
        codes,
        density,
        z_full,
        z_table,
        y_table,
        factors,
        edge_y,
        interface_full,
        interface,
        spectrum,
        place_rows,
        places,
        blocks,
        sems,
        *charges,
    ) = refs
    x_len, y_len, y_pad, x_pad = plan.x_len, plan.y_len, plan.y_pad, plan.x_pad
    grid, lane_count, planes = plan.grid, plan.lanes, plan.planes
    slabs = slab_count(plan)
    lane_ids = lax.broadcasted_iota(jnp.int32, (1, 128), 1)
    loads = start_copies(
        [
            (codes_hbm, codes),
            (density_hbm, density),
            (z_full_hbm, z_full),
            (y_table_hbm, y_table),
            (factors_hbm, factors),
            (edge_y_hbm, edge_y),
            (interface_hbm, interface_full),
        ],
        sems,
    )
    loads[0].wait()
    charge_copies = [pltpu.make_async_copy(codes, target, sems.at[7]) for target in charges]
    for copy in charge_copies:
        copy.start()
    mark_places(codes, first_code[0], place_rows, block_atoms)
    place_copies = [
        pltpu.make_async_copy(place_rows, places, sems.at[8]),
        pltpu.make_async_copy(place_rows, places_hbm, sems.at[9]),
    ]
    for copy in place_copies:
        copy.start()

    def clear(step, carry):
        place = pl.ds(pl.multiple_of(step * y_pad, 8), y_pad)
        added[place, :] = jnp.zeros((y_pad, 128), jnp.float32)
        return carry

    chunked_loop(plan.lane_tiles * x_len, 4, clear, 0)
    loads[2].wait()
    split_table(z_full, z_table, 0)
    for copy in [*charge_copies, place_copies[0]]:
        copy.wait()
    count = list_owned(plan, places, blocks, plan.n_gx * n_blocks)

    def deposit(slot, carry):
        block = blocks[slot]
        row_codes = places.at[block]
        charge_row = charges[0].at[block] if charges else codes[pl.ds(block, 1), :]

        def raised(code, k):
            lane = block_atoms + k
            charge = charge_row[lane] if charges else charge_row[:, lane : lane + 1]
            hit = jnp.where(lane_ids == (code & 127), charge, 0.0)
            return added[pl.ds(lax.shift_right_logical(code, 7), 1), :] + hit

        @pl.when(row_codes[block_atoms] == 0)
        def _():
            for start in range(0, block_atoms, BATCH):
                local = [row_codes[start + k] for k in range(BATCH)]
                rows = [raised(code, start + k) for k, code in enumerate(local)]
                for code, row in zip(local, rows):
                    added[pl.ds(lax.shift_right_logical(code, 7), 1), :] = row

        @pl.when(row_codes[block_atoms] != 0)
        def _():
            for k in range(block_atoms):
                code = row_codes[k]
                row = raised(code, k)
                added[pl.ds(lax.shift_right_logical(code, 7), 1), :] = row

        return carry

    lax.fori_loop(0, count, deposit, 0)
    loads[1].wait()
    loads[3].wait()

    def transform(step, carry):
        start = step * slabs
        count = slabs * y_pad
        pieces = []
        for tile in range(plan.lane_tiles):
            low = tile * 128
            width = min(128, grid - low)
            piece = density.at[pl.ds(start, slabs)][:, :, low : low + width]
            if y_pad == y_len:
                piece = piece.reshape(count, width)
            else:
                rows = jnp.zeros((y_pad - y_len, width), jnp.float32)
                piece = jnp.concatenate([piece[0], rows], axis=0)
            if width < 128:
                rest = jnp.zeros((count, 128 - width), jnp.float32)
                piece = jnp.concatenate([piece, rest], axis=1)
            place = pl.ds(pl.multiple_of(tile * planes + start * y_pad, 8), count)
            pieces.append(piece + added.at[place][...])
        lines = right_apply(jnp.concatenate(pieces, axis=1), z_table[...])
        lines = lines.reshape(slabs, y_pad, lane_count)
        for slab in range(slabs):
            x = start + slab
            for tile in range(plan.lane_tiles):
                heads[tile, pl.ds(x, 1), :] = lines[slab, 0:1, tile * 128 : tile * 128 + 128]
            spectrum.at[x][...] = left_apply(y_table[...], lines[slab])

        @pl.when(step == 0)
        def _():
            stack[2 * y_pad : 3 * y_pad, :] = lines[0]

        return carry

    chunked_loop(x_len // slabs, 3, transform, 0)
    spectrum_copy = pltpu.make_async_copy(spectrum, spectrum_hbm, sems.at[10])
    spectrum_copy.start()
    for copy in loads[4:]:
        copy.wait()
    split_table(interface_full, interface, 0)
    stack[3 * y_pad :, :] = jnp.zeros((stack.shape[0] - 3 * y_pad, lane_count), jnp.float32)
    for tile in range(plan.lane_tiles):
        lanes = slice(tile * 128, tile * 128 + 128)
        near_weight = edge_y[0]
        far_weight = edge_y[1]

        def eliminate(step, carry):
            x = step + 1
            value = (spectrum.at[x][:, lanes] + carry) * factors.at[x][:, lanes]
            solved.at[x][...] = value
            return value

        def substitute(step, value):
            x = x_len - 1 - step
            value = solved.at[x][...] + factors.at[x][:, lanes] * value
            near_row = jnp.sum(value * near_weight, axis=0, keepdims=True)
            far_row = jnp.sum(value * far_weight, axis=0, keepdims=True)
            edge_rows[0, pl.ds(x, 1), :] = near_row + heads[tile, pl.ds(x, 1), :]
            edge_rows[1, pl.ds(x, 1), :] = far_row
            return value

        zero = jnp.zeros((y_pad, 128), jnp.float32)
        chunked_loop(x_len - 1, 5, eliminate, zero)
        stack[y_pad : 2 * y_pad, lanes] = solved[x_len - 1]
        stack[0:y_pad, lanes] = chunked_loop(x_len - 1, 5, substitute, zero)
        for side in range(2):
            row = 3 * y_pad + side * x_pad
            stack[row + 1 : row + x_len, lanes] = edge_rows[side, 1:x_len, :]
    turned[...] = right_apply(jnp.transpose(stack[...]), interface[...])
    total = plan.parts * plan.modes
    for mode in range(grid):
        message[mode] = turned[mode : mode + 1, :]
    if total > grid:
        message[grid:total] = jnp.zeros((total - grid, 1, 2 * plan.half), jnp.float32)
    spectrum_copy.wait()
    place_copies[1].wait()


def interface_kernel(
    plan,
    first_mode,
    stiff_z,
    _,
    incoming_hbm,
    gather_hbm,
    along_y_hbm,
    along_x_hbm,
    expand_hbm,
    expand_back_hbm,
    stiff_x_hbm,
    stiff_y_hbm,
    scatter_hbm,
    outgoing,
    rows,
    folded_y,
    folded_x,
    lines,
    incoming,
    gather,
    along_y_full,
    along_x_full,
    expand,
    expand_back,
    stiff_x,
    stiff_y,
    scatter,
    along_y,
    along_x,
    along_y_back,
    along_x_back,
    sems,
):
    loads = start_copies(
        [
            (incoming_hbm, incoming),
            (gather_hbm, gather),
            (along_y_hbm, along_y_full),
            (along_x_hbm, along_x_full),
            (expand_hbm, expand),
            (expand_back_hbm, expand_back),
            (stiff_x_hbm, stiff_x),
            (stiff_y_hbm, stiff_y),
            (scatter_hbm, scatter),
        ],
        sems,
    )
    grid, half, parts, modes = plan.grid, plan.half, plan.parts, plan.modes
    kx_pad, j_pad, n_gx, n_gy = plan.kx_pad, plan.j_pad, plan.n_gx, plan.n_gy
    lane_count = plan.lanes
    groups = grid // n_gx

    def collect(source, carry):
        for mode in range(modes):
            both = incoming.at[source * modes + mode][...]
            rows[mode, pl.ds(source, 1), :] = both[:, :half]
            rows[mode, pl.ds(parts + source, 1), :] = both[:, half:]
        return carry

    loads[0].wait()
    lax.fori_loop(0, parts, collect, 0)
    loads[1].wait()
    for mode in range(modes):
        lines[mode] = left_apply(gather[...], rows[mode])
    base = n_gy * kx_pad
    y_slots = [slice(j * kx_pad, (j + 1) * kx_pad) for j in range(n_gy)]
    x_slots = [slice(base + i * j_pad, base + (i + 1) * j_pad) for i in range(n_gx)]

    def side_by_side(slots, count):
        return jnp.concatenate(
            [lines[:, slot, :].reshape(modes * count, half) for slot in slots], axis=1
        )

    loads[2].wait()
    split_table(along_y_full, along_y, 0)
    loads[3].wait()
    split_table(along_x_full, along_x, 0)
    folded_y[...] = right_apply(side_by_side(y_slots, kx_pad), along_y[...]).reshape(
        modes, kx_pad, lane_count
    )
    folded_x[...] = right_apply(side_by_side(x_slots, j_pad), along_x[...]).reshape(
        modes, j_pad, lane_count
    )

    def solve(mode, carry):
        across = value_parts(folded_x[mode, :, :grid], 0, expand.shape[0] // j_pad)
        spread = dot(across, expand[...], ((0,), (0,)))
        number = spread.reshape(groups, kx_pad, lane_count) + folded_y[mode][None]
        bottom = stiff_x[...] + (stiff_y[...] + stiff_z[first_mode[0] + mode])
        value = number * inverse(bottom).reshape(groups, kx_pad, lane_count)
        folded_y[mode] = jnp.sum(value, axis=0)
        value = value_parts(value.reshape(grid, lane_count), 1, expand.shape[0] // j_pad)
        value = value.astype(jnp.bfloat16)
        folded_x[mode, :, :grid] = dot(expand_back[...], value, ((1,), (1,)))
        return carry

    for copy in loads[4:8]:
        copy.wait()
    chunked_loop(modes, 3, solve, 0)
    loads[8].wait()
    split_table(along_y_full, along_y_back, 1)
    split_table(along_x_full, along_x_back, 1)
    all_y = folded_y[...].reshape(modes * kx_pad, lane_count)
    all_y = dot(value_triple(all_y, 1), along_y_back[...], ((1,), (1,)))
    for j, slot in enumerate(y_slots):
        lines[:, slot, :] = all_y[:, j * half : (j + 1) * half].reshape(modes, kx_pad, half)
    all_x = folded_x[...].reshape(modes * j_pad, lane_count)
    all_x = dot(value_triple(all_x, 1), along_x_back[...], ((1,), (1,)))
    for i, slot in enumerate(x_slots):
        lines[:, slot, :] = all_x[:, i * half : (i + 1) * half].reshape(modes, j_pad, half)
    for mode in range(modes):
        rows[mode] = left_apply(scatter[...], lines[mode])

    def distribute(target, carry):
        for mode in range(modes):
            outgoing[target * modes + mode, :, :half] = rows[mode, pl.ds(target, 1), :]
            outgoing[target * modes + mode, :, half:] = rows[mode, pl.ds(parts + target, 1), :]
        return carry

    lax.fori_loop(0, parts, distribute, 0)


def backward_kernel(
    plan,
    n_blocks,
    block_atoms,
    places_hbm,
    message_hbm,
    interface_hbm,
    factors_hbm,
    edge_y_hbm,
    spectrum_hbm,
    y_table_hbm,
    z_full_hbm,
    _,
    potential_hbm,
    values,
    lookup,
    work,
    solved,
    stack,
    heads,
    edge_rows,
    turned,
    picked,
    potential,
    places,
    message,
    interface_full,
    interface,
    factors,
    edge_y,
    spectrum,
    y_table,
    z_full,
    z_table,
    blocks,
    sems,
):
    x_len, y_len, y_pad, x_pad = plan.x_len, plan.y_len, plan.y_pad, plan.x_pad
    grid, lane_count, planes = plan.grid, plan.lanes, plan.planes
    slabs = slab_count(plan)
    loads = start_copies(
        [
            (message_hbm, message),
            (interface_hbm, interface_full),
            (places_hbm, places),
            (factors_hbm, factors),
            (edge_y_hbm, edge_y),
            (spectrum_hbm, spectrum),
            (y_table_hbm, y_table),
            (z_full_hbm, z_full),
        ],
        sems,
    )
    loads[0].wait()
    for mode in range(grid):
        turned[mode : mode + 1, :] = message[mode]
    if lane_count > grid:
        turned[grid:, :] = jnp.zeros((lane_count - grid, turned.shape[1]), jnp.float32)
    loads[1].wait()
    split_table(interface_full, interface, 1)
    stack[...] = dot(interface[...], value_triple(turned[...], 1), ((1,), (1,)))
    loads[2].wait()
    count = list_owned(plan, places, blocks, plan.n_gx * n_blocks)
    for copy in loads[3:]:
        copy.wait()
    split_table(z_full, z_table, 0)
    for tile in range(plan.lane_tiles):
        lanes = slice(tile * 128, tile * 128 + 128)
        near_weight = edge_y[0]
        far_weight = edge_y[1]
        heads[tile] = stack[3 * y_pad : 3 * y_pad + x_pad, lanes]
        edge_rows[...] = stack[3 * y_pad + x_pad : 3 * y_pad + 2 * x_pad, lanes]

        def eliminate(step, carry):
            x = step + 1
            load = spectrum.at[x][:, lanes] + near_weight * heads[tile, pl.ds(x, 1), :]
            load = load + far_weight * edge_rows[pl.ds(x, 1), :]
            value = (load + carry) * factors.at[x][:, lanes]
            solved.at[x][...] = value
            return value

        def substitute(step, value):
            x = x_len - 1 - step
            value = solved.at[x][...] + factors.at[x][:, lanes] * value
            work.at[x][:, lanes] = value
            return value

        chunked_loop(x_len - 1, 5, eliminate, stack[0:y_pad, lanes])
        chunked_loop(x_len - 1, 5, substitute, stack[y_pad : 2 * y_pad, lanes])
    work[0] = jnp.zeros((y_pad, lane_count), jnp.float32)

    def transform(step, carry):
        start = step * slabs
        for slab in range(slabs):
            x = start + slab
            slab_work = work.at[x]
            slab_work[...] = left_apply(y_table[...], slab_work[...])
            for tile in range(plan.lane_tiles):
                lanes = slice(tile * 128, tile * 128 + 128)
                slab_work[0:1, lanes] = heads[tile, pl.ds(x, 1), :]

        @pl.when(step == 0)
        def _():
            work[0] = stack[2 * y_pad : 3 * y_pad, :]

        lines = work.at[pl.ds(start, slabs)][...].reshape(slabs * y_pad, lane_count)
        lines = right_apply(lines, z_table[...])
        for tile in range(plan.lane_tiles):
            low = tile * 128
            place = pl.ds(pl.multiple_of(tile * planes + start * y_pad, 8), slabs * y_pad)
            lookup.at[place][...] = lines[:, low : low + 128]
        lines = lines.reshape(slabs, y_pad, lane_count)
        potential.at[pl.ds(start, slabs)][...] = lines[:, :y_len, :grid]
        return carry

    chunked_loop(x_len // slabs, 3, transform, 0)
    potential_copy = pltpu.make_async_copy(potential, potential_hbm, sems.at[8])
    potential_copy.start()
    values[...] = jnp.zeros(values.shape, jnp.float32)
    lane_ids = lax.broadcasted_iota(jnp.int32, (1, 128), 1)
    shape = (block_atoms, 128)
    own_lane = lax.broadcasted_iota(jnp.int32, shape, 0) == lax.broadcasted_iota(
        jnp.int32, shape, 1
    )

    def reduce_rows(rows, block):
        found = jnp.sum(rows, axis=1, keepdims=True)
        found = jnp.sum(jnp.where(own_lane, found, 0.0), axis=0, keepdims=True)
        values[pl.ds(block, 1), :] = found

    def sample(slot, before):
        block = blocks[slot]
        row_codes = places.at[block]
        rows_before = picked[...]
        for first in range(0, block_atoms, 16):
            rows = []
            for atom in range(first, first + 16):
                code = row_codes[atom]
                row = lookup[pl.ds(lax.shift_right_logical(code, 7), 1), :]
                rows.append(jnp.where(lane_ids == (code & 127), row, 0.0))
            for k in range(16):
                picked[first + k : first + k + 1, :] = rows[k]
        reduce_rows(rows_before, before)
        return block

    picked[...] = jnp.zeros(picked.shape, jnp.float32)
    last = lax.fori_loop(0, count, sample, blocks[0])

    @pl.when(count > 0)
    def _():
        reduce_rows(picked[...], last)

    potential_copy.wait()


def prepare_kernel(
    plan, n_blocks, block_atoms, counts, owners, type_radius, coords, charge, types, cells,
    copies, atom_rows, payload,
):
    tile_atoms = n_blocks * block_atoms
    lane = lax.broadcasted_iota(jnp.int32, (1, 128), 1)
    slot = lane // block_atoms
    atom = lane - slot * block_atoms
    per_row = 128 // block_atoms
    for start in range(0, tile_atoms, 128):
        lanes = slice(start, start + 128)
        first = start // block_atoms
        count = jnp.full((1, 128), counts[0, first], jnp.int32)
        owner = jnp.full((1, 128), owners[0, first], jnp.int32)
        for k in range(1, per_row):
            count = jnp.where(slot >= k, counts[0, first + k], count)
            owner = jnp.where(slot >= k, owners[0, first + k], owner)
        live = jnp.where(atom < count, charge[0, :, lanes], 0.0)
        cell = cells[0, :, lanes]
        line = jnp.floor((cell.astype(jnp.float32) + 0.5) * (1.0 / plan.grid)).astype(jnp.int32)
        depth = cell - line * plan.grid
        x = jnp.floor((line.astype(jnp.float32) + 0.5) * (1.0 / plan.y_len)).astype(jnp.int32)
        plane = x * plan.y_pad + (line - x * plan.y_len)
        code = ((depth >> 7) * plan.planes + plane) * 128 + (depth & 127)
        code = (owner * plan.span + code).astype(jnp.float32)
        for k in range(per_row):
            shift = k * block_atoms
            row = pltpu.roll(code, (128 - shift) % 128, 1)
            charges = pltpu.roll(live, (128 + block_atoms - shift) % 128, 1)
            row = jnp.where(lane < block_atoms, row, charges)
            payload[first + k : first + k + 1, :] = jnp.where(lane < 2 * block_atoms, row, 0.0)
        radius = jnp.zeros((1, 128), jnp.float32)
        for kind in range(type_radius.shape[0]):
            radius = jnp.where(types[0, :, lanes] == kind, type_radius[kind], radius)
        atom_rows[0, 0:3, lanes] = coords[0, :, 0, lanes]
        atom_rows[0, 3:4, lanes] = live
        atom_rows[0, 4:5, lanes] = radius
    for target in range(plan.n_gx):
        copies[target * n_blocks : (target + 1) * n_blocks, :] = payload[...]


def pair_kernel(
    n_blocks, block_atoms, listed, first, part_atoms, listing, low, middle, high, earlier, forces,
    table, columns, results,
):
    tile_atoms = n_blocks * block_atoms
    sides = (low, middle, high)
    for step_x in range(3):
        for step_y in range(3):
            rows = sides[step_y][step_x]
            shifts = (step_x - 1.0, step_y - 1.0, 0.0, 0.0, 0.0)
            for k in range(5):
                row = rows[k : k + 1, :]
                if shifts[k]:
                    row = row + shifts[k]
                table[step_x * 3 + step_y, k] = jnp.broadcast_to(row, (8, tile_atoms))
    columns[0:5, :] = middle[1, :, first : first + part_atoms]
    columns[5:, :] = jnp.zeros((columns.shape[0] - 5, part_atoms), jnp.float32)
    results[...] = jnp.transpose(columns[...])
    lane_ids = lax.broadcasted_iota(jnp.int32, (block_atoms, 128), 1)
    groups = block_atoms // 8

    def group(number, carry):
        place = pl.ds(pl.multiple_of(number * block_atoms, block_atoms), block_atoms)
        block = first // block_atoms + number
        own = results[place, :]
        mine = [
            jnp.broadcast_to(own[:, k : k + 1], (block_atoms, 128)).reshape(groups, 8, 128)
            for k in (0, 1, 2, 4)
        ]
        force_x = force_y = force_z = jnp.zeros((groups, 8, 128), jnp.float32)
        for slot in range(listed):
            rows = table.at[listing[0, slot, 0, block]]
            for start in range(0, tile_atoms, 128):
                lanes = slice(start, start + 128)
                sep_x = mine[0] - rows[0, :, lanes][None]
                sep_y = mine[1] - rows[1, :, lanes][None]
                sep_z = mine[2] - rows[2, :, lanes][None]
                reach = mine[3] + rows[4, :, lanes][None]
                root = lax.rsqrt(sep_x * sep_x + sep_y * sep_y + sep_z * sep_z + reach * reach)
                strength = rows[3, :, lanes][None] * root * (root * root)
                force_x = force_x + strength * sep_x
                force_y = force_y + strength * sep_y
                force_z = force_z + strength * sep_z
        out = jnp.zeros((block_atoms, 128), jnp.float32)
        for axis, total in enumerate((force_x, force_y, force_z)):
            total = jnp.sum(total.reshape(block_atoms, 128), axis=1, keepdims=True)
            out = jnp.where(lane_ids == axis, own[:, 3:4] * total, out)
        results[place, :] = out
        return carry

    lax.fori_loop(0, part_atoms // block_atoms, group, 0)
    columns[...] = jnp.transpose(results[...])
    if first:
        for axis in range(3):
            forces[axis, :, :first] = earlier[axis, :, :first]
    for axis in range(3):
        forces[axis, :, first : first + part_atoms] = columns[axis : axis + 1, :]


VMEM = pl.BlockSpec(memory_space=pltpu.VMEM)
SMEM = pl.BlockSpec(memory_space=pltpu.SMEM)
HBM = pl.BlockSpec(memory_space=pl.ANY)


def shaped(*shape):
    return jax.ShapeDtypeStruct(shape, jnp.float32)


def buffer(*shape):
    return pltpu.VMEM(shape, jnp.float32)


def like(table):
    return pltpu.VMEM(table.shape, table.dtype)


def limit(mib):
    return pltpu.CompilerParams(vmem_limit_bytes=mib * MIB)


def after(message, others):
    lane = message.shape[2] - len(others)
    marks = jnp.stack([other[0, 0, 0] for other in others]).reshape(1, 1, -1)
    return lax.dynamic_update_slice(message, marks, (0, 0, lane))


def solve_poisson(plan, density, codes, first_code, n_blocks, block_atoms, neighbours, pair_part):
    x_len, y_len, grid = density.shape
    y_pad, x_pad, half, lanes = plan.y_pad, plan.x_pad, plan.half, plan.lanes
    total = plan.parts * plan.modes
    z_full = f32(plan.z_matrix())
    y_table = table_triple(plan.y_matrix(), 1)
    factors = f32(plan.elimination_factors())
    edge_y = f32(plan.edge_weights())
    interface = f32(plan.interface_table())
    bf16 = jnp.bfloat16
    code_shape = codes.shape
    shared = [
        buffer(x_len, y_pad, 128),
        buffer(plan.stack_rows, lanes),
        buffer(plan.lane_tiles, x_pad, 128),
    ]
    spectrum, places, message = pl.pallas_call(
        functools.partial(forward_kernel, plan, n_blocks, block_atoms),
        out_shape=(
            shaped(x_len, y_pad, lanes),
            jax.ShapeDtypeStruct(code_shape, jnp.int32),
            shaped(total, 1, 2 * half),
        ),
        in_specs=[SMEM] + [HBM] * 8,
        out_specs=(HBM, HBM, VMEM),
        scratch_shapes=[buffer(plan.lane_tiles * plan.planes, 128)]
        + shared
        + [
            buffer(2, x_pad, 128),
            buffer(lanes, 2 * half),
            buffer(*code_shape),
            buffer(x_len, y_len, grid),
            like(z_full),
            pltpu.VMEM((3 * lanes, lanes), bf16),
            like(y_table),
            like(factors),
            like(edge_y),
            like(interface),
            pltpu.VMEM((3 * plan.stack_rows, 2 * half), bf16),
            buffer(x_len, y_pad, lanes),
            pltpu.VMEM(code_shape, jnp.int32),
            pltpu.SMEM(code_shape, jnp.int32),
            pltpu.SMEM((code_shape[0],), jnp.int32),
            pltpu.SemaphoreType.DMA((11,)),
        ]
        + [pltpu.SMEM(code_shape, jnp.float32)] * (code_shape[0] <= 512),
        compiler_params=limit(VMEM_MIB),
        name="forward_solve",
    )(first_code, codes, density, z_full, y_table, factors, edge_y, interface, neighbours[0])
    message = after(message, neighbours[1:])
    eighth = n_blocks * block_atoms // 8
    first_pairs = pair_part(0, 4 * eighth, None)
    incoming = lax.all_to_all(message, ("gx", "gy"), split_axis=0, concat_axis=0, tiled=True)
    gather = plan.gather_table()
    along_y, along_x = plan.line_tables()
    expand = plan.expand_table()
    position = lax.axis_index("gx") * plan.n_gy + lax.axis_index("gy")
    first_mode = (position * plan.modes).astype(jnp.int32).reshape(1)
    stiff = stiffness(grid, grid)
    padded_z = np.zeros(total)
    padded_z[:grid] = stiff
    padded_y = np.zeros((1, lanes))
    padded_y[0, :grid] = stiff
    tables = [
        table_triple(gather, 1),
        f32(along_y),
        f32(along_x),
        f32(table_parts(expand, 0)),
        table_parts(expand, 1),
        f32(stiff[:, None] * grid),
        f32(padded_y * grid),
        table_triple(gather.T, 1),
    ]
    outgoing = pl.pallas_call(
        functools.partial(interface_kernel, plan),
        out_shape=shaped(total, 1, 2 * half),
        in_specs=[SMEM] * 2 + [HBM] * 10,
        out_specs=VMEM,
        scratch_shapes=[
            buffer(plan.modes, 2 * plan.parts, half),
            buffer(plan.modes, plan.kx_pad, lanes),
            buffer(plan.modes, plan.j_pad, lanes),
            buffer(plan.modes, gather.shape[0], half),
            buffer(total, 1, 2 * half),
            *[like(table) for table in tables],
            pltpu.VMEM((3 * along_y.shape[0], lanes), bf16),
            pltpu.VMEM((3 * along_x.shape[0], lanes), bf16),
            pltpu.VMEM((along_y.shape[0], 3 * lanes), bf16),
            pltpu.VMEM((along_x.shape[0], 3 * lanes), bf16),
            pltpu.SemaphoreType.DMA((9,)),
        ],
        compiler_params=limit(VMEM_MIB),
        name="interface_solve",
    )(first_mode, f32((padded_z + SCREENING) * grid), first_pairs, incoming, *tables)
    returned = lax.all_to_all(outgoing, ("gx", "gy"), split_axis=0, concat_axis=0, tiled=True)
    more_pairs = pair_part(4 * eighth, 3 * eighth, first_pairs)
    potential, values = pl.pallas_call(
        functools.partial(backward_kernel, plan, n_blocks, block_atoms),
        out_shape=(shaped(x_len, y_len, grid), shaped(plan.n_gx * n_blocks, 128)),
        in_specs=[HBM] * 9,
        out_specs=(HBM, VMEM),
        scratch_shapes=[
            buffer(plan.lane_tiles * plan.planes, 128),
            buffer(x_len, y_pad, lanes),
        ]
        + shared
        + [
            buffer(x_pad, 128),
            buffer(lanes, 2 * half),
            buffer(block_atoms, 128),
            buffer(x_len, y_len, grid),
            pltpu.SMEM(code_shape, jnp.int32),
            buffer(total, 1, 2 * half),
            like(interface),
            pltpu.VMEM((plan.stack_rows, 6 * half), bf16),
            like(factors),
            like(edge_y),
            buffer(x_len, y_pad, lanes),
            like(y_table),
            like(z_full),
            pltpu.VMEM((3 * lanes, lanes), bf16),
            pltpu.SMEM((code_shape[0],), jnp.int32),
            pltpu.SemaphoreType.DMA((9,)),
        ],
        compiler_params=limit(VMEM_MIB),
        name="backward_solve",
    )(places, returned, interface, factors, edge_y, spectrum, y_table, z_full, more_pairs)
    pair_force = pair_part(7 * eighth, eighth, more_pairs)
    return potential, values, pair_force


def shifted(block, axis, step):
    count = lax.axis_size(axis)
    return lax.ppermute(block, axis, [(i, (i + step) % count) for i in range(count)])


def body(
    qm_density,
    mm_coords,
    mm_charge,
    mm_types,
    type_radius,
    mm_cells,
    block_counts,
    block_owner,
    neighbour_tiles,
):
    n_blocks = block_counts.shape[2]
    tile_atoms = mm_charge.shape[2]
    block_atoms = tile_atoms // n_blocks
    x_local, local_y_rows, grid_len = qm_density.shape
    n_gx = lax.axis_size("gx")
    plan = Plan(x_local, local_y_rows, grid_len, n_gx, lax.axis_size("gy"))
    copies, atom_rows = pl.pallas_call(
        functools.partial(prepare_kernel, plan, n_blocks, block_atoms),
        out_shape=(shaped(n_gx * n_blocks, 128), shaped(1, 5, tile_atoms)),
        in_specs=[SMEM] * 3 + [VMEM] * 4,
        out_specs=(VMEM, VMEM),
        scratch_shapes=[buffer(n_blocks, 128)],
        compiler_params=limit(VMEM_MIB),
        name="prepare_atoms",
    )(
        block_counts.reshape(1, n_blocks),
        block_owner.reshape(1, n_blocks),
        type_radius,
        mm_coords.transpose(0, 2, 1, 3),
        mm_charge,
        mm_types,
        mm_cells,
    )
    codes = lax.all_to_all(copies, "gx", split_axis=0, concat_axis=0, tiled=True)
    first_code = (lax.axis_index("gx") * plan.span).astype(jnp.int32).reshape(1)
    triple = jnp.concatenate(
        [shifted(atom_rows, "gx", 1), atom_rows, shifted(atom_rows, "gx", -1)], axis=0
    )
    below, above = shifted(triple, "gy", 1), shifted(triple, "gy", -1)
    listed = neighbour_tiles.shape[3]
    listing = neighbour_tiles.transpose(0, 3, 1, 2)

    def pair_part(first, part_atoms, earlier):
        if earlier is None:
            earlier = jnp.zeros((3, 1, 128), jnp.float32)
        return pl.pallas_call(
            functools.partial(pair_kernel, n_blocks, block_atoms, listed, first, part_atoms),
            out_shape=shaped(3, 1, first + part_atoms),
            in_specs=[SMEM] + [VMEM] * 4,
            out_specs=VMEM,
            scratch_shapes=[
                buffer(9, 5, 8, tile_atoms),
                buffer(128, part_atoms),
                buffer(part_atoms, 128),
            ],
            compiler_params=limit(VMEM_MIB),
            cost_estimate=pl.CostEstimate(
                flops=21 * listed * tile_atoms * part_atoms,
                bytes_accessed=4 * 50 * tile_atoms,
                transcendentals=listed * tile_atoms * part_atoms,
            ),
            name="pair_forces",
        )(listing, below, triple, above, earlier)

    potential, values, pair_force = solve_poisson(
        plan, qm_density, codes, first_code, n_blocks, block_atoms, (triple, below, above), pair_part
    )
    values = lax.all_to_all(values, "gx", split_axis=0, concat_axis=0, tiled=True)
    sampled = jnp.sum(values.reshape(n_gx, n_blocks, 128), axis=0)[:, :block_atoms]
    lanes = jnp.arange(block_atoms, dtype=jnp.int32)
    live = lanes[None, :] < block_counts.reshape(n_blocks, 1)
    mm_potential = jnp.where(live, sampled, 0.0).reshape(1, 1, tile_atoms)
    return (potential, mm_potential, pair_force[None].transpose(0, 2, 1, 3))


def solution(mesh):
    placed = (
        P("gx", "gy", None),
        P("gx", "gy", None, None),
        P("gx", "gy", None),
        P("gx", "gy", None),
        P(),
        P("gx", "gy", None),
        P("gx", "gy", None),
        P("gx", "gy", None, None),
        P("gx", "gy", None, None),
    )
    return jax.shard_map(
        body,
        mesh=mesh,
        in_specs=placed,
        out_specs=(P("gx", "gy", None), P("gx", "gy", None), P("gx", "gy", None, None)),
        check_vma=False,
    )
```

```python
import functools

import jax
import jax.numpy as jnp
import ml_dtypes
import numpy as np
from jax import lax
from jax.experimental import pallas as pl
from jax.experimental.pallas import tpu as pltpu
from jax.sharding import PartitionSpec as P

SCREENING = 0.003
HIGH_ACCURACY = lax.Precision.HIGHEST
VMEM_MIB = 60
BATCH = 16
MIB = 1024 * 1024


def round_up(value, unit):
    return -(-value // unit) * unit


def sine_matrix(length):
    nodes = np.arange(length, dtype=np.float64)
    return np.sqrt(2.0 / length) * np.sin(np.pi * np.outer(nodes, nodes) / length)


def cas_matrix(length):
    nodes = np.arange(length)
    angle = 2.0 * np.pi * (np.outer(nodes, nodes) % length) / length
    return np.cos(angle) + np.sin(angle)


def stiffness(count, length):
    return 4.0 * np.sin(np.pi * np.arange(count) / length) ** 2


def split_pair(matrix):
    full = np.asarray(matrix, np.float32)
    high = full.astype(ml_dtypes.bfloat16)
    low = (full - high.astype(np.float32)).astype(ml_dtypes.bfloat16)
    return high, low


def table_triple(matrix, axis):
    high, low = split_pair(matrix)
    return np.concatenate([high, low, high], axis=axis)


def f32(table):
    return np.asarray(table, np.float32)


class Plan:
    def __init__(self, x_len, y_len, grid, n_gx, n_gy):
        self.x_len, self.y_len, self.grid = x_len, y_len, grid
        self.n_gx, self.n_gy = n_gx, n_gy
        self.y_pad = round_up(y_len, 8)
        self.x_pad = round_up(x_len, 8)
        self.lanes = round_up(grid, 128)
        self.lane_tiles = self.lanes // 128
        self.planes = x_len * self.y_pad
        self.span = self.lane_tiles * self.planes * 128
        self.parts = n_gx * n_gy
        self.modes = -(-grid // self.parts)
        self.half = round_up(y_len + x_len, 128)
        self.kx_pad = round_up(n_gx, 8)
        self.j_pad = round_up(n_gy, 8)
        self.stack_rows = round_up(3 * self.y_pad + 2 * self.x_pad, 128)

    def y_matrix(self):
        out = np.zeros((self.y_pad, self.y_pad))
        out[: self.y_len, : self.y_len] = sine_matrix(self.y_len)
        return out

    def z_matrix(self):
        out = np.zeros((self.lanes, self.lanes))
        out[: self.grid, : self.grid] = cas_matrix(self.grid) / np.sqrt(self.grid)
        return out

    def elimination_factors(self):
        z_part = np.zeros(self.lanes)
        z_part[: self.grid] = stiffness(self.grid, self.grid)
        y_part = stiffness(self.y_pad, 2 * self.y_len)
        diagonal = 2.0 + y_part[:, None] + z_part[None, :] + SCREENING
        out = np.zeros((self.x_len, self.y_pad, self.lanes))
        for x in range(1, self.x_len):
            out[x] = 1.0 / (diagonal - out[x - 1])
        return out

    def edge_weights(self):
        sine_y = self.y_matrix()
        both = np.stack([sine_y[1], sine_y[self.y_len - 1]])
        return np.broadcast_to(both[:, :, None], (2, self.y_pad, 128))

    def interface_table(self):
        x_len, y_len, half = self.x_len, self.y_len, self.half
        y_pad, x_pad = self.y_pad, self.x_pad
        sine_y = sine_matrix(y_len)
        out = np.zeros((self.stack_rows, 2 * half))
        out[:y_len, :y_len] = sine_y
        row = y_pad
        out[row : row + y_len, half : half + y_len] = sine_y
        row += y_pad
        out[row : row + y_len, :y_len] = np.eye(y_len)
        row += y_pad
        out[row + 1 : row + x_len, y_len + 1 : y_len + x_len] = np.eye(x_len - 1)
        row += x_pad
        far = half + y_len
        out[row + 1 : row + x_len, far + 1 : far + x_len] = np.eye(x_len - 1)
        return out

    def gather_table(self):
        n_gx, n_gy, parts = self.n_gx, self.n_gy, self.parts
        cas_x = cas_matrix(n_gx)
        out = np.zeros((n_gy * self.kx_pad + n_gx * self.j_pad, 2 * parts))
        for i in range(n_gx):
            for j in range(n_gy):
                col = i * n_gy + j
                base = j * self.kx_pad
                out[base : base + n_gx, col] = cas_x[:, i]
                out[base : base + n_gx, parts + col] = cas_x[:, (i + 1) % n_gx]
                base = n_gy * self.kx_pad + i * self.j_pad
                out[base + j, col] = 1.0
                out[base + (j + 1) % n_gy, parts + col] = 1.0
        return out

    def line_tables(self):
        scaled = cas_matrix(self.grid) / np.sqrt(self.grid)
        along_y = np.zeros((self.n_gy, self.half, self.lanes))
        along_x = np.zeros((self.n_gx, self.half, self.lanes))
        y_len, x_len, grid = self.y_len, self.x_len, self.grid
        for j in range(self.n_gy):
            along_y[j, :y_len, :grid] = scaled[j * y_len : (j + 1) * y_len]
        for i in range(self.n_gx):
            along_x[i, y_len : y_len + x_len, :grid] = scaled[i * x_len : (i + 1) * x_len]
        return along_y.reshape(-1, self.lanes), along_x.reshape(-1, self.lanes)

    def expand_table(self):
        ratio = self.grid // self.n_gy
        full = cas_matrix(self.grid)
        out = np.zeros((self.j_pad, self.lanes))
        for j in range(self.n_gy):
            out[j, : self.grid] = full[(j * ratio) % self.grid]
        return np.where(np.abs(out - np.round(out)) < 1e-9, np.round(out), out)


def dot(a, b, dims=((1,), (0,)), precision=None):
    return lax.dot_general(
        a, b, (dims, ((), ())), precision=precision, preferred_element_type=jnp.float32
    )


def value_parts(value, axis, count):
    high = value.astype(jnp.bfloat16).astype(jnp.float32)
    return jnp.concatenate([high] * (count - 1) + [value - high], axis=axis)


def table_parts(matrix, axis):
    high, low = split_pair(matrix)
    if low.astype(np.float32).any():
        return np.concatenate([high, low, high], axis=axis)
    return np.concatenate([high, high], axis=axis)


def value_triple(value, axis):
    high = value.astype(jnp.bfloat16).astype(jnp.float32)
    return jnp.concatenate([high, high, value - high], axis=axis).astype(jnp.bfloat16)


def split_table(source, target, axis):
    value = source[...]
    high = value.astype(jnp.bfloat16).astype(jnp.float32)
    parts = jnp.concatenate([high, value - high, high], axis=axis)
    target[...] = parts.astype(jnp.bfloat16)


def left_apply(table, value):
    return dot(table, value_triple(value, 0))


def right_apply(value, table):
    return dot(value_triple(value, 1), table)


def slab_count(plan):
    if plan.y_pad != plan.y_len:
        return 1
    return max(count for count in (4, 3, 2, 1) if plan.x_len % count == 0)


def inverse(value):
    guess = pl.reciprocal(value, approx=True)
    guess = guess * (2.0 - value * guess)
    return guess * (2.0 - value * guess)


def start_copies(pairs, sems):
    copies = [
        pltpu.make_async_copy(source, target, sems.at[k])
        for k, (source, target) in enumerate(pairs)
    ]
    for copy in copies:
        copy.start()
    return copies


def list_owned(plan, places, blocks, block_count):
    def several(step, count):
        for k in range(8):
            number = step * 8 + k
            lead = places[number, 0]
            blocks[count] = number
            count = count + jnp.where((lead >= 0) & (lead < plan.span), 1, 0)
        return count

    return lax.fori_loop(0, block_count // 8, several, 0)


def chunked_loop(count, unroll, body, init):
    while count % unroll:
        unroll -= 1

    def group(step, carry):
        for k in range(unroll):
            carry = body(step * unroll + k, carry)
        return carry

    return lax.fori_loop(0, count // unroll, group, init)


def mark_places(codes, first_code, place_rows, block_atoms):
    lane = lax.broadcasted_iota(jnp.int32, codes.shape, 1)
    code = codes[...].astype(jnp.int32) - first_code
    place = lax.shift_right_arithmetic(code, 7)
    shared = jnp.zeros_like(place)
    for step in range(1, BATCH):
        same = (pltpu.roll(place, step, 1) == place) & (lane % BATCH >= step)
        shared = jnp.where(same & (lane < block_atoms), 1, shared)
    step = block_atoms // 2
    while step:
        shared = shared | pltpu.roll(shared, 128 - step, 1)
        step //= 2
    mark = pltpu.roll(shared, block_atoms, 1)
    place_rows[...] = jnp.where(lane == block_atoms, mark, code)


def forward_kernel(
    plan,
    n_blocks,
    block_atoms,
    first_code,
    *refs,
):
    (
        codes_hbm,
        density_hbm,
        z_full_hbm,
        y_table_hbm,
        factors_hbm,
        edge_y_hbm,
        interface_hbm,
        _,
        spectrum_hbm,
        places_hbm,
        message,
        added,
        solved,
        stack,
        heads,
        edge_rows,
        turned,
        codes,
        density,
        z_full,
        z_table,
        y_table,
        factors,
        edge_y,
        interface_full,
        interface,
        spectrum,
        place_rows,
        places,
        blocks,
        sems,
        *charges,
    ) = refs
    x_len, y_len, y_pad, x_pad = plan.x_len, plan.y_len, plan.y_pad, plan.x_pad
    grid, lane_count, planes = plan.grid, plan.lanes, plan.planes
    slabs = slab_count(plan)
    lane_ids = lax.broadcasted_iota(jnp.int32, (1, 128), 1)
    loads = start_copies(
        [
            (codes_hbm, codes),
            (density_hbm, density),
            (z_full_hbm, z_full),
            (y_table_hbm, y_table),
            (factors_hbm, factors),
            (edge_y_hbm, edge_y),
            (interface_hbm, interface_full),
        ],
        sems,
    )
    loads[0].wait()
    charge_copies = [pltpu.make_async_copy(codes, target, sems.at[7]) for target in charges]
    for copy in charge_copies:
        copy.start()
    mark_places(codes, first_code[0], place_rows, block_atoms)
    place_copies = [
        pltpu.make_async_copy(place_rows, places, sems.at[8]),
        pltpu.make_async_copy(place_rows, places_hbm, sems.at[9]),
    ]
    for copy in place_copies:
        copy.start()

    def clear(step, carry):
        place = pl.ds(pl.multiple_of(step * y_pad, 8), y_pad)
        added[place, :] = jnp.zeros((y_pad, 128), jnp.float32)
        return carry

    chunked_loop(plan.lane_tiles * x_len, 4, clear, 0)
    loads[2].wait()
    split_table(z_full, z_table, 0)
    for copy in [*charge_copies, place_copies[0]]:
        copy.wait()
    count = list_owned(plan, places, blocks, plan.n_gx * n_blocks)

    def deposit(slot, carry):
        block = blocks[slot]
        row_codes = places.at[block]
        charge_row = charges[0].at[block] if charges else codes[pl.ds(block, 1), :]

        def raised(code, k):
            lane = block_atoms + k
            charge = charge_row[lane] if charges else charge_row[:, lane : lane + 1]
            hit = jnp.where(lane_ids == (code & 127), charge, 0.0)
            return added[pl.ds(lax.shift_right_logical(code, 7), 1), :] + hit

        @pl.when(row_codes[block_atoms] == 0)
        def _():
            for start in range(0, block_atoms, BATCH):
                local = [row_codes[start + k] for k in range(BATCH)]
                rows = [raised(code, start + k) for k, code in enumerate(local)]
                for code, row in zip(local, rows):
                    added[pl.ds(lax.shift_right_logical(code, 7), 1), :] = row

        @pl.when(row_codes[block_atoms] != 0)
        def _():
            for k in range(block_atoms):
                code = row_codes[k]
                row = raised(code, k)
                added[pl.ds(lax.shift_right_logical(code, 7), 1), :] = row

        return carry

    lax.fori_loop(0, count, deposit, 0)
    loads[1].wait()
    loads[3].wait()

    def transform(step, carry):
        start = step * slabs
        count = slabs * y_pad
        pieces = []
        for tile in range(plan.lane_tiles):
            low = tile * 128
            width = min(128, grid - low)
            piece = density.at[pl.ds(start, slabs)][:, :, low : low + width]
            if y_pad == y_len:
                piece = piece.reshape(count, width)
            else:
                rows = jnp.zeros((y_pad - y_len, width), jnp.float32)
                piece = jnp.concatenate([piece[0], rows], axis=0)
            if width < 128:
                rest = jnp.zeros((count, 128 - width), jnp.float32)
                piece = jnp.concatenate([piece, rest], axis=1)
            place = pl.ds(pl.multiple_of(tile * planes + start * y_pad, 8), count)
            pieces.append(piece + added.at[place][...])
        lines = right_apply(jnp.concatenate(pieces, axis=1), z_table[...])
        lines = lines.reshape(slabs, y_pad, lane_count)
        for slab in range(slabs):
            x = start + slab
            for tile in range(plan.lane_tiles):
                heads[tile, pl.ds(x, 1), :] = lines[slab, 0:1, tile * 128 : tile * 128 + 128]
            spectrum.at[x][...] = left_apply(y_table[...], lines[slab])

        @pl.when(step == 0)
        def _():
            stack[2 * y_pad : 3 * y_pad, :] = lines[0]

        return carry

    chunked_loop(x_len // slabs, 3, transform, 0)
    spectrum_copy = pltpu.make_async_copy(spectrum, spectrum_hbm, sems.at[10])
    spectrum_copy.start()
    for copy in loads[4:]:
        copy.wait()
    split_table(interface_full, interface, 0)
    stack[3 * y_pad :, :] = jnp.zeros((stack.shape[0] - 3 * y_pad, lane_count), jnp.float32)
    for tile in range(plan.lane_tiles):
        lanes = slice(tile * 128, tile * 128 + 128)
        near_weight = edge_y[0]
        far_weight = edge_y[1]

        def eliminate(step, carry):
            x = step + 1
            value = (spectrum.at[x][:, lanes] + carry) * factors.at[x][:, lanes]
            solved.at[x][...] = value
            return value

        def substitute(step, value):
            x = x_len - 1 - step
            value = solved.at[x][...] + factors.at[x][:, lanes] * value
            near_row = jnp.sum(value * near_weight, axis=0, keepdims=True)
            far_row = jnp.sum(value * far_weight, axis=0, keepdims=True)
            edge_rows[0, pl.ds(x, 1), :] = near_row + heads[tile, pl.ds(x, 1), :]
            edge_rows[1, pl.ds(x, 1), :] = far_row
            return value

        zero = jnp.zeros((y_pad, 128), jnp.float32)
        chunked_loop(x_len - 1, 5, eliminate, zero)
        stack[y_pad : 2 * y_pad, lanes] = solved[x_len - 1]
        stack[0:y_pad, lanes] = chunked_loop(x_len - 1, 5, substitute, zero)
        for side in range(2):
            row = 3 * y_pad + side * x_pad
            stack[row + 1 : row + x_len, lanes] = edge_rows[side, 1:x_len, :]
    turned[...] = right_apply(jnp.transpose(stack[...]), interface[...])
    total = plan.parts * plan.modes
    for mode in range(grid):
        message[mode] = turned[mode : mode + 1, :]
    if total > grid:
        message[grid:total] = jnp.zeros((total - grid, 1, 2 * plan.half), jnp.float32)
    spectrum_copy.wait()
    place_copies[1].wait()


def interface_kernel(
    plan,
    first_mode,
    stiff_z,
    _,
    incoming_hbm,
    gather_hbm,
    along_y_hbm,
    along_x_hbm,
    expand_hbm,
    expand_back_hbm,
    stiff_x_hbm,
    stiff_y_hbm,
    scatter_hbm,
    outgoing,
    rows,
    folded_y,
    folded_x,
    lines,
    incoming,
    gather,
    along_y_full,
    along_x_full,
    expand,
    expand_back,
    stiff_x,
    stiff_y,
    scatter,
    along_y,
    along_x,
    along_y_back,
    along_x_back,
    sems,
):
    loads = start_copies(
        [
            (incoming_hbm, incoming),
            (gather_hbm, gather),
            (along_y_hbm, along_y_full),
            (along_x_hbm, along_x_full),
            (expand_hbm, expand),
            (expand_back_hbm, expand_back),
            (stiff_x_hbm, stiff_x),
            (stiff_y_hbm, stiff_y),
            (scatter_hbm, scatter),
        ],
        sems,
    )
    grid, half, parts, modes = plan.grid, plan.half, plan.parts, plan.modes
    kx_pad, j_pad, n_gx, n_gy = plan.kx_pad, plan.j_pad, plan.n_gx, plan.n_gy
    lane_count = plan.lanes
    groups = grid // n_gx

    def collect(source, carry):
        for mode in range(modes):
            both = incoming.at[source * modes + mode][...]
            rows[mode, pl.ds(source, 1), :] = both[:, :half]
            rows[mode, pl.ds(parts + source, 1), :] = both[:, half:]
        return carry

    loads[0].wait()
    lax.fori_loop(0, parts, collect, 0)
    loads[1].wait()
    for mode in range(modes):
        lines[mode] = left_apply(gather[...], rows[mode])
    base = n_gy * kx_pad
    y_slots = [slice(j * kx_pad, (j + 1) * kx_pad) for j in range(n_gy)]
    x_slots = [slice(base + i * j_pad, base + (i + 1) * j_pad) for i in range(n_gx)]

    def side_by_side(slots, count):
        return jnp.concatenate(
            [lines[:, slot, :].reshape(modes * count, half) for slot in slots], axis=1
        )

    loads[2].wait()
    split_table(along_y_full, along_y, 0)
    loads[3].wait()
    split_table(along_x_full, along_x, 0)
    folded_y[...] = right_apply(side_by_side(y_slots, kx_pad), along_y[...]).reshape(
        modes, kx_pad, lane_count
    )
    folded_x[...] = right_apply(side_by_side(x_slots, j_pad), along_x[...]).reshape(
        modes, j_pad, lane_count
    )

    def solve(mode, carry):
        across = value_parts(folded_x[mode, :, :grid], 0, expand.shape[0] // j_pad)
        spread = dot(across, expand[...], ((0,), (0,)))
        number = spread.reshape(groups, kx_pad, lane_count) + folded_y[mode][None]
        bottom = stiff_x[...] + (stiff_y[...] + stiff_z[first_mode[0] + mode])
        value = number * inverse(bottom).reshape(groups, kx_pad, lane_count)
        folded_y[mode] = jnp.sum(value, axis=0)
        value = value_parts(value.reshape(grid, lane_count), 1, expand.shape[0] // j_pad)
        value = value.astype(jnp.bfloat16)
        folded_x[mode, :, :grid] = dot(expand_back[...], value, ((1,), (1,)))
        return carry

    for copy in loads[4:8]:
        copy.wait()
    chunked_loop(modes, 3, solve, 0)
    loads[8].wait()
    split_table(along_y_full, along_y_back, 1)
    split_table(along_x_full, along_x_back, 1)
    all_y = folded_y[...].reshape(modes * kx_pad, lane_count)
    all_y = dot(value_triple(all_y, 1), along_y_back[...], ((1,), (1,)))
    for j, slot in enumerate(y_slots):
        lines[:, slot, :] = all_y[:, j * half : (j + 1) * half].reshape(modes, kx_pad, half)
    all_x = folded_x[...].reshape(modes * j_pad, lane_count)
    all_x = dot(value_triple(all_x, 1), along_x_back[...], ((1,), (1,)))
    for i, slot in enumerate(x_slots):
        lines[:, slot, :] = all_x[:, i * half : (i + 1) * half].reshape(modes, j_pad, half)
    for mode in range(modes):
        rows[mode] = left_apply(scatter[...], lines[mode])

    def distribute(target, carry):
        for mode in range(modes):
            outgoing[target * modes + mode, :, :half] = rows[mode, pl.ds(target, 1), :]
            outgoing[target * modes + mode, :, half:] = rows[mode, pl.ds(parts + target, 1), :]
        return carry

    lax.fori_loop(0, parts, distribute, 0)


def backward_kernel(
    plan,
    n_blocks,
    block_atoms,
    places_hbm,
    message_hbm,
    interface_hbm,
    factors_hbm,
    edge_y_hbm,
    spectrum_hbm,
    y_table_hbm,
    z_full_hbm,
    _,
    potential_hbm,
    values,
    lookup,
    work,
    solved,
    stack,
    heads,
    edge_rows,
    turned,
    picked,
    potential,
    places,
    message,
    interface_full,
    interface,
    factors,
    edge_y,
    spectrum,
    y_table,
    z_full,
    z_table,
    blocks,
    sems,
):
    x_len, y_len, y_pad, x_pad = plan.x_len, plan.y_len, plan.y_pad, plan.x_pad
    grid, lane_count, planes = plan.grid, plan.lanes, plan.planes
    slabs = slab_count(plan)
    loads = start_copies(
        [
            (message_hbm, message),
            (interface_hbm, interface_full),
            (places_hbm, places),
            (factors_hbm, factors),
            (edge_y_hbm, edge_y),
            (spectrum_hbm, spectrum),
            (y_table_hbm, y_table),
            (z_full_hbm, z_full),
        ],
        sems,
    )
    loads[0].wait()
    for mode in range(grid):
        turned[mode : mode + 1, :] = message[mode]
    if lane_count > grid:
        turned[grid:, :] = jnp.zeros((lane_count - grid, turned.shape[1]), jnp.float32)
    loads[1].wait()
    split_table(interface_full, interface, 1)
    stack[...] = dot(interface[...], value_triple(turned[...], 1), ((1,), (1,)))
    loads[2].wait()
    count = list_owned(plan, places, blocks, plan.n_gx * n_blocks)
    for copy in loads[3:]:
        copy.wait()
    split_table(z_full, z_table, 0)
    for tile in range(plan.lane_tiles):
        lanes = slice(tile * 128, tile * 128 + 128)
        near_weight = edge_y[0]
        far_weight = edge_y[1]
        heads[tile] = stack[3 * y_pad : 3 * y_pad + x_pad, lanes]
        edge_rows[...] = stack[3 * y_pad + x_pad : 3 * y_pad + 2 * x_pad, lanes]

        def eliminate(step, carry):
            x = step + 1
            load = spectrum.at[x][:, lanes] + near_weight * heads[tile, pl.ds(x, 1), :]
            load = load + far_weight * edge_rows[pl.ds(x, 1), :]
            value = (load + carry) * factors.at[x][:, lanes]
            solved.at[x][...] = value
            return value

        def substitute(step, value):
            x = x_len - 1 - step
            value = solved.at[x][...] + factors.at[x][:, lanes] * value
            work.at[x][:, lanes] = value
            return value

        chunked_loop(x_len - 1, 5, eliminate, stack[0:y_pad, lanes])
        chunked_loop(x_len - 1, 5, substitute, stack[y_pad : 2 * y_pad, lanes])
    work[0] = jnp.zeros((y_pad, lane_count), jnp.float32)

    def transform(step, carry):
        start = step * slabs
        for slab in range(slabs):
            x = start + slab
            slab_work = work.at[x]
            slab_work[...] = left_apply(y_table[...], slab_work[...])
            for tile in range(plan.lane_tiles):
                lanes = slice(tile * 128, tile * 128 + 128)
                slab_work[0:1, lanes] = heads[tile, pl.ds(x, 1), :]

        @pl.when(step == 0)
        def _():
            work[0] = stack[2 * y_pad : 3 * y_pad, :]

        lines = work.at[pl.ds(start, slabs)][...].reshape(slabs * y_pad, lane_count)
        lines = right_apply(lines, z_table[...])
        for tile in range(plan.lane_tiles):
            low = tile * 128
            place = pl.ds(pl.multiple_of(tile * planes + start * y_pad, 8), slabs * y_pad)
            lookup.at[place][...] = lines[:, low : low + 128]
        lines = lines.reshape(slabs, y_pad, lane_count)
        potential.at[pl.ds(start, slabs)][...] = lines[:, :y_len, :grid]
        return carry

    chunked_loop(x_len // slabs, 3, transform, 0)
    potential_copy = pltpu.make_async_copy(potential, potential_hbm, sems.at[8])
    potential_copy.start()
    values[...] = jnp.zeros(values.shape, jnp.float32)
    lane_ids = lax.broadcasted_iota(jnp.int32, (1, 128), 1)
    shape = (block_atoms, 128)
    own_lane = lax.broadcasted_iota(jnp.int32, shape, 0) == lax.broadcasted_iota(
        jnp.int32, shape, 1
    )

    def reduce_rows(rows, block):
        found = jnp.sum(rows, axis=1, keepdims=True)
        found = jnp.sum(jnp.where(own_lane, found, 0.0), axis=0, keepdims=True)
        values[pl.ds(block, 1), :] = found

    def sample(slot, before):
        block = blocks[slot]
        row_codes = places.at[block]
        rows_before = picked[...]
        for first in range(0, block_atoms, 16):
            rows = []
            for atom in range(first, first + 16):
                code = row_codes[atom]
                row = lookup[pl.ds(lax.shift_right_logical(code, 7), 1), :]
                rows.append(jnp.where(lane_ids == (code & 127), row, 0.0))
            for k in range(16):
                picked[first + k : first + k + 1, :] = rows[k]
        reduce_rows(rows_before, before)
        return block

    picked[...] = jnp.zeros(picked.shape, jnp.float32)
    last = lax.fori_loop(0, count, sample, blocks[0])

    @pl.when(count > 0)
    def _():
        reduce_rows(picked[...], last)

    potential_copy.wait()


def prepare_kernel(
    plan, n_blocks, block_atoms, counts, owners, type_radius, coords, charge, types, cells,
    copies, atom_rows, payload,
):
    tile_atoms = n_blocks * block_atoms
    lane = lax.broadcasted_iota(jnp.int32, (1, 128), 1)
    slot = lane // block_atoms
    atom = lane - slot * block_atoms
    per_row = 128 // block_atoms
    for start in range(0, tile_atoms, 128):
        lanes = slice(start, start + 128)
        first = start // block_atoms
        count = jnp.full((1, 128), counts[0, first], jnp.int32)
        owner = jnp.full((1, 128), owners[0, first], jnp.int32)
        for k in range(1, per_row):
            count = jnp.where(slot >= k, counts[0, first + k], count)
            owner = jnp.where(slot >= k, owners[0, first + k], owner)
        live = jnp.where(atom < count, charge[0, :, lanes], 0.0)
        cell = cells[0, :, lanes]
        line = jnp.floor((cell.astype(jnp.float32) + 0.5) * (1.0 / plan.grid)).astype(jnp.int32)
        depth = cell - line * plan.grid
        x = jnp.floor((line.astype(jnp.float32) + 0.5) * (1.0 / plan.y_len)).astype(jnp.int32)
        plane = x * plan.y_pad + (line - x * plan.y_len)
        code = ((depth >> 7) * plan.planes + plane) * 128 + (depth & 127)
        code = (owner * plan.span + code).astype(jnp.float32)
        for k in range(per_row):
            shift = k * block_atoms
            row = pltpu.roll(code, (128 - shift) % 128, 1)
            charges = pltpu.roll(live, (128 + block_atoms - shift) % 128, 1)
            row = jnp.where(lane < block_atoms, row, charges)
            payload[first + k : first + k + 1, :] = jnp.where(lane < 2 * block_atoms, row, 0.0)
        radius = jnp.zeros((1, 128), jnp.float32)
        for kind in range(type_radius.shape[0]):
            radius = jnp.where(types[0, :, lanes] == kind, type_radius[kind], radius)
        atom_rows[0, 0:3, lanes] = coords[0, :, 0, lanes]
        atom_rows[0, 3:4, lanes] = live
        atom_rows[0, 4:5, lanes] = radius
    for target in range(plan.n_gx):
        copies[target * n_blocks : (target + 1) * n_blocks, :] = payload[...]


def pair_kernel(
    n_blocks, block_atoms, listed, first, part_atoms, listing, low, middle, high, earlier, forces,
    table, columns, results,
):
    tile_atoms = n_blocks * block_atoms
    sides = (low, middle, high)
    for step_x in range(3):
        for step_y in range(3):
            rows = sides[step_y][step_x]
            shifts = (step_x - 1.0, step_y - 1.0, 0.0, 0.0, 0.0)
            for k in range(5):
                row = rows[k : k + 1, :]
                if shifts[k]:
                    row = row + shifts[k]
                table[step_x * 3 + step_y, k] = jnp.broadcast_to(row, (8, tile_atoms))
    columns[0:5, :] = middle[1, :, first : first + part_atoms]
    columns[5:, :] = jnp.zeros((columns.shape[0] - 5, part_atoms), jnp.float32)
    results[...] = jnp.transpose(columns[...])
    lane_ids = lax.broadcasted_iota(jnp.int32, (block_atoms, 128), 1)
    groups = block_atoms // 8

    def group(number, carry):
        place = pl.ds(pl.multiple_of(number * block_atoms, block_atoms), block_atoms)
        block = first // block_atoms + number
        own = results[place, :]
        mine = [
            jnp.broadcast_to(own[:, k : k + 1], (block_atoms, 128)).reshape(groups, 8, 128)
            for k in (0, 1, 2, 4)
        ]
        force_x = force_y = force_z = jnp.zeros((groups, 8, 128), jnp.float32)
        for slot in range(listed):
            rows = table.at[listing[0, slot, 0, block]]
            for start in range(0, tile_atoms, 128):
                lanes = slice(start, start + 128)
                sep_x = mine[0] - rows[0, :, lanes][None]
                sep_y = mine[1] - rows[1, :, lanes][None]
                sep_z = mine[2] - rows[2, :, lanes][None]
                reach = mine[3] + rows[4, :, lanes][None]
                root = lax.rsqrt(sep_x * sep_x + sep_y * sep_y + sep_z * sep_z + reach * reach)
                strength = rows[3, :, lanes][None] * root * (root * root)
                force_x = force_x + strength * sep_x
                force_y = force_y + strength * sep_y
                force_z = force_z + strength * sep_z
        out = jnp.zeros((block_atoms, 128), jnp.float32)
        for axis, total in enumerate((force_x, force_y, force_z)):
            total = jnp.sum(total.reshape(block_atoms, 128), axis=1, keepdims=True)
            out = jnp.where(lane_ids == axis, own[:, 3:4] * total, out)
        results[place, :] = out
        return carry

    lax.fori_loop(0, part_atoms // block_atoms, group, 0)
    columns[...] = jnp.transpose(results[...])
    if first:
        for axis in range(3):
            forces[axis, :, :first] = earlier[axis, :, :first]
    for axis in range(3):
        forces[axis, :, first : first + part_atoms] = columns[axis : axis + 1, :]


VMEM = pl.BlockSpec(memory_space=pltpu.VMEM)
SMEM = pl.BlockSpec(memory_space=pltpu.SMEM)
HBM = pl.BlockSpec(memory_space=pl.ANY)


def shaped(*shape):
    return jax.ShapeDtypeStruct(shape, jnp.float32)


def buffer(*shape):
    return pltpu.VMEM(shape, jnp.float32)


def like(table):
    return pltpu.VMEM(table.shape, table.dtype)


def limit(mib):
    return pltpu.CompilerParams(vmem_limit_bytes=mib * MIB)


def order_kernel(*refs):
    pass


def after(message, others):
    return pl.pallas_call(
        order_kernel,
        out_shape=shaped(*message.shape),
        in_specs=[HBM] + [VMEM] * len(others),
        out_specs=HBM,
        input_output_aliases={0: 0},
        compiler_params=limit(VMEM_MIB),
        name="order_message",
    )(message, *others)


def solve_poisson(plan, density, codes, first_code, n_blocks, block_atoms, neighbours, pair_part):
    x_len, y_len, grid = density.shape
    y_pad, x_pad, half, lanes = plan.y_pad, plan.x_pad, plan.half, plan.lanes
    total = plan.parts * plan.modes
    z_full = f32(plan.z_matrix())
    y_table = table_triple(plan.y_matrix(), 1)
    factors = f32(plan.elimination_factors())
    edge_y = f32(plan.edge_weights())
    interface = f32(plan.interface_table())
    bf16 = jnp.bfloat16
    code_shape = codes.shape
    shared = [
        buffer(x_len, y_pad, 128),
        buffer(plan.stack_rows, lanes),
        buffer(plan.lane_tiles, x_pad, 128),
    ]
    spectrum, places, message = pl.pallas_call(
        functools.partial(forward_kernel, plan, n_blocks, block_atoms),
        out_shape=(
            shaped(x_len, y_pad, lanes),
            jax.ShapeDtypeStruct(code_shape, jnp.int32),
            shaped(total, 1, 2 * half),
        ),
        in_specs=[SMEM] + [HBM] * 7 + [VMEM],
        out_specs=(HBM, HBM, VMEM),
        scratch_shapes=[buffer(plan.lane_tiles * plan.planes, 128)]
        + shared
        + [
            buffer(2, x_pad, 128),
            buffer(lanes, 2 * half),
            buffer(*code_shape),
            buffer(x_len, y_len, grid),
            like(z_full),
            pltpu.VMEM((3 * lanes, lanes), bf16),
            like(y_table),
            like(factors),
            like(edge_y),
            like(interface),
            pltpu.VMEM((3 * plan.stack_rows, 2 * half), bf16),
            buffer(x_len, y_pad, lanes),
            pltpu.VMEM(code_shape, jnp.int32),
            pltpu.SMEM(code_shape, jnp.int32),
            pltpu.SMEM((code_shape[0],), jnp.int32),
            pltpu.SemaphoreType.DMA((11,)),
        ]
        + [pltpu.SMEM(code_shape, jnp.float32)] * (code_shape[0] <= 512),
        compiler_params=limit(VMEM_MIB),
        name="forward_solve",
    )(first_code, codes, density, z_full, y_table, factors, edge_y, interface, neighbours[0])
    message = after(message, neighbours[1:])
    eighth = n_blocks * block_atoms // 8
    first_pairs = pair_part(0, 4 * eighth, None)
    incoming = lax.all_to_all(message, ("gx", "gy"), split_axis=0, concat_axis=0, tiled=True)
    gather = plan.gather_table()
    along_y, along_x = plan.line_tables()
    expand = plan.expand_table()
    position = lax.axis_index("gx") * plan.n_gy + lax.axis_index("gy")
    first_mode = (position * plan.modes).astype(jnp.int32).reshape(1)
    stiff = stiffness(grid, grid)
    padded_z = np.zeros(total)
    padded_z[:grid] = stiff
    padded_y = np.zeros((1, lanes))
    padded_y[0, :grid] = stiff
    tables = [
        table_triple(gather, 1),
        f32(along_y),
        f32(along_x),
        f32(table_parts(expand, 0)),
        table_parts(expand, 1),
        f32(stiff[:, None] * grid),
        f32(padded_y * grid),
        table_triple(gather.T, 1),
    ]
    outgoing = pl.pallas_call(
        functools.partial(interface_kernel, plan),
        out_shape=shaped(total, 1, 2 * half),
        in_specs=[SMEM] * 2 + [VMEM] + [HBM] * 9,
        out_specs=VMEM,
        scratch_shapes=[
            buffer(plan.modes, 2 * plan.parts, half),
            buffer(plan.modes, plan.kx_pad, lanes),
            buffer(plan.modes, plan.j_pad, lanes),
            buffer(plan.modes, gather.shape[0], half),
            buffer(total, 1, 2 * half),
            *[like(table) for table in tables],
            pltpu.VMEM((3 * along_y.shape[0], lanes), bf16),
            pltpu.VMEM((3 * along_x.shape[0], lanes), bf16),
            pltpu.VMEM((along_y.shape[0], 3 * lanes), bf16),
            pltpu.VMEM((along_x.shape[0], 3 * lanes), bf16),
            pltpu.SemaphoreType.DMA((9,)),
        ],
        compiler_params=limit(VMEM_MIB),
        name="interface_solve",
    )(first_mode, f32((padded_z + SCREENING) * grid), first_pairs, incoming, *tables)
    returned = lax.all_to_all(outgoing, ("gx", "gy"), split_axis=0, concat_axis=0, tiled=True)
    more_pairs = pair_part(4 * eighth, 3 * eighth, first_pairs)
    potential, values = pl.pallas_call(
        functools.partial(backward_kernel, plan, n_blocks, block_atoms),
        out_shape=(shaped(x_len, y_len, grid), shaped(plan.n_gx * n_blocks, 128)),
        in_specs=[HBM] * 8 + [VMEM],
        out_specs=(HBM, VMEM),
        scratch_shapes=[
            buffer(plan.lane_tiles * plan.planes, 128),
            buffer(x_len, y_pad, lanes),
        ]
        + shared
        + [
            buffer(x_pad, 128),
            buffer(lanes, 2 * half),
            buffer(block_atoms, 128),
            buffer(x_len, y_len, grid),
            pltpu.SMEM(code_shape, jnp.int32),
            buffer(total, 1, 2 * half),
            like(interface),
            pltpu.VMEM((plan.stack_rows, 6 * half), bf16),
            like(factors),
            like(edge_y),
            buffer(x_len, y_pad, lanes),
            like(y_table),
            like(z_full),
            pltpu.VMEM((3 * lanes, lanes), bf16),
            pltpu.SMEM((code_shape[0],), jnp.int32),
            pltpu.SemaphoreType.DMA((9,)),
        ],
        compiler_params=limit(VMEM_MIB),
        name="backward_solve",
    )(places, returned, interface, factors, edge_y, spectrum, y_table, z_full, more_pairs)
    pair_force = pair_part(7 * eighth, eighth, more_pairs)
    return potential, values, pair_force


def shifted(block, axis, step):
    count = lax.axis_size(axis)
    return lax.ppermute(block, axis, [(i, (i + step) % count) for i in range(count)])


def body(
    qm_density,
    mm_coords,
    mm_charge,
    mm_types,
    type_radius,
    mm_cells,
    block_counts,
    block_owner,
    neighbour_tiles,
):
    n_blocks = block_counts.shape[2]
    tile_atoms = mm_charge.shape[2]
    block_atoms = tile_atoms // n_blocks
    x_local, local_y_rows, grid_len = qm_density.shape
    n_gx = lax.axis_size("gx")
    plan = Plan(x_local, local_y_rows, grid_len, n_gx, lax.axis_size("gy"))
    copies, atom_rows = pl.pallas_call(
        functools.partial(prepare_kernel, plan, n_blocks, block_atoms),
        out_shape=(shaped(n_gx * n_blocks, 128), shaped(1, 5, tile_atoms)),
        in_specs=[SMEM] * 3 + [VMEM] * 4,
        out_specs=(VMEM, VMEM),
        scratch_shapes=[buffer(n_blocks, 128)],
        compiler_params=limit(VMEM_MIB),
        name="prepare_atoms",
    )(
        block_counts.reshape(1, n_blocks),
        block_owner.reshape(1, n_blocks),
        type_radius,
        mm_coords.transpose(0, 2, 1, 3),
        mm_charge,
        mm_types,
        mm_cells,
    )
    codes = lax.all_to_all(copies, "gx", split_axis=0, concat_axis=0, tiled=True)
    first_code = (lax.axis_index("gx") * plan.span).astype(jnp.int32).reshape(1)
    triple = jnp.concatenate(
        [shifted(atom_rows, "gx", 1), atom_rows, shifted(atom_rows, "gx", -1)], axis=0
    )
    below, above = shifted(triple, "gy", 1), shifted(triple, "gy", -1)
    listed = neighbour_tiles.shape[3]
    listing = neighbour_tiles.transpose(0, 3, 1, 2)

    def pair_part(first, part_atoms, earlier):
        if earlier is None:
            earlier = jnp.zeros((3, 1, 128), jnp.float32)
        return pl.pallas_call(
            functools.partial(pair_kernel, n_blocks, block_atoms, listed, first, part_atoms),
            out_shape=shaped(3, 1, first + part_atoms),
            in_specs=[SMEM] + [VMEM] * 4,
            out_specs=VMEM,
            scratch_shapes=[
                buffer(9, 5, 8, tile_atoms),
                buffer(128, part_atoms),
                buffer(part_atoms, 128),
            ],
            compiler_params=limit(VMEM_MIB),
            cost_estimate=pl.CostEstimate(
                flops=21 * listed * tile_atoms * part_atoms,
                bytes_accessed=4 * 50 * tile_atoms,
                transcendentals=listed * tile_atoms * part_atoms,
            ),
            name="pair_forces",
        )(listing, below, triple, above, earlier)

    potential, values, pair_force = solve_poisson(
        plan, qm_density, codes, first_code, n_blocks, block_atoms, (triple, below, above), pair_part
    )
    values = lax.all_to_all(values, "gx", split_axis=0, concat_axis=0, tiled=True)
    sampled = jnp.sum(values.reshape(n_gx, n_blocks, 128), axis=0)[:, :block_atoms]
    lanes = jnp.arange(block_atoms, dtype=jnp.int32)
    live = lanes[None, :] < block_counts.reshape(n_blocks, 1)
    mm_potential = jnp.where(live, sampled, 0.0).reshape(1, 1, tile_atoms)
    return (potential, mm_potential, pair_force[None].transpose(0, 2, 1, 3))


def solution(mesh):
    placed = (
        P("gx", "gy", None),
        P("gx", "gy", None, None),
        P("gx", "gy", None),
        P("gx", "gy", None),
        P(),
        P("gx", "gy", None),
        P("gx", "gy", None),
        P("gx", "gy", None, None),
        P("gx", "gy", None, None),
    )
    return jax.shard_map(
        body,
        mesh=mesh,
        in_specs=placed,
        out_specs=(P("gx", "gy", None), P("gx", "gy", None), P("gx", "gy", None, None)),
        check_vma=False,
    )
```

```python
import functools

import jax
import jax.numpy as jnp
import ml_dtypes
import numpy as np
from jax import lax
from jax.experimental import pallas as pl
from jax.experimental.pallas import tpu as pltpu
from jax.sharding import PartitionSpec as P

SCREENING = 0.003
HIGH_ACCURACY = lax.Precision.HIGHEST
VMEM_MIB = 60
BATCH = 16
MIB = 1024 * 1024


def round_up(value, unit):
    return -(-value // unit) * unit


def sine_matrix(length):
    nodes = np.arange(length, dtype=np.float64)
    return np.sqrt(2.0 / length) * np.sin(np.pi * np.outer(nodes, nodes) / length)


def cas_matrix(length):
    nodes = np.arange(length)
    angle = 2.0 * np.pi * (np.outer(nodes, nodes) % length) / length
    return np.cos(angle) + np.sin(angle)


def stiffness(count, length):
    return 4.0 * np.sin(np.pi * np.arange(count) / length) ** 2


def split_pair(matrix):
    full = np.asarray(matrix, np.float32)
    high = full.astype(ml_dtypes.bfloat16)
    low = (full - high.astype(np.float32)).astype(ml_dtypes.bfloat16)
    return high, low


def table_triple(matrix, axis):
    high, low = split_pair(matrix)
    return np.concatenate([high, low, high], axis=axis)


def f32(table):
    return np.asarray(table, np.float32)


class Plan:
    def __init__(self, x_len, y_len, grid, n_gx, n_gy):
        self.x_len, self.y_len, self.grid = x_len, y_len, grid
        self.n_gx, self.n_gy = n_gx, n_gy
        self.y_pad = round_up(y_len, 8)
        self.x_pad = round_up(x_len, 8)
        self.lanes = round_up(grid, 128)
        self.lane_tiles = self.lanes // 128
        self.planes = x_len * self.y_pad
        self.span = self.lane_tiles * self.planes * 128
        self.parts = n_gx * n_gy
        self.modes = -(-grid // self.parts)
        self.half = round_up(y_len + x_len, 128)
        self.kx_pad = round_up(n_gx, 8)
        self.j_pad = round_up(n_gy, 8)
        self.stack_rows = round_up(3 * self.y_pad + 2 * self.x_pad, 128)

    def y_matrix(self):
        out = np.zeros((self.y_pad, self.y_pad))
        out[: self.y_len, : self.y_len] = sine_matrix(self.y_len)
        return out

    def z_matrix(self):
        out = np.zeros((self.lanes, self.lanes))
        out[: self.grid, : self.grid] = cas_matrix(self.grid) / np.sqrt(self.grid)
        return out

    def elimination_factors(self):
        z_part = np.zeros(self.lanes)
        z_part[: self.grid] = stiffness(self.grid, self.grid)
        y_part = stiffness(self.y_pad, 2 * self.y_len)
        diagonal = 2.0 + y_part[:, None] + z_part[None, :] + SCREENING
        out = np.zeros((self.x_len, self.y_pad, self.lanes))
        for x in range(1, self.x_len):
            out[x] = 1.0 / (diagonal - out[x - 1])
        return out

    def edge_weights(self):
        sine_y = self.y_matrix()
        both = np.stack([sine_y[1], sine_y[self.y_len - 1]])
        return np.broadcast_to(both[:, :, None], (2, self.y_pad, 128))

    def interface_table(self):
        x_len, y_len, half = self.x_len, self.y_len, self.half
        y_pad, x_pad = self.y_pad, self.x_pad
        sine_y = sine_matrix(y_len)
        out = np.zeros((self.stack_rows, 2 * half))
        out[:y_len, :y_len] = sine_y
        row = y_pad
        out[row : row + y_len, half : half + y_len] = sine_y
        row += y_pad
        out[row : row + y_len, :y_len] = np.eye(y_len)
        row += y_pad
        out[row + 1 : row + x_len, y_len + 1 : y_len + x_len] = np.eye(x_len - 1)
        row += x_pad
        far = half + y_len
        out[row + 1 : row + x_len, far + 1 : far + x_len] = np.eye(x_len - 1)
        return out

    def gather_table(self):
        n_gx, n_gy, parts = self.n_gx, self.n_gy, self.parts
        cas_x = cas_matrix(n_gx)
        out = np.zeros((n_gy * self.kx_pad + n_gx * self.j_pad, 2 * parts))
        for i in range(n_gx):
            for j in range(n_gy):
                col = i * n_gy + j
                base = j * self.kx_pad
                out[base : base + n_gx, col] = cas_x[:, i]
                out[base : base + n_gx, parts + col] = cas_x[:, (i + 1) % n_gx]
                base = n_gy * self.kx_pad + i * self.j_pad
                out[base + j, col] = 1.0
                out[base + (j + 1) % n_gy, parts + col] = 1.0
        return out

    def line_tables(self):
        scaled = cas_matrix(self.grid) / np.sqrt(self.grid)
        along_y = np.zeros((self.n_gy, self.half, self.lanes))
        along_x = np.zeros((self.n_gx, self.half, self.lanes))
        y_len, x_len, grid = self.y_len, self.x_len, self.grid
        for j in range(self.n_gy):
            along_y[j, :y_len, :grid] = scaled[j * y_len : (j + 1) * y_len]
        for i in range(self.n_gx):
            along_x[i, y_len : y_len + x_len, :grid] = scaled[i * x_len : (i + 1) * x_len]
        return along_y.reshape(-1, self.lanes), along_x.reshape(-1, self.lanes)

    def expand_table(self):
        ratio = self.grid // self.n_gy
        full = cas_matrix(self.grid)
        out = np.zeros((self.j_pad, self.lanes))
        for j in range(self.n_gy):
            out[j, : self.grid] = full[(j * ratio) % self.grid]
        return np.where(np.abs(out - np.round(out)) < 1e-9, np.round(out), out)


def dot(a, b, dims=((1,), (0,)), precision=None):
    return lax.dot_general(
        a, b, (dims, ((), ())), precision=precision, preferred_element_type=jnp.float32
    )


def value_parts(value, axis, count):
    high = value.astype(jnp.bfloat16).astype(jnp.float32)
    return jnp.concatenate([high] * (count - 1) + [value - high], axis=axis)


def table_parts(matrix, axis):
    high, low = split_pair(matrix)
    if low.astype(np.float32).any():
        return np.concatenate([high, low, high], axis=axis)
    return np.concatenate([high, high], axis=axis)


def value_triple(value, axis):
    high = value.astype(jnp.bfloat16).astype(jnp.float32)
    return jnp.concatenate([high, high, value - high], axis=axis).astype(jnp.bfloat16)


def split_table(source, target, axis):
    value = source[...]
    high = value.astype(jnp.bfloat16).astype(jnp.float32)
    parts = jnp.concatenate([high, value - high, high], axis=axis)
    target[...] = parts.astype(jnp.bfloat16)


def left_apply(table, value):
    return dot(table, value_triple(value, 0))


def right_apply(value, table):
    return dot(value_triple(value, 1), table)


def slab_count(plan):
    if plan.y_pad != plan.y_len:
        return 1
    return max(count for count in (4, 3, 2, 1) if plan.x_len % count == 0)


def inverse(value):
    guess = pl.reciprocal(value, approx=True)
    guess = guess * (2.0 - value * guess)
    return guess * (2.0 - value * guess)


def start_copies(pairs, sems):
    copies = [
        pltpu.make_async_copy(source, target, sems.at[k])
        for k, (source, target) in enumerate(pairs)
    ]
    for copy in copies:
        copy.start()
    return copies


def list_owned(plan, places, blocks, block_count):
    def several(step, count):
        for k in range(8):
            number = step * 8 + k
            lead = places[number, 0]
            blocks[count] = number
            count = count + jnp.where((lead >= 0) & (lead < plan.span), 1, 0)
        return count

    return lax.fori_loop(0, block_count // 8, several, 0)


def chunked_loop(count, unroll, body, init):
    while count % unroll:
        unroll -= 1

    def group(step, carry):
        for k in range(unroll):
            carry = body(step * unroll + k, carry)
        return carry

    return lax.fori_loop(0, count // unroll, group, init)


def mark_places(codes, first_code, place_rows, block_atoms):
    lane = lax.broadcasted_iota(jnp.int32, codes.shape, 1)
    code = codes[...].astype(jnp.int32) - first_code
    place = lax.shift_right_arithmetic(code, 7)
    shared = jnp.zeros_like(place)
    for step in range(1, BATCH):
        same = (pltpu.roll(place, step, 1) == place) & (lane % BATCH >= step)
        shared = jnp.where(same & (lane < block_atoms), 1, shared)
    step = block_atoms // 2
    while step:
        shared = shared | pltpu.roll(shared, 128 - step, 1)
        step //= 2
    mark = pltpu.roll(shared, block_atoms, 1)
    place_rows[...] = jnp.where(lane == block_atoms, mark, code)


def forward_kernel(
    plan,
    n_blocks,
    block_atoms,
    first_code,
    *refs,
):
    (
        codes_hbm,
        density_hbm,
        z_full_hbm,
        y_table_hbm,
        factors_hbm,
        edge_y_hbm,
        interface_hbm,
        _,
        spectrum_hbm,
        places_hbm,
        message,
        added,
        solved,
        stack,
        heads,
        edge_rows,
        turned,
        codes,
        density,
        z_full,
        z_table,
        y_table,
        factors,
        edge_y,
        interface_full,
        interface,
        spectrum,
        place_rows,
        places,
        blocks,
        sems,
        *charges,
    ) = refs
    x_len, y_len, y_pad, x_pad = plan.x_len, plan.y_len, plan.y_pad, plan.x_pad
    grid, lane_count, planes = plan.grid, plan.lanes, plan.planes
    slabs = slab_count(plan)
    lane_ids = lax.broadcasted_iota(jnp.int32, (1, 128), 1)
    loads = start_copies(
        [
            (codes_hbm, codes),
            (density_hbm, density),
            (z_full_hbm, z_full),
            (y_table_hbm, y_table),
            (factors_hbm, factors),
            (edge_y_hbm, edge_y),
            (interface_hbm, interface_full),
        ],
        sems,
    )
    loads[0].wait()
    charge_copies = [pltpu.make_async_copy(codes, target, sems.at[7]) for target in charges]
    for copy in charge_copies:
        copy.start()
    mark_places(codes, first_code[0], place_rows, block_atoms)
    place_copies = [
        pltpu.make_async_copy(place_rows, places, sems.at[8]),
        pltpu.make_async_copy(place_rows, places_hbm, sems.at[9]),
    ]
    for copy in place_copies:
        copy.start()

    def clear(step, carry):
        place = pl.ds(pl.multiple_of(step * y_pad, 8), y_pad)
        added[place, :] = jnp.zeros((y_pad, 128), jnp.float32)
        return carry

    chunked_loop(plan.lane_tiles * x_len, 4, clear, 0)
    loads[2].wait()
    split_table(z_full, z_table, 0)
    for copy in [*charge_copies, place_copies[0]]:
        copy.wait()
    count = list_owned(plan, places, blocks, plan.n_gx * n_blocks)

    def deposit(slot, carry):
        block = blocks[slot]
        row_codes = places.at[block]
        charge_row = charges[0].at[block] if charges else codes[pl.ds(block, 1), :]

        def raised(code, k):
            lane = block_atoms + k
            charge = charge_row[lane] if charges else charge_row[:, lane : lane + 1]
            hit = jnp.where(lane_ids == (code & 127), charge, 0.0)
            return added[pl.ds(lax.shift_right_logical(code, 7), 1), :] + hit

        @pl.when(row_codes[block_atoms] == 0)
        def _():
            for start in range(0, block_atoms, BATCH):
                local = [row_codes[start + k] for k in range(BATCH)]
                rows = [raised(code, start + k) for k, code in enumerate(local)]
                for code, row in zip(local, rows):
                    added[pl.ds(lax.shift_right_logical(code, 7), 1), :] = row

        @pl.when(row_codes[block_atoms] != 0)
        def _():
            for k in range(block_atoms):
                code = row_codes[k]
                row = raised(code, k)
                added[pl.ds(lax.shift_right_logical(code, 7), 1), :] = row

        return carry

    lax.fori_loop(0, count, deposit, 0)
    loads[1].wait()
    loads[3].wait()

    def transform(step, carry):
        start = step * slabs
        count = slabs * y_pad
        pieces = []
        for tile in range(plan.lane_tiles):
            low = tile * 128
            width = min(128, grid - low)
            piece = density.at[pl.ds(start, slabs)][:, :, low : low + width]
            if y_pad == y_len:
                piece = piece.reshape(count, width)
            else:
                rows = jnp.zeros((y_pad - y_len, width), jnp.float32)
                piece = jnp.concatenate([piece[0], rows], axis=0)
            if width < 128:
                rest = jnp.zeros((count, 128 - width), jnp.float32)
                piece = jnp.concatenate([piece, rest], axis=1)
            place = pl.ds(pl.multiple_of(tile * planes + start * y_pad, 8), count)
            pieces.append(piece + added.at[place][...])
        lines = right_apply(jnp.concatenate(pieces, axis=1), z_table[...])
        lines = lines.reshape(slabs, y_pad, lane_count)
        for slab in range(slabs):
            x = start + slab
            for tile in range(plan.lane_tiles):
                heads[tile, pl.ds(x, 1), :] = lines[slab, 0:1, tile * 128 : tile * 128 + 128]
            spectrum.at[x][...] = left_apply(y_table[...], lines[slab])

        @pl.when(step == 0)
        def _():
            stack[2 * y_pad : 3 * y_pad, :] = lines[0]

        return carry

    chunked_loop(x_len // slabs, 3, transform, 0)
    spectrum_copy = pltpu.make_async_copy(spectrum, spectrum_hbm, sems.at[10])
    spectrum_copy.start()
    for copy in loads[4:]:
        copy.wait()
    split_table(interface_full, interface, 0)
    stack[3 * y_pad :, :] = jnp.zeros((stack.shape[0] - 3 * y_pad, lane_count), jnp.float32)
    for tile in range(plan.lane_tiles):
        lanes = slice(tile * 128, tile * 128 + 128)
        near_weight = edge_y[0]
        far_weight = edge_y[1]

        def eliminate(step, carry):
            x = step + 1
            value = (spectrum.at[x][:, lanes] + carry) * factors.at[x][:, lanes]
            solved.at[x][...] = value
            return value

        def substitute(step, value):
            x = x_len - 1 - step
            value = solved.at[x][...] + factors.at[x][:, lanes] * value
            near_row = jnp.sum(value * near_weight, axis=0, keepdims=True)
            far_row = jnp.sum(value * far_weight, axis=0, keepdims=True)
            edge_rows[0, pl.ds(x, 1), :] = near_row + heads[tile, pl.ds(x, 1), :]
            edge_rows[1, pl.ds(x, 1), :] = far_row
            return value

        zero = jnp.zeros((y_pad, 128), jnp.float32)
        chunked_loop(x_len - 1, 5, eliminate, zero)
        stack[y_pad : 2 * y_pad, lanes] = solved[x_len - 1]
        stack[0:y_pad, lanes] = chunked_loop(x_len - 1, 5, substitute, zero)
        for side in range(2):
            row = 3 * y_pad + side * x_pad
            stack[row + 1 : row + x_len, lanes] = edge_rows[side, 1:x_len, :]
    turned[...] = right_apply(jnp.transpose(stack[...]), interface[...])
    total = plan.parts * plan.modes
    for mode in range(grid):
        message[mode] = turned[mode : mode + 1, :]
    if total > grid:
        message[grid:total] = jnp.zeros((total - grid, 1, 2 * plan.half), jnp.float32)
    spectrum_copy.wait()
    place_copies[1].wait()


def interface_kernel(
    plan,
    first_mode,
    stiff_z,
    _,
    incoming_hbm,
    gather_hbm,
    along_y_hbm,
    along_x_hbm,
    expand_hbm,
    expand_back_hbm,
    stiff_x_hbm,
    stiff_y_hbm,
    scatter_hbm,
    outgoing,
    rows,
    folded_y,
    folded_x,
    lines,
    incoming,
    gather,
    along_y_full,
    along_x_full,
    expand,
    expand_back,
    stiff_x,
    stiff_y,
    scatter,
    along_y,
    along_x,
    along_y_back,
    along_x_back,
    sems,
):
    loads = start_copies(
        [
            (incoming_hbm, incoming),
            (gather_hbm, gather),
            (along_y_hbm, along_y_full),
            (along_x_hbm, along_x_full),
            (expand_hbm, expand),
            (expand_back_hbm, expand_back),
            (stiff_x_hbm, stiff_x),
            (stiff_y_hbm, stiff_y),
            (scatter_hbm, scatter),
        ],
        sems,
    )
    grid, half, parts, modes = plan.grid, plan.half, plan.parts, plan.modes
    kx_pad, j_pad, n_gx, n_gy = plan.kx_pad, plan.j_pad, plan.n_gx, plan.n_gy
    lane_count = plan.lanes
    groups = grid // n_gx

    def collect(source, carry):
        for mode in range(modes):
            both = incoming.at[source * modes + mode][...]
            rows[mode, pl.ds(source, 1), :] = both[:, :half]
            rows[mode, pl.ds(parts + source, 1), :] = both[:, half:]
        return carry

    loads[0].wait()
    lax.fori_loop(0, parts, collect, 0)
    loads[1].wait()
    for mode in range(modes):
        lines[mode] = left_apply(gather[...], rows[mode])
    base = n_gy * kx_pad
    y_slots = [slice(j * kx_pad, (j + 1) * kx_pad) for j in range(n_gy)]
    x_slots = [slice(base + i * j_pad, base + (i + 1) * j_pad) for i in range(n_gx)]

    def side_by_side(slots, count):
        return jnp.concatenate(
            [lines[:, slot, :].reshape(modes * count, half) for slot in slots], axis=1
        )

    loads[2].wait()
    split_table(along_y_full, along_y, 0)
    loads[3].wait()
    split_table(along_x_full, along_x, 0)
    folded_y[...] = right_apply(side_by_side(y_slots, kx_pad), along_y[...]).reshape(
        modes, kx_pad, lane_count
    )
    folded_x[...] = right_apply(side_by_side(x_slots, j_pad), along_x[...]).reshape(
        modes, j_pad, lane_count
    )

    def solve(mode, carry):
        across = value_parts(folded_x[mode, :, :grid], 0, expand.shape[0] // j_pad)
        spread = dot(across, expand[...], ((0,), (0,)))
        number = spread.reshape(groups, kx_pad, lane_count) + folded_y[mode][None]
        bottom = stiff_x[...] + (stiff_y[...] + stiff_z[first_mode[0] + mode])
        value = number * inverse(bottom).reshape(groups, kx_pad, lane_count)
        folded_y[mode] = jnp.sum(value, axis=0)
        value = value_parts(value.reshape(grid, lane_count), 1, expand.shape[0] // j_pad)
        value = value.astype(jnp.bfloat16)
        folded_x[mode, :, :grid] = dot(expand_back[...], value, ((1,), (1,)))
        return carry

    for copy in loads[4:8]:
        copy.wait()
    chunked_loop(modes, 3, solve, 0)
    loads[8].wait()
    split_table(along_y_full, along_y_back, 1)
    split_table(along_x_full, along_x_back, 1)
    all_y = folded_y[...].reshape(modes * kx_pad, lane_count)
    all_y = dot(value_triple(all_y, 1), along_y_back[...], ((1,), (1,)))
    for j, slot in enumerate(y_slots):
        lines[:, slot, :] = all_y[:, j * half : (j + 1) * half].reshape(modes, kx_pad, half)
    all_x = folded_x[...].reshape(modes * j_pad, lane_count)
    all_x = dot(value_triple(all_x, 1), along_x_back[...], ((1,), (1,)))
    for i, slot in enumerate(x_slots):
        lines[:, slot, :] = all_x[:, i * half : (i + 1) * half].reshape(modes, j_pad, half)
    for mode in range(modes):
        rows[mode] = left_apply(scatter[...], lines[mode])

    def distribute(target, carry):
        for mode in range(modes):
            outgoing[target * modes + mode, :, :half] = rows[mode, pl.ds(target, 1), :]
            outgoing[target * modes + mode, :, half:] = rows[mode, pl.ds(parts + target, 1), :]
        return carry

    lax.fori_loop(0, parts, distribute, 0)


def backward_kernel(
    plan,
    n_blocks,
    block_atoms,
    places_hbm,
    message_hbm,
    interface_hbm,
    factors_hbm,
    edge_y_hbm,
    spectrum_hbm,
    y_table_hbm,
    z_full_hbm,
    _,
    potential_hbm,
    values,
    lookup,
    work,
    solved,
    stack,
    heads,
    edge_rows,
    turned,
    picked,
    potential,
    places,
    message,
    interface_full,
    interface,
    factors,
    edge_y,
    spectrum,
    y_table,
    z_full,
    z_table,
    blocks,
    sems,
):
    x_len, y_len, y_pad, x_pad = plan.x_len, plan.y_len, plan.y_pad, plan.x_pad
    grid, lane_count, planes = plan.grid, plan.lanes, plan.planes
    slabs = slab_count(plan)
    loads = start_copies(
        [
            (message_hbm, message),
            (interface_hbm, interface_full),
            (places_hbm, places),
            (factors_hbm, factors),
            (edge_y_hbm, edge_y),
            (spectrum_hbm, spectrum),
            (y_table_hbm, y_table),
            (z_full_hbm, z_full),
        ],
        sems,
    )
    loads[0].wait()
    for mode in range(grid):
        turned[mode : mode + 1, :] = message[mode]
    if lane_count > grid:
        turned[grid:, :] = jnp.zeros((lane_count - grid, turned.shape[1]), jnp.float32)
    loads[1].wait()
    split_table(interface_full, interface, 1)
    stack[...] = dot(interface[...], value_triple(turned[...], 1), ((1,), (1,)))
    loads[2].wait()
    count = list_owned(plan, places, blocks, plan.n_gx * n_blocks)
    for copy in loads[3:]:
        copy.wait()
    split_table(z_full, z_table, 0)
    for tile in range(plan.lane_tiles):
        lanes = slice(tile * 128, tile * 128 + 128)
        near_weight = edge_y[0]
        far_weight = edge_y[1]
        heads[tile] = stack[3 * y_pad : 3 * y_pad + x_pad, lanes]
        edge_rows[...] = stack[3 * y_pad + x_pad : 3 * y_pad + 2 * x_pad, lanes]

        def eliminate(step, carry):
            x = step + 1
            load = spectrum.at[x][:, lanes] + near_weight * heads[tile, pl.ds(x, 1), :]
            load = load + far_weight * edge_rows[pl.ds(x, 1), :]
            value = (load + carry) * factors.at[x][:, lanes]
            solved.at[x][...] = value
            return value

        def substitute(step, value):
            x = x_len - 1 - step
            value = solved.at[x][...] + factors.at[x][:, lanes] * value
            work.at[x][:, lanes] = value
            return value

        chunked_loop(x_len - 1, 5, eliminate, stack[0:y_pad, lanes])
        chunked_loop(x_len - 1, 5, substitute, stack[y_pad : 2 * y_pad, lanes])
    work[0] = jnp.zeros((y_pad, lane_count), jnp.float32)

    def transform(step, carry):
        start = step * slabs
        for slab in range(slabs):
            x = start + slab
            slab_work = work.at[x]
            slab_work[...] = left_apply(y_table[...], slab_work[...])
            for tile in range(plan.lane_tiles):
                lanes = slice(tile * 128, tile * 128 + 128)
                slab_work[0:1, lanes] = heads[tile, pl.ds(x, 1), :]

        @pl.when(step == 0)
        def _():
            work[0] = stack[2 * y_pad : 3 * y_pad, :]

        lines = work.at[pl.ds(start, slabs)][...].reshape(slabs * y_pad, lane_count)
        lines = right_apply(lines, z_table[...])
        for tile in range(plan.lane_tiles):
            low = tile * 128
            place = pl.ds(pl.multiple_of(tile * planes + start * y_pad, 8), slabs * y_pad)
            lookup.at[place][...] = lines[:, low : low + 128]
        lines = lines.reshape(slabs, y_pad, lane_count)
        potential.at[pl.ds(start, slabs)][...] = lines[:, :y_len, :grid]
        return carry

    chunked_loop(x_len // slabs, 3, transform, 0)
    potential_copy = pltpu.make_async_copy(potential, potential_hbm, sems.at[8])
    potential_copy.start()
    values[...] = jnp.zeros(values.shape, jnp.float32)
    lane_ids = lax.broadcasted_iota(jnp.int32, (1, 128), 1)
    shape = (block_atoms, 128)
    own_lane = lax.broadcasted_iota(jnp.int32, shape, 0) == lax.broadcasted_iota(
        jnp.int32, shape, 1
    )

    def reduce_rows(rows, block):
        found = jnp.sum(rows, axis=1, keepdims=True)
        found = jnp.sum(jnp.where(own_lane, found, 0.0), axis=0, keepdims=True)
        values[pl.ds(block, 1), :] = found

    def sample(slot, before):
        block = blocks[slot]
        row_codes = places.at[block]
        rows_before = picked[...]
        for first in range(0, block_atoms, 16):
            rows = []
            for atom in range(first, first + 16):
                code = row_codes[atom]
                row = lookup[pl.ds(lax.shift_right_logical(code, 7), 1), :]
                rows.append(jnp.where(lane_ids == (code & 127), row, 0.0))
            for k in range(16):
                picked[first + k : first + k + 1, :] = rows[k]
        reduce_rows(rows_before, before)
        return block

    picked[...] = jnp.zeros(picked.shape, jnp.float32)
    last = lax.fori_loop(0, count, sample, blocks[0])

    @pl.when(count > 0)
    def _():
        reduce_rows(picked[...], last)

    potential_copy.wait()


def prepare_kernel(
    plan, n_blocks, block_atoms, counts, owners, type_radius, coords, charge, types, cells,
    copies, atom_rows, payload,
):
    tile_atoms = n_blocks * block_atoms
    lane = lax.broadcasted_iota(jnp.int32, (1, 128), 1)
    slot = lane // block_atoms
    atom = lane - slot * block_atoms
    per_row = 128 // block_atoms
    for start in range(0, tile_atoms, 128):
        lanes = slice(start, start + 128)
        first = start // block_atoms
        count = jnp.full((1, 128), counts[0, first], jnp.int32)
        owner = jnp.full((1, 128), owners[0, first], jnp.int32)
        for k in range(1, per_row):
            count = jnp.where(slot >= k, counts[0, first + k], count)
            owner = jnp.where(slot >= k, owners[0, first + k], owner)
        live = jnp.where(atom < count, charge[0, :, lanes], 0.0)
        cell = cells[0, :, lanes]
        line = jnp.floor((cell.astype(jnp.float32) + 0.5) * (1.0 / plan.grid)).astype(jnp.int32)
        depth = cell - line * plan.grid
        x = jnp.floor((line.astype(jnp.float32) + 0.5) * (1.0 / plan.y_len)).astype(jnp.int32)
        plane = x * plan.y_pad + (line - x * plan.y_len)
        code = ((depth >> 7) * plan.planes + plane) * 128 + (depth & 127)
        code = (owner * plan.span + code).astype(jnp.float32)
        for k in range(per_row):
            shift = k * block_atoms
            row = pltpu.roll(code, (128 - shift) % 128, 1)
            charges = pltpu.roll(live, (128 + block_atoms - shift) % 128, 1)
            row = jnp.where(lane < block_atoms, row, charges)
            payload[first + k : first + k + 1, :] = jnp.where(lane < 2 * block_atoms, row, 0.0)
        radius = jnp.zeros((1, 128), jnp.float32)
        for kind in range(type_radius.shape[0]):
            radius = jnp.where(types[0, :, lanes] == kind, type_radius[kind], radius)
        atom_rows[0, 0:3, lanes] = coords[0, :, 0, lanes]
        atom_rows[0, 3:4, lanes] = live
        atom_rows[0, 4:5, lanes] = radius
    for target in range(plan.n_gx):
        copies[target * n_blocks : (target + 1) * n_blocks, :] = payload[...]


def pair_kernel(n_blocks, block_atoms, listed, first, part_atoms, listing, low, middle, high, *rest):
    *earlier, forces, table, columns, results = rest
    tile_atoms = n_blocks * block_atoms
    sides = (low, middle, high)
    for step_x in range(3):
        for step_y in range(3):
            rows = sides[step_y][step_x]
            shifts = (step_x - 1.0, step_y - 1.0, 0.0, 0.0, 0.0)
            for k in range(5):
                row = rows[k : k + 1, :]
                if shifts[k]:
                    row = row + shifts[k]
                table[step_x * 3 + step_y, k] = jnp.broadcast_to(row, (8, tile_atoms))
    columns[0:5, :] = middle[1, :, first : first + part_atoms]
    columns[5:, :] = jnp.zeros((columns.shape[0] - 5, part_atoms), jnp.float32)
    results[...] = jnp.transpose(columns[...])
    lane_ids = lax.broadcasted_iota(jnp.int32, (block_atoms, 128), 1)
    groups = block_atoms // 8

    def group(number, carry):
        place = pl.ds(pl.multiple_of(number * block_atoms, block_atoms), block_atoms)
        block = first // block_atoms + number
        own = results[place, :]
        mine = [
            jnp.broadcast_to(own[:, k : k + 1], (block_atoms, 128)).reshape(groups, 8, 128)
            for k in (0, 1, 2, 4)
        ]
        force_x = force_y = force_z = jnp.zeros((groups, 8, 128), jnp.float32)
        for slot in range(listed):
            rows = table.at[listing[0, slot, 0, block]]
            for start in range(0, tile_atoms, 128):
                lanes = slice(start, start + 128)
                sep_x = mine[0] - rows[0, :, lanes][None]
                sep_y = mine[1] - rows[1, :, lanes][None]
                sep_z = mine[2] - rows[2, :, lanes][None]
                reach = mine[3] + rows[4, :, lanes][None]
                root = lax.rsqrt(sep_x * sep_x + sep_y * sep_y + sep_z * sep_z + reach * reach)
                strength = rows[3, :, lanes][None] * root * (root * root)
                force_x = force_x + strength * sep_x
                force_y = force_y + strength * sep_y
                force_z = force_z + strength * sep_z
        out = jnp.zeros((block_atoms, 128), jnp.float32)
        for axis, total in enumerate((force_x, force_y, force_z)):
            total = jnp.sum(total.reshape(block_atoms, 128), axis=1, keepdims=True)
            out = jnp.where(lane_ids == axis, own[:, 3:4] * total, out)
        results[place, :] = out
        return carry

    lax.fori_loop(0, part_atoms // block_atoms, group, 0)
    columns[...] = jnp.transpose(results[...])
    if first:
        for axis in range(3):
            forces[axis, :, :first] = earlier[0][axis, :, :first]
    for axis in range(3):
        forces[axis, :, first : first + part_atoms] = columns[axis : axis + 1, :]


VMEM = pl.BlockSpec(memory_space=pltpu.VMEM)
SMEM = pl.BlockSpec(memory_space=pltpu.SMEM)
HBM = pl.BlockSpec(memory_space=pl.ANY)


def shaped(*shape):
    return jax.ShapeDtypeStruct(shape, jnp.float32)


def buffer(*shape):
    return pltpu.VMEM(shape, jnp.float32)


def like(table):
    return pltpu.VMEM(table.shape, table.dtype)


def limit(mib):
    return pltpu.CompilerParams(vmem_limit_bytes=mib * MIB)


def order_kernel(*refs):
    pass


def after(message, others):
    return pl.pallas_call(
        order_kernel,
        out_shape=shaped(*message.shape),
        in_specs=[HBM] * (1 + len(others)),
        out_specs=HBM,
        input_output_aliases={0: 0},
        compiler_params=limit(VMEM_MIB),
        name="order_message",
    )(message, *others)


def solve_poisson(plan, density, codes, first_code, n_blocks, block_atoms, neighbours, pair_part):
    x_len, y_len, grid = density.shape
    y_pad, x_pad, half, lanes = plan.y_pad, plan.x_pad, plan.half, plan.lanes
    total = plan.parts * plan.modes
    z_full = f32(plan.z_matrix())
    y_table = table_triple(plan.y_matrix(), 1)
    factors = f32(plan.elimination_factors())
    edge_y = f32(plan.edge_weights())
    interface = f32(plan.interface_table())
    bf16 = jnp.bfloat16
    code_shape = codes.shape
    shared = [
        buffer(x_len, y_pad, 128),
        buffer(plan.stack_rows, lanes),
        buffer(plan.lane_tiles, x_pad, 128),
    ]
    spectrum, places, message = pl.pallas_call(
        functools.partial(forward_kernel, plan, n_blocks, block_atoms),
        out_shape=(
            shaped(x_len, y_pad, lanes),
            jax.ShapeDtypeStruct(code_shape, jnp.int32),
            shaped(total, 1, 2 * half),
        ),
        in_specs=[SMEM] + [HBM] * 8,
        out_specs=(HBM, HBM, VMEM),
        scratch_shapes=[buffer(plan.lane_tiles * plan.planes, 128)]
        + shared
        + [
            buffer(2, x_pad, 128),
            buffer(lanes, 2 * half),
            buffer(*code_shape),
            buffer(x_len, y_len, grid),
            like(z_full),
            pltpu.VMEM((3 * lanes, lanes), bf16),
            like(y_table),
            like(factors),
            like(edge_y),
            like(interface),
            pltpu.VMEM((3 * plan.stack_rows, 2 * half), bf16),
            buffer(x_len, y_pad, lanes),
            pltpu.VMEM(code_shape, jnp.int32),
            pltpu.SMEM(code_shape, jnp.int32),
            pltpu.SMEM((code_shape[0],), jnp.int32),
            pltpu.SemaphoreType.DMA((11,)),
        ]
        + [pltpu.SMEM(code_shape, jnp.float32)] * (code_shape[0] <= 512),
        compiler_params=limit(VMEM_MIB),
        name="forward_solve",
    )(first_code, codes, density, z_full, y_table, factors, edge_y, interface, neighbours[0])
    message = after(message, neighbours[1:])
    eighth = n_blocks * block_atoms // 8
    first_pairs = pair_part(0, 4 * eighth)
    incoming = lax.all_to_all(message, ("gx", "gy"), split_axis=0, concat_axis=0, tiled=True)
    gather = plan.gather_table()
    along_y, along_x = plan.line_tables()
    expand = plan.expand_table()
    position = lax.axis_index("gx") * plan.n_gy + lax.axis_index("gy")
    first_mode = (position * plan.modes).astype(jnp.int32).reshape(1)
    stiff = stiffness(grid, grid)
    padded_z = np.zeros(total)
    padded_z[:grid] = stiff
    padded_y = np.zeros((1, lanes))
    padded_y[0, :grid] = stiff
    tables = [
        table_triple(gather, 1),
        f32(along_y),
        f32(along_x),
        f32(table_parts(expand, 0)),
        table_parts(expand, 1),
        f32(stiff[:, None] * grid),
        f32(padded_y * grid),
        table_triple(gather.T, 1),
    ]
    outgoing = pl.pallas_call(
        functools.partial(interface_kernel, plan),
        out_shape=shaped(total, 1, 2 * half),
        in_specs=[SMEM] * 2 + [HBM] * 10,
        out_specs=VMEM,
        scratch_shapes=[
            buffer(plan.modes, 2 * plan.parts, half),
            buffer(plan.modes, plan.kx_pad, lanes),
            buffer(plan.modes, plan.j_pad, lanes),
            buffer(plan.modes, gather.shape[0], half),
            buffer(total, 1, 2 * half),
            *[like(table) for table in tables],
            pltpu.VMEM((3 * along_y.shape[0], lanes), bf16),
            pltpu.VMEM((3 * along_x.shape[0], lanes), bf16),
            pltpu.VMEM((along_y.shape[0], 3 * lanes), bf16),
            pltpu.VMEM((along_x.shape[0], 3 * lanes), bf16),
            pltpu.SemaphoreType.DMA((9,)),
        ],
        compiler_params=limit(VMEM_MIB),
        name="interface_solve",
    )(first_mode, f32((padded_z + SCREENING) * grid), first_pairs, incoming, *tables)
    returned = lax.all_to_all(outgoing, ("gx", "gy"), split_axis=0, concat_axis=0, tiled=True)
    more_pairs = pair_part(4 * eighth, 3 * eighth, first_pairs)
    potential, values = pl.pallas_call(
        functools.partial(backward_kernel, plan, n_blocks, block_atoms),
        out_shape=(shaped(x_len, y_len, grid), shaped(plan.n_gx * n_blocks, 128)),
        in_specs=[HBM] * 9,
        out_specs=(HBM, VMEM),
        scratch_shapes=[
            buffer(plan.lane_tiles * plan.planes, 128),
            buffer(x_len, y_pad, lanes),
        ]
        + shared
        + [
            buffer(x_pad, 128),
            buffer(lanes, 2 * half),
            buffer(block_atoms, 128),
            buffer(x_len, y_len, grid),
            pltpu.SMEM(code_shape, jnp.int32),
            buffer(total, 1, 2 * half),
            like(interface),
            pltpu.VMEM((plan.stack_rows, 6 * half), bf16),
            like(factors),
            like(edge_y),
            buffer(x_len, y_pad, lanes),
            like(y_table),
            like(z_full),
            pltpu.VMEM((3 * lanes, lanes), bf16),
            pltpu.SMEM((code_shape[0],), jnp.int32),
            pltpu.SemaphoreType.DMA((9,)),
        ],
        compiler_params=limit(VMEM_MIB),
        name="backward_solve",
    )(places, returned, interface, factors, edge_y, spectrum, y_table, z_full, more_pairs)
    pair_force = pair_part(7 * eighth, eighth, more_pairs)
    return potential, values, pair_force


def shifted(block, axis, step):
    count = lax.axis_size(axis)
    return lax.ppermute(block, axis, [(i, (i + step) % count) for i in range(count)])


def body(
    qm_density,
    mm_coords,
    mm_charge,
    mm_types,
    type_radius,
    mm_cells,
    block_counts,
    block_owner,
    neighbour_tiles,
):
    n_blocks = block_counts.shape[2]
    tile_atoms = mm_charge.shape[2]
    block_atoms = tile_atoms // n_blocks
    x_local, local_y_rows, grid_len = qm_density.shape
    n_gx = lax.axis_size("gx")
    plan = Plan(x_local, local_y_rows, grid_len, n_gx, lax.axis_size("gy"))
    copies, atom_rows = pl.pallas_call(
        functools.partial(prepare_kernel, plan, n_blocks, block_atoms),
        out_shape=(shaped(n_gx * n_blocks, 128), shaped(1, 5, tile_atoms)),
        in_specs=[SMEM] * 3 + [VMEM] * 4,
        out_specs=(VMEM, VMEM),
        scratch_shapes=[buffer(n_blocks, 128)],
        compiler_params=limit(VMEM_MIB),
        name="prepare_atoms",
    )(
        block_counts.reshape(1, n_blocks),
        block_owner.reshape(1, n_blocks),
        type_radius,
        mm_coords.transpose(0, 2, 1, 3),
        mm_charge,
        mm_types,
        mm_cells,
    )
    codes = lax.all_to_all(copies, "gx", split_axis=0, concat_axis=0, tiled=True)
    first_code = (lax.axis_index("gx") * plan.span).astype(jnp.int32).reshape(1)
    triple = jnp.concatenate(
        [shifted(atom_rows, "gx", 1), atom_rows, shifted(atom_rows, "gx", -1)], axis=0
    )
    below, above = shifted(triple, "gy", 1), shifted(triple, "gy", -1)
    listed = neighbour_tiles.shape[3]
    listing = neighbour_tiles.transpose(0, 3, 1, 2)

    def pair_part(first, part_atoms, *earlier):
        return pl.pallas_call(
            functools.partial(pair_kernel, n_blocks, block_atoms, listed, first, part_atoms),
            out_shape=shaped(3, 1, first + part_atoms),
            in_specs=[SMEM] + [VMEM] * (3 + len(earlier)),
            out_specs=VMEM,
            scratch_shapes=[
                buffer(9, 5, 8, tile_atoms),
                buffer(128, part_atoms),
                buffer(part_atoms, 128),
            ],
            compiler_params=limit(VMEM_MIB),
            cost_estimate=pl.CostEstimate(
                flops=21 * listed * tile_atoms * part_atoms,
                bytes_accessed=4 * 50 * tile_atoms,
                transcendentals=listed * tile_atoms * part_atoms,
            ),
            name="pair_forces",
        )(listing, below, triple, above, *earlier)

    potential, values, pair_force = solve_poisson(
        plan, qm_density, codes, first_code, n_blocks, block_atoms, (triple, below, above), pair_part
    )
    values = lax.all_to_all(values, "gx", split_axis=0, concat_axis=0, tiled=True)
    sampled = jnp.sum(values.reshape(n_gx, n_blocks, 128), axis=0)[:, :block_atoms]
    lanes = jnp.arange(block_atoms, dtype=jnp.int32)
    live = lanes[None, :] < block_counts.reshape(n_blocks, 1)
    mm_potential = jnp.where(live, sampled, 0.0).reshape(1, 1, tile_atoms)
    return (potential, mm_potential, pair_force[None].transpose(0, 2, 1, 3))


def solution(mesh):
    placed = (
        P("gx", "gy", None),
        P("gx", "gy", None, None),
        P("gx", "gy", None),
        P("gx", "gy", None),
        P(),
        P("gx", "gy", None),
        P("gx", "gy", None),
        P("gx", "gy", None, None),
        P("gx", "gy", None, None),
    )
    return jax.shard_map(
        body,
        mesh=mesh,
        in_specs=placed,
        out_specs=(P("gx", "gy", None), P("gx", "gy", None), P("gx", "gy", None, None)),
        check_vma=False,
    )
```
